32 devices in a mesh: wide: 8 (over z, y), narrow: 4 (over x, core).
Axes of the slice: x: 2, y: 2, z: 4, core: 2. Of those that a mesh axis runs over, the one named last changes fastest.
Arguments:
- inputs: bfloat16 [8192, 1024], P('wide', 'narrow'), may hold values from -6 to 6
- segments: int32 [8, 1024], P('wide'), may hold values from 0 to 2, never falling along the last dimension, each value on 1 to 512 neighbouring positions
- attn_gain: bfloat16 [1024], P('wide'), may hold values from 0.5 to 1.5
- qkv_weight: bfloat16 [1024, 3, 1024], P('wide', None, 'narrow'), may hold values from -0.1875 to 0.1875
- out_weight: bfloat16 [1024, 1024], P('narrow', 'wide'), may hold values from -1.5 to 1.5
- memory_gain: bfloat16 [1024], P('wide'), may hold values from 0.5 to 1.5
- query_weight: bfloat16 [1024, 8, 256], P('wide', 'narrow'), may hold values from -0.1875 to 0.1875
- sub_keys: bfloat16 [8, 256, 256], P('narrow', 'wide'), may hold values from -0.5 to 0.5
- gate_weight: bfloat16 [1024, 1024], P('wide', 'narrow'), may hold values from -0.1875 to 0.1875
- memory_values: bfloat16 [65536, 1024], P('wide', 'narrow'), may hold values from -6 to 6
- memory_out: bfloat16 [1024, 1024], P('narrow', 'wide'), may hold values from -0.375 to 0.375
- picks: int32 [8192, 128], P('wide'), may hold values from 0 to 65535, as said below
- cotangent: bfloat16 [8192, 1024], P('wide', 'narrow'), may hold values from -6 to 6
Outputs:
- outputs: bfloat16 [8192, 1024], P('wide', 'narrow')
- input_grad: float32 [8192, 1024], P('wide', 'narrow')
- attn_gain_grad: float32 [1024], P('wide')
- qkv_grad: float32 [1024, 3, 1024], P('wide', None, 'narrow')
- out_grad: float32 [1024, 1024], P('narrow', 'wide')
- memory_gain_grad: float32 [1024], P('wide')
- query_grad: float32 [1024, 8, 256], P('wide', 'narrow')
- sub_keys_grad: float32 [8, 256, 256], P('narrow', 'wide')
- gate_grad: float32 [1024, 1024], P('wide', 'narrow')
- values_grad: float32 [65536, 1024], P('wide', 'narrow')
- memory_out_grad: float32 [1024, 1024], P('narrow', 'wide')
The draws below stay inside these ranges and needn't reach their ends.
Inputs may be any that keep to these rules, and one draw needn't show every extreme that they name: `segments`: segment numbers never fall along a sequence; every document spans 1 to 512 positions. The 128 rows of one token are all different; columns k * 32 to (k + 1) * 32 - 1 are the picks of memory head k.
All inputs are finite; a program needn't handle non-finite values.
Results may differ from the reference program's by a relative error of at most 0.023.
Values may be sent and summed in bfloat16 or wider, within the bound.
No kernel may reach another device: no remote copies, remote signals or barrier semaphores. Data moves between devices by JAX's collectives and lax.ppermute only.
A program may use at most 320 MiB of HBM per device.

```python
import math
import jax
import jax.numpy as jnp
import numpy as np
from jax import lax

D = 1024
H = 16
HD = 64
PKH = 4
NKEYS = 256
HALF = 256
TOPK = 32
SEQ = 1024
MROWS = 65536
UNITS = 8
PICKS = 128
NSEQ = 8
TOKENS = 8192
DOCS = 3
DOC_MOST = 512


def draw_picks(key, part):
    key = jax.random.fold_in(key, 7)
    stride = MROWS // PICKS
    first_key, second_key = jax.random.split(key)
    jitter = jax.random.randint(first_key, (TOKENS, PICKS), 0, stride, dtype=jnp.int32)
    offsets = jnp.arange(PICKS, dtype=jnp.int32)[None, :] * stride + jitter
    starts = jax.random.randint(second_key, (TOKENS, 1), 0, MROWS, dtype=jnp.int32)
    starts = starts.at[0, 0].set((MROWS - 1 - offsets[0, 0]) % MROWS)
    starts = starts.at[1, 0].set((MROWS - offsets[1, 0]) % MROWS)
    return ((starts + offsets) % MROWS).astype(jnp.int32)


def steps_of(stream_key, extent, cuts, low, top_value):
    loudness = 1.0
    for position, blocks in cuts:
        heights = jax.random.uniform(jax.random.fold_in(jax.random.fold_in(stream_key, 6), position), (blocks,), jnp.float32, low / len(cuts), top_value / len(cuts))
        loudness = loudness * jnp.repeat(jnp.exp(heights), extent[position] // blocks).reshape((-1,) + (1,) * (len(extent) - 1 - position))
    return loudness


def profile(amount, total, limit, lean):
    loads = [(1 << 20) // math.isqrt(rank ** lean) + 1 for rank in range(2, amount + 1)]
    rest, given = total - limit - (amount - 1), [1] * (amount - 1)
    while rest > 0:
        movable = [i for i in range(amount - 1) if given[i] < limit]
        pool, budget = sum([loads[i] for i in movable]), rest
        for i in movable:
            more = min(limit - given[i], max(1, budget * loads[i] // pool), rest)
            given[i] = given[i] + more
            rest = rest - more
    return np.array([limit] + given)


def uneven_parts(rng, amount, total, bound, skew):
    if amount == 2:
        one = jax.random.randint(rng, (), max(1, total - bound), min(bound, total - 1) + 1)
        return jnp.stack([one, total - one])
    tallies = jnp.asarray(profile(amount, total, bound, skew), jnp.int32)
    couples = (amount - 1) // 2
    donor, receiver = tallies[1:1 + 2 * couples:2], tallies[2:2 + 2 * couples:2]
    margin = jnp.minimum(donor - 1, bound - receiver)
    moved = jax.random.randint(jax.random.fold_in(rng, 1), (couples,), 0, 1 << 20) % (margin + 1)
    tallies = tallies.at[1:1 + 2 * couples:2].set(donor - moved).at[2:2 + 2 * couples:2].set(receiver + moved)
    return tallies[jax.random.permutation(jax.random.fold_in(rng, 2), amount)]


def normal_values(stream_key, extent, width, limit, cuts=(), kind=jnp.bfloat16):
    entries = jax.random.normal(stream_key, extent, jnp.float32) * width
    if len(cuts) > 0:
        entries = steps_of(stream_key, extent, cuts, -0.22, 0.18) * entries
    return jnp.clip(entries, min=-limit, max=limit).astype(kind)


def setup_inputs(seed: int = 0) -> dict:
    arg_keys = jax.random.split(jax.random.key(seed), 14)
    return {
        "inputs": normal_values(arg_keys[0], (TOKENS, D), 1.0, 6.0, ((0, 8), (1, 4))),
        "segments": jax.vmap(lambda own: jnp.searchsorted(jnp.cumsum(uneven_parts(own, DOCS, SEQ, DOC_MOST, 1)), jnp.arange(SEQ), side="right"))(jax.random.split(arg_keys[1], NSEQ)).reshape((NSEQ, SEQ)).astype(jnp.int32),
        "attn_gain": jnp.clip(1.0 + 0.1 * jax.random.normal(arg_keys[2], (D,), jnp.float32), 0.5, 1.5).astype(jnp.bfloat16),
        "qkv_weight": normal_values(arg_keys[3], (D, 3, D), D ** -0.5, 0.1875, ((0, 8), (2, 4))),
        "out_weight": normal_values(arg_keys[4], (D, D), (D // 64) ** -0.5, 1.5, ((0, 4), (1, 8))),
        "memory_gain": jnp.clip(1.0 + 0.1 * jax.random.normal(arg_keys[5], (D,), jnp.float32), 0.5, 1.5).astype(jnp.bfloat16),
        "query_weight": normal_values(arg_keys[6], (D, UNITS, HALF), D ** -0.5, 0.1875, ((0, 8), (1, 4))),
        "sub_keys": normal_values(arg_keys[7], (UNITS, NKEYS, HALF), (HALF // 2) ** -0.5, 0.5, ((0, 4), (1, 8))),
        "gate_weight": normal_values(arg_keys[8], (D, D), D ** -0.5, 0.1875, ((0, 8), (1, 4))),
        "memory_values": normal_values(arg_keys[9], (MROWS, D), 1.0, 6.0, ((0, 8), (1, 4))),
        "memory_out": normal_values(arg_keys[10], (D, D), (D // 4) ** -0.5, 0.375, ((0, 4), (1, 8))),
        "picks": draw_picks(jax.random.fold_in(arg_keys[13], 71), 0),
        "cotangent": normal_values(arg_keys[12], (TOKENS, D), 1.0, 6.0, ((0, 8), (1, 4))),
    }


EPSILON = 1e-06
HIGHEST = lax.Precision.HIGHEST
MASKED = -1e+30

@jax.custom_vjp
def low(v):
    return lax.optimization_barrier(v.astype(jnp.bfloat16)).astype(jnp.float32)

@jax.custom_vjp
def low_back(v):
    return v

def low_keep(v):
    return (low(v), None)

def low_pass(kept, grad):
    return (grad,)

def back_keep(v):
    return (v, None)

def back_low(kept, grad):
    return (low(grad),)
low.defvjp(low_keep, low_pass)
low_back.defvjp(back_keep, back_low)

def norm_rows(activations, gain_row):
    factor = lax.rsqrt(lax.optimization_barrier(jnp.mean(activations * activations, axis=-1, keepdims=True)) + EPSILON)
    return activations * factor * gain_row

def attend_sequence(bundle):
    mixture, segment_row = bundle
    block_rows = min(512, SEQ)
    queries = mixture[:, 0]
    key_rows = mixture[:, 1]
    value_rows = mixture[:, 2]
    positions = jnp.arange(SEQ, dtype=jnp.int32)

    def one_block(number):
        offset = number * block_rows
        query_block = lax.dynamic_slice_in_dim(queries, offset, block_rows, 0)
        segment_block = lax.dynamic_slice_in_dim(segment_row, offset, block_rows, 0)
        scores = jnp.einsum('qhd,khd->hqk', query_block, key_rows, precision=HIGHEST) * HD ** (-0.5)
        scores = low_back(scores)
        allowed = (positions[None, :] <= (offset + positions[:block_rows])[:, None]) & (segment_block[:, None] == segment_row[None, :])
        scores = jnp.where(allowed[None], scores, MASKED)
        attention = low(jax.nn.softmax(scores, axis=-1))
        return jnp.einsum('hqk,khd->qhd', attention, value_rows, precision=HIGHEST)
    result = lax.map(jax.checkpoint(one_block), jnp.arange(SEQ // block_rows, dtype=jnp.int32))
    return result.reshape(SEQ, H * HD)

def bag_sums(pick_weights, picks, memory_values):
    block_rows = min(256, SEQ)

    def one_block(number):
        offset = number * block_rows
        row_numbers = lax.dynamic_slice_in_dim(picks, offset, block_rows, 0)
        block_weights = lax.dynamic_slice_in_dim(pick_weights, offset, block_rows, 0)
        return jnp.einsum('tp,tpc->tc', block_weights, memory_values[row_numbers], precision=HIGHEST)
    result = lax.map(jax.checkpoint(one_block), jnp.arange(TOKENS // block_rows, dtype=jnp.int32))
    return result.reshape(TOKENS, D)

def forward(params, segments, picks):
    inputs, attn_gain, qkv_weight, out_weight, memory_gain, query_weight, sub_keys, gate_weight, memory_values, memory_out = params
    normed = low(norm_rows(inputs, attn_gain))
    mixture = jnp.einsum('td,djc->tjc', normed, qkv_weight, precision=HIGHEST)
    mixture = low_back(low(mixture)).reshape(NSEQ, SEQ, 3, H, HD)
    head_rows = lax.map(attend_sequence, (mixture, segments))
    head_rows = low_back(low(head_rows.reshape(TOKENS, D)))
    hidden = inputs + low_back(jnp.dot(head_rows, out_weight, precision=HIGHEST))
    second = low(norm_rows(hidden, memory_gain))
    gate_value = low_back(jnp.dot(second, gate_weight, precision=HIGHEST))
    memory_query = low_back(low(jnp.einsum('td,due->tue', second, query_weight, precision=HIGHEST)))
    full_scores = jnp.einsum('tue,uke->tuk', memory_query, sub_keys, precision=HIGHEST)
    grouped = picks.reshape(TOKENS, PKH, 1, TOPK)
    halves = jnp.concatenate([grouped // NKEYS, grouped % NKEYS], axis=2).reshape(TOKENS, UNITS, TOPK)
    unit_scores = jnp.take_along_axis(full_scores, halves, axis=2)
    mem_scores = low_back(lax.optimization_barrier(jnp.sum(unit_scores.reshape(TOKENS, PKH, 2, TOPK), axis=2)))
    pick_weights = low(jax.nn.softmax(mem_scores, axis=-1)).reshape(TOKENS, PICKS)
    memory = low_back(bag_sums(pick_weights, picks, memory_values))
    product = low(jax.nn.silu(gate_value) * memory)
    return hidden + jnp.dot(product, memory_out, precision=HIGHEST)

def reference(inputs, segments, attn_gain, qkv_weight, out_weight, memory_gain, query_weight, sub_keys, gate_weight, memory_values, memory_out, picks, cotangent):
    floats = tuple((member.astype(jnp.float32) for member in (inputs, attn_gain, qkv_weight, out_weight, memory_gain, query_weight, sub_keys, gate_weight, memory_values, memory_out)))

    def whole_layer(params):
        return forward(params, segments, picks)
    outputs, pullback = jax.vjp(whole_layer, floats)
    gradients, = pullback(cotangent.astype(jnp.float32))
    return (outputs.astype(jnp.bfloat16), gradients[0], gradients[1], gradients[2], gradients[3], gradients[4], gradients[5], gradients[6], gradients[7], gradients[8], gradients[9])
```

```python
import functools

import jax
import jax.numpy as jnp
from jax import lax
from jax.experimental import pallas as pl
from jax.experimental.pallas import tpu as pltpu
from jax.sharding import PartitionSpec as P

HD = 64
PKH = 4
NKEYS = 256
TOPK = 32
PICKS = 128
LANES = 128


EPSILON = 1e-06
MASKED = -1e30
BF16 = jnp.bfloat16
F32 = jnp.float32
NT = (((1,), (1,)), ((), ()))
TN = (((0,), (0,)), ((), ()))


def norm_rows(activations, gain_row):
    factor = lax.rsqrt(jnp.mean(activations * activations, axis=-1, keepdims=True) + EPSILON)
    return (factor, activations * factor * gain_row)


def norm_back(activations, factor, gain_row, upstream):
    inner_sum = jnp.mean(gain_row * upstream * activations, axis=-1, keepdims=True)
    through = factor * gain_row * upstream - activations * (factor * factor * factor) * inner_sum
    return (through, jnp.sum(upstream * activations * factor, axis=0))


def masked_scores(query_block, key_rows, segment_block, segment_row, offset):
    block_rows = query_block.shape[0]
    positions = jnp.arange(key_rows.shape[0], dtype=jnp.int32)
    scores = jnp.einsum("qhd,khd->hqk", query_block, key_rows, preferred_element_type=jnp.float32)
    scores = scores * query_block.shape[2] ** (-0.5)
    allowed = (positions[None, :] <= (offset + positions[:block_rows])[:, None]) & (
        segment_block[:, None] == segment_row[None, :]
    )
    return jnp.where(allowed[None], scores, MASKED)


def attend_forward(queries, key_rows, value_rows, segment_row):
    length = queries.shape[0]
    block_rows = min(512, length)

    def one_block(number):
        offset = number * block_rows
        query_block = lax.dynamic_slice_in_dim(queries, offset, block_rows, 0)
        segment_block = lax.dynamic_slice_in_dim(segment_row, offset, block_rows, 0)
        scores = masked_scores(query_block, key_rows, segment_block, segment_row, offset)
        row_peak = jnp.max(scores, axis=-1, keepdims=True)
        raised = jnp.exp(scores - row_peak)
        totals = jnp.sum(raised, axis=-1, keepdims=True)
        attention = (raised / totals).astype(jnp.bfloat16)
        mixture = jnp.einsum(
            "hqk,khd->qhd", attention, value_rows, preferred_element_type=jnp.float32
        )
        return (mixture.astype(jnp.bfloat16), (row_peak + jnp.log(totals))[:, :, 0])

    outputs, logsum = lax.map(one_block, jnp.arange(length // block_rows, dtype=jnp.int32))
    head_width = queries.shape[1] * queries.shape[2]
    logsum = jnp.transpose(logsum, (1, 0, 2)).reshape(queries.shape[1], length)
    return (outputs.reshape(length, head_width), logsum)


def attend_backward(queries, key_rows, value_rows, segment_row, logsum, heads_grad):
    length = queries.shape[0]
    block_rows = min(512, length)
    factor = queries.shape[2] ** (-0.5)

    def one_block(running, number):
        key_sum, value_sum = running
        offset = number * block_rows
        query_block = lax.dynamic_slice_in_dim(queries, offset, block_rows, 0)
        segment_block = lax.dynamic_slice_in_dim(segment_row, offset, block_rows, 0)
        grad_block = lax.dynamic_slice_in_dim(heads_grad, offset, block_rows, 0)
        logsum_block = lax.dynamic_slice_in_dim(logsum, offset, block_rows, 1)
        scores = masked_scores(query_block, key_rows, segment_block, segment_row, offset)
        attention = jnp.exp(scores - logsum_block[:, :, None])
        prob_grad = jnp.einsum(
            "qhd,khd->hqk", grad_block, value_rows, preferred_element_type=jnp.float32
        )
        centre = jnp.sum(attention * prob_grad, axis=-1, keepdims=True)
        score_grad = (attention * (prob_grad - centre)).astype(jnp.bfloat16)
        query_grad = (
            jnp.einsum("hqk,khd->qhd", score_grad, key_rows, preferred_element_type=jnp.float32)
            * factor
        )
        key_sum = (
            key_sum
            + jnp.einsum(
                "hqk,qhd->khd", score_grad, query_block, preferred_element_type=jnp.float32
            )
            * factor
        )
        value_sum = value_sum + jnp.einsum(
            "hqk,qhd->khd",
            attention.astype(jnp.bfloat16),
            grad_block,
            preferred_element_type=jnp.float32,
        )
        return ((key_sum, value_sum), query_grad)

    empty_sum = jnp.zeros(key_rows.shape, jnp.float32)
    carried, query_parts = lax.scan(
        one_block, (empty_sum, empty_sum), jnp.arange(length // block_rows, dtype=jnp.int32)
    )
    return (query_parts.reshape(queries.shape), carried[0], carried[1])


def params(mib):
    return pltpu.CompilerParams(vmem_limit_bytes=mib << 20)


def picked_body(base_ref, picks_ref, grad_ref, table_ref, out_ref, *, chunk):
    local = picks_ref[...] - base_ref[0]
    upper = local >> 7
    lower = local & (LANES - 1)
    grads = grad_ref[...]
    total = jnp.zeros(local.shape, F32)
    for start in range(0, table_ref.shape[0], chunk):
        products = lax.dot_general(
            grads, table_ref[pl.ds(start, chunk), :], NT, preferred_element_type=F32
        )
        for lane in range(0, chunk, LANES):
            found = jnp.take_along_axis(products[:, lane : lane + LANES], lower, axis=1)
            total = jnp.where(upper == (start + lane) // LANES, found, total)
    out_ref[...] = total


def picked_products(base, picks, grads, table, rows=256, chunk=1024):
    amount, width = grads.shape
    total = table.shape[0]
    return pl.pallas_call(
        functools.partial(picked_body, chunk=chunk),
        grid=(amount // rows,),
        in_specs=[
            pl.BlockSpec(memory_space=pltpu.SMEM),
            pl.BlockSpec((rows, PICKS), lambda i: (i, 0)),
            pl.BlockSpec((rows, width), lambda i: (i, 0)),
            pl.BlockSpec((total, width), lambda i: (0, 0)),
        ],
        out_specs=pl.BlockSpec((rows, PICKS), lambda i: (i, 0)),
        out_shape=jax.ShapeDtypeStruct((amount, PICKS), F32),
        compiler_params=params(48),
        cost_estimate=pl.CostEstimate(
            flops=8 * amount * total * width, bytes_accessed=amount * width * 4, transcendentals=0
        ),
        name="picked_products",
    )(base, picks, grads, table)


def bag_body(
    base_ref, picks_ref, weight_ref, table_ref, out_ref, keep_ref, held, upper, lower, weights,
    *, chunk, unroll
):
    rows = picks_ref.shape[0]
    groups = table_ref.shape[0] // LANES
    local = picks_ref[...] - base_ref[0]
    upper[...] = (local >> 7).astype(F32)
    lower[...] = (local & (LANES - 1)).astype(F32)
    weights[...] = weight_ref[...].astype(F32)
    group_ids = lax.broadcasted_iota(jnp.int32, (groups, LANES), 0).astype(F32).astype(BF16)
    lane_ids = lax.broadcasted_iota(jnp.int32, (LANES, LANES), 0).astype(F32).astype(BF16)
    zero = jnp.zeros((), BF16)
    one = jnp.ones((), BF16)

    def spread_row(ref, token, count):
        row = jnp.broadcast_to(ref[pl.ds(token, 1), :], (16, LANES)).astype(BF16)
        return jnp.concatenate([row] * (count // 16), axis=0)

    def some_tokens(step, carried):
        for slot in range(unroll):
            token = step * unroll + slot
            first = jnp.where(
                group_ids == spread_row(upper, token, groups),
                spread_row(weights, token, groups),
                zero,
            )
            second = jnp.where(lane_ids == spread_row(lower, token, LANES), one, zero)
            held[pl.ds(token, groups, stride=rows), :] = lax.dot_general(
                first, second, NT, preferred_element_type=F32
            )
        return carried

    lax.fori_loop(0, rows // unroll, some_tokens, 0)
    total = jnp.zeros(out_ref.shape, F32)
    for start in range(0, table_ref.shape[0], chunk):
        parts = [
            held[pl.ds(group * rows, rows), :].astype(BF16)
            for group in range(start // LANES, (start + chunk) // LANES)
        ]
        block = jnp.concatenate(parts, axis=1)
        keep_ref[:, pl.ds(start, chunk)] = block
        total = total + jnp.dot(
            block, table_ref[pl.ds(start, chunk), :], preferred_element_type=F32
        )
    out_ref[...] = total.astype(out_ref.dtype)


def bag_sums(base, picks, weights, table, rows=256, chunk=1024, unroll=32):
    amount = picks.shape[0]
    total, width = table.shape
    return pl.pallas_call(
        functools.partial(bag_body, chunk=chunk, unroll=unroll),
        grid=(amount // rows,),
        in_specs=[
            pl.BlockSpec(memory_space=pltpu.SMEM),
            pl.BlockSpec((rows, PICKS), lambda i: (i, 0)),
            pl.BlockSpec((rows, PICKS), lambda i: (i, 0)),
            pl.BlockSpec((total, width), lambda i: (0, 0)),
        ],
        out_specs=[
            pl.BlockSpec((rows, width), lambda i: (i, 0)),
            pl.BlockSpec((rows, total), lambda i: (i, 0)),
        ],
        out_shape=[
            jax.ShapeDtypeStruct((amount, width), BF16),
            jax.ShapeDtypeStruct((amount, total), BF16),
        ],
        scratch_shapes=[pltpu.VMEM((total // LANES * rows, LANES), F32)]
        + [pltpu.VMEM((rows, LANES), F32)] * 3,
        compiler_params=params(56),
        cost_estimate=pl.CostEstimate(
            flops=12 * amount * total * width, bytes_accessed=amount * total * 2, transcendentals=0
        ),
        name="bag_sums",
    )(base, picks, weights, table)


def unit_indices(picks, number):
    return jnp.where(number % 2 == 0, picks >> 8, picks & (NKEYS - 1))


def scores_body(column_ref, picks_ref, query_ref, keys_ref, out_ref, *, units):
    picks = picks_ref[...]
    lanes = lax.broadcasted_iota(jnp.int32, picks.shape, 1)
    total = jnp.zeros(picks.shape, F32)
    for unit in range(units):
        number = column_ref[0] * units + unit
        index = unit_indices(picks, number)
        scores = lax.dot_general(
            query_ref[:, unit * NKEYS : (unit + 1) * NKEYS],
            keys_ref[unit],
            NT,
            preferred_element_type=F32,
        )
        lower = index & (LANES - 1)
        low_part = jnp.take_along_axis(scores[:, :LANES], lower, axis=1)
        high_part = jnp.take_along_axis(scores[:, LANES:], lower, axis=1)
        found = jnp.where(index < LANES, low_part, high_part)
        total = total + jnp.where(lanes // TOPK == number // 2, found, 0.0)
    out_ref[...] = total


def pick_scores(column, picks, queries, keys, rows=256):
    amount = picks.shape[0]
    units = keys.shape[0]
    return pl.pallas_call(
        functools.partial(scores_body, units=units),
        grid=(amount // rows,),
        in_specs=[
            pl.BlockSpec(memory_space=pltpu.SMEM),
            pl.BlockSpec((rows, PICKS), lambda i: (i, 0)),
            pl.BlockSpec((rows, units * NKEYS), lambda i: (i, 0)),
            pl.BlockSpec(keys.shape, lambda i: (0, 0, 0)),
        ],
        out_specs=pl.BlockSpec((rows, PICKS), lambda i: (i, 0)),
        out_shape=jax.ShapeDtypeStruct((amount, PICKS), F32),
        compiler_params=params(32),
        name="pick_scores",
    )(column, picks, queries, keys)


def spread_body(
    column_ref, picks_ref, grad_ref, query_ref, keys_ref, out_ref, sum_ref, held_index, held_grad,
    *, units
):
    rows = picks_ref.shape[0]
    held_grad[...] = grad_ref[...].astype(F32).T

    @pl.when(pl.program_id(0) == 0)
    def clear():
        sum_ref[...] = jnp.zeros_like(sum_ref)

    key_ids = lax.broadcasted_iota(jnp.int32, (NKEYS, rows), 0)
    for unit in range(units):
        number = column_ref[0] * units + unit
        first = (number // 2) * TOPK
        held_index[...] = unit_indices(picks_ref[...], number).T
        table = jnp.zeros((NKEYS, rows), F32)
        for slot in range(TOPK):
            index = held_index[pl.ds(first + slot, 1), :]
            grad = held_grad[pl.ds(first + slot, 1), :]
            table = table + jnp.where(key_ids == index, grad, 0.0)
        table = table.astype(BF16)
        span = slice(unit * NKEYS, (unit + 1) * NKEYS)
        out_ref[:, span] = lax.dot_general(
            table, keys_ref[unit], TN, preferred_element_type=F32
        ).astype(BF16)
        sum_ref[unit] += jnp.dot(table, query_ref[:, span], preferred_element_type=F32)


def spread_grads(column, picks, grads, queries, keys, rows=128):
    amount = picks.shape[0]
    units = keys.shape[0]
    return pl.pallas_call(
        functools.partial(spread_body, units=units),
        grid=(amount // rows,),
        in_specs=[
            pl.BlockSpec(memory_space=pltpu.SMEM),
            pl.BlockSpec((rows, PICKS), lambda i: (i, 0)),
            pl.BlockSpec((rows, PICKS), lambda i: (i, 0)),
            pl.BlockSpec((rows, units * NKEYS), lambda i: (i, 0)),
            pl.BlockSpec(keys.shape, lambda i: (0, 0, 0)),
        ],
        out_specs=[
            pl.BlockSpec((rows, units * NKEYS), lambda i: (i, 0)),
            pl.BlockSpec(keys.shape, lambda i: (0, 0, 0)),
        ],
        out_shape=[
            jax.ShapeDtypeStruct((amount, units * NKEYS), BF16),
            jax.ShapeDtypeStruct(keys.shape, F32),
        ],
        scratch_shapes=[pltpu.VMEM((PICKS, rows), jnp.int32), pltpu.VMEM((PICKS, rows), F32)],
        compiler_params=params(32),
        name="spread_grads",
    )(column, picks, grads, queries, keys)


def gather_wide(block):
    return lax.all_gather(block, "wide")


def sum_wide(block):
    return lax.psum_scatter(block, "wide", scatter_dimension=0)


def rows_last(blocks):
    parts, rows, columns = blocks.shape
    return jnp.transpose(blocks, (1, 0, 2)).reshape(rows, parts * columns)


def columns_first(block, parts):
    rows = block.shape[0]
    return jnp.transpose(block.reshape(rows, parts, -1), (1, 0, 2))


def per_device(
    inputs,
    segments,
    attn_gain,
    qkv_weight,
    out_weight,
    memory_gain,
    query_weight,
    sub_keys,
    gate_weight,
    memory_values,
    memory_out,
    picks,
    cotangent,
):
    length, width = inputs.shape
    shards = lax.axis_size("wide")
    column = lax.axis_index("narrow")
    column_ref = column.astype(jnp.int32).reshape(1)
    shard_rows = memory_values.shape[0]
    base = (lax.axis_index("wide") * shard_rows).astype(jnp.int32).reshape(1)
    units = sub_keys.shape[0]
    model = qkv_weight.shape[0] * shards

    rows_one = lax.all_gather(inputs, "narrow", axis=1, tiled=True).astype(F32)
    gains = gather_wide(jnp.stack([attn_gain, memory_gain])).astype(F32)
    gain_one = gains[:, 0].reshape(model)
    gain_two = gains[:, 1].reshape(model)
    qkv_full = gather_wide(qkv_weight).reshape(model, 3, width)
    out_full = rows_last(gather_wide(out_weight))
    query_full = gather_wide(query_weight.reshape(-1, units * NKEYS)).reshape(model, units * NKEYS)
    gate_full = gather_wide(gate_weight).reshape(model, width)
    keys_full = jnp.transpose(gather_wide(sub_keys), (1, 0, 2, 3)).reshape(units, NKEYS, NKEYS)
    mixer_full = rows_last(gather_wide(memory_out))
    upstream = lax.all_gather(cotangent, "narrow", axis=1, tiled=True)
    all_picks = gather_wide(picks).reshape(shards * length, PICKS)

    factor_one, normed = norm_rows(rows_one, gain_one)
    normed = normed.astype(BF16)
    mixture = jnp.einsum("td,djc->tjc", normed, qkv_full, preferred_element_type=F32).astype(BF16)
    head_count = width // HD
    queries = mixture[:, 0].reshape(length, head_count, HD)
    key_rows = mixture[:, 1].reshape(length, head_count, HD)
    value_rows = mixture[:, 2].reshape(length, head_count, HD)
    segment_row = segments[0]
    head_rows, logsum = attend_forward(queries, key_rows, value_rows, segment_row)
    branch_part = jnp.dot(head_rows, out_full, preferred_element_type=F32).astype(BF16)
    hidden = rows_one + lax.psum(branch_part, "narrow").astype(F32)
    factor_two, second = norm_rows(hidden, gain_two)
    second = second.astype(BF16)

    gate_value = jnp.dot(second, gate_full, preferred_element_type=F32)
    gate_act = jax.nn.silu(gate_value)
    product_grad = lax.dot_general(upstream, mixer_full, NT, preferred_element_type=F32)
    memory_grad = (product_grad * gate_act).astype(BF16)
    all_grads = gather_wide(memory_grad).reshape(shards * length, width)

    memory_query = jnp.dot(second, query_full, preferred_element_type=F32).astype(BF16)
    own_scores = pick_scores(column_ref, picks, memory_query, keys_full)
    mem_scores = lax.psum(own_scores, "narrow").reshape(length, PKH, TOPK)
    score_peak = jnp.max(mem_scores, axis=-1, keepdims=True)
    raised = jnp.exp(mem_scores - score_peak)
    mem_probs = raised / jnp.sum(raised, axis=-1, keepdims=True)
    pick_weights = mem_probs.astype(BF16).reshape(length, PICKS)
    all_weights = gather_wide(pick_weights).reshape(shards * length, PICKS)

    pick_part = picked_products(base, all_picks, all_grads, memory_values).astype(BF16)
    memory_part, tables = bag_sums(base, all_picks, all_weights, memory_values)
    pick_own = sum_wide(pick_part.reshape(shards, length, PICKS)).astype(F32)
    memory = sum_wide(memory_part.reshape(shards, length, width)).astype(F32)
    values_grad = lax.dot_general(tables, all_grads, TN, preferred_element_type=F32)

    product = (gate_act * memory).astype(BF16)
    mixer_part = jnp.dot(product, mixer_full, preferred_element_type=F32)
    mixer_sum = lax.psum_scatter(
        mixer_part.astype(BF16), "narrow", scatter_dimension=1, tiled=True
    ).astype(F32)
    own_hidden = lax.dynamic_slice_in_dim(hidden, column * width, width, 1)
    outputs = (own_hidden + mixer_sum).astype(BF16)
    mixer_grad = lax.dot_general(product, upstream, TN, preferred_element_type=F32)
    sigmoid = jax.nn.sigmoid(gate_value)
    gate_rows_grad = (
        product_grad * memory * sigmoid * (1.0 + gate_value * (1.0 - sigmoid))
    ).astype(BF16)

    pick_own, mem_probs = lax.optimization_barrier((pick_own, mem_probs))
    pick_grad = lax.psum(pick_own, "narrow").reshape(length, PKH, TOPK)
    centre = jnp.sum(mem_probs * pick_grad, axis=-1, keepdims=True)
    score_grad = (mem_probs * (pick_grad - centre)).astype(BF16).reshape(length, PICKS)
    memory_query_grad, key_grad = spread_grads(
        column_ref, picks, score_grad, memory_query, keys_full
    )
    query_weight_grad = lax.dot_general(second, memory_query_grad, TN, preferred_element_type=F32)
    gate_weight_grad = lax.dot_general(second, gate_rows_grad, TN, preferred_element_type=F32)
    second_part = lax.dot_general(gate_rows_grad, gate_full, NT, preferred_element_type=F32)
    second_part = second_part + lax.dot_general(
        memory_query_grad, query_full, NT, preferred_element_type=F32
    )
    second_grad = lax.psum(second_part.astype(BF16), "narrow").astype(F32)
    through_two, gain_two_part = norm_back(hidden, factor_two, gain_two, second_grad)
    hidden_grad = upstream.astype(F32) + through_two
    branch_grad = hidden_grad.astype(BF16)
    out_weight_grad = lax.dot_general(head_rows, branch_grad, TN, preferred_element_type=F32)
    heads_grad = lax.dot_general(branch_grad, out_full, NT, preferred_element_type=F32)
    heads_grad = heads_grad.astype(BF16).reshape(length, head_count, HD)
    query_back, key_back, value_back = attend_backward(
        queries, key_rows, value_rows, segment_row, logsum, heads_grad
    )
    mixed_grad = jnp.stack(
        [
            query_back.reshape(length, width),
            key_back.reshape(length, width),
            value_back.reshape(length, width),
        ],
        axis=1,
    ).astype(BF16)
    qkv_weight_grad = jnp.einsum("td,tjc->djc", normed, mixed_grad, preferred_element_type=F32)
    normed_part = jnp.einsum("tjc,djc->td", mixed_grad, qkv_full, preferred_element_type=F32)
    normed_grad = lax.psum(normed_part.astype(BF16), "narrow").astype(F32)
    through_one, gain_one_part = norm_back(rows_one, factor_one, gain_one, normed_grad)
    input_full = hidden_grad + through_one
    input_grad = lax.dynamic_slice_in_dim(input_full, column * width, width, 1)

    gain_sums = sum_wide(
        jnp.stack([gain_one_part, gain_two_part], axis=1).astype(BF16).reshape(shards, -1, 2)
    ).astype(F32)
    qkv_sum = sum_wide(qkv_weight_grad.astype(BF16).reshape(shards, -1, 3, width)).astype(F32)
    out_sum = sum_wide(columns_first(out_weight_grad.astype(BF16), shards)).astype(F32)
    query_sum = sum_wide(query_weight_grad.astype(BF16).reshape(shards, -1, units, NKEYS))
    key_sum = sum_wide(
        jnp.transpose(key_grad.astype(BF16).reshape(units, shards, -1, NKEYS), (1, 0, 2, 3))
    ).astype(F32)
    gate_sum = sum_wide(gate_weight_grad.astype(BF16).reshape(shards, -1, width)).astype(F32)
    mixer_grad_sum = sum_wide(columns_first(mixer_grad.astype(BF16), shards)).astype(F32)
    return (
        outputs,
        input_grad,
        gain_sums[:, 0],
        qkv_sum,
        out_sum,
        gain_sums[:, 1],
        query_sum.astype(F32),
        key_sum,
        gate_sum,
        values_grad,
        mixer_grad_sum,
    )


def solution(mesh):
    return jax.shard_map(
        per_device,
        mesh=mesh,
        in_specs=(
            P("wide", "narrow"),
            P("wide", None),
            P("wide"),
            P("wide", None, "narrow"),
            P("narrow", "wide"),
            P("wide"),
            P("wide", "narrow", None),
            P("narrow", "wide", None),
            P("wide", "narrow"),
            P("wide", "narrow"),
            P("narrow", "wide"),
            P("wide", None),
            P("wide", "narrow"),
        ),
        out_specs=(
            P("wide", "narrow"),
            P("wide", "narrow"),
            P("wide"),
            P("wide", None, "narrow"),
            P("narrow", "wide"),
            P("wide"),
            P("wide", "narrow", None),
            P("narrow", "wide", None),
            P("wide", "narrow"),
            P("wide", "narrow"),
            P("narrow", "wide"),
        ),
        check_vma=False,
    )
```

```python
import functools

import jax
import jax.numpy as jnp
from jax import lax
from jax.experimental import pallas as pl
from jax.experimental.pallas import tpu as pltpu
from jax.sharding import PartitionSpec as P

HD = 64
PKH = 4
NKEYS = 256
TOPK = 32
PICKS = 128
LANES = 128


EPSILON = 1e-06
MASKED = -1e30
BF16 = jnp.bfloat16
F32 = jnp.float32
NT = (((1,), (1,)), ((), ()))
TN = (((0,), (0,)), ((), ()))


def norm_rows(activations, gain_row):
    factor = lax.rsqrt(jnp.mean(activations * activations, axis=-1, keepdims=True) + EPSILON)
    return (factor, activations * factor * gain_row)


def norm_back(activations, factor, gain_row, upstream):
    inner_sum = jnp.mean(gain_row * upstream * activations, axis=-1, keepdims=True)
    through = factor * gain_row * upstream - activations * (factor * factor * factor) * inner_sum
    return (through, jnp.sum(upstream * activations * factor, axis=0))


def masked_scores(query_block, key_rows, segment_block, segment_row, offset):
    block_rows = query_block.shape[0]
    positions = jnp.arange(key_rows.shape[0], dtype=jnp.int32)
    scores = jnp.einsum("qhd,khd->hqk", query_block, key_rows, preferred_element_type=jnp.float32)
    scores = scores * query_block.shape[2] ** (-0.5)
    allowed = (positions[None, :] <= (offset + positions[:block_rows])[:, None]) & (
        segment_block[:, None] == segment_row[None, :]
    )
    return jnp.where(allowed[None], scores, MASKED)


def attend_forward(queries, key_rows, value_rows, segment_row):
    length = queries.shape[0]
    block_rows = min(512, length)

    def one_block(number):
        offset = number * block_rows
        query_block = lax.dynamic_slice_in_dim(queries, offset, block_rows, 0)
        segment_block = lax.dynamic_slice_in_dim(segment_row, offset, block_rows, 0)
        scores = masked_scores(query_block, key_rows, segment_block, segment_row, offset)
        row_peak = jnp.max(scores, axis=-1, keepdims=True)
        raised = jnp.exp(scores - row_peak)
        totals = jnp.sum(raised, axis=-1, keepdims=True)
        attention = (raised / totals).astype(jnp.bfloat16)
        mixture = jnp.einsum(
            "hqk,khd->qhd", attention, value_rows, preferred_element_type=jnp.float32
        )
        return (mixture.astype(jnp.bfloat16), (row_peak + jnp.log(totals))[:, :, 0])

    outputs, logsum = lax.map(one_block, jnp.arange(length // block_rows, dtype=jnp.int32))
    head_width = queries.shape[1] * queries.shape[2]
    logsum = jnp.transpose(logsum, (1, 0, 2)).reshape(queries.shape[1], length)
    return (outputs.reshape(length, head_width), logsum)


def attend_backward(queries, key_rows, value_rows, segment_row, logsum, heads_grad):
    length = queries.shape[0]
    block_rows = min(512, length)
    factor = queries.shape[2] ** (-0.5)

    def one_block(running, number):
        key_sum, value_sum = running
        offset = number * block_rows
        query_block = lax.dynamic_slice_in_dim(queries, offset, block_rows, 0)
        segment_block = lax.dynamic_slice_in_dim(segment_row, offset, block_rows, 0)
        grad_block = lax.dynamic_slice_in_dim(heads_grad, offset, block_rows, 0)
        logsum_block = lax.dynamic_slice_in_dim(logsum, offset, block_rows, 1)
        scores = masked_scores(query_block, key_rows, segment_block, segment_row, offset)
        attention = jnp.exp(scores - logsum_block[:, :, None])
        prob_grad = jnp.einsum(
            "qhd,khd->hqk", grad_block, value_rows, preferred_element_type=jnp.float32
        )
        centre = jnp.sum(attention * prob_grad, axis=-1, keepdims=True)
        score_grad = (attention * (prob_grad - centre)).astype(jnp.bfloat16)
        query_grad = (
            jnp.einsum("hqk,khd->qhd", score_grad, key_rows, preferred_element_type=jnp.float32)
            * factor
        )
        key_sum = (
            key_sum
            + jnp.einsum(
                "hqk,qhd->khd", score_grad, query_block, preferred_element_type=jnp.float32
            )
            * factor
        )
        value_sum = value_sum + jnp.einsum(
            "hqk,qhd->khd",
            attention.astype(jnp.bfloat16),
            grad_block,
            preferred_element_type=jnp.float32,
        )
        return ((key_sum, value_sum), query_grad)

    empty_sum = jnp.zeros(key_rows.shape, jnp.float32)
    carried, query_parts = lax.scan(
        one_block, (empty_sum, empty_sum), jnp.arange(length // block_rows, dtype=jnp.int32)
    )
    return (query_parts.reshape(queries.shape), carried[0], carried[1])


def params(mib):
    return pltpu.CompilerParams(vmem_limit_bytes=mib << 20)


def picked_body(base_ref, picks_ref, grad_ref, table_ref, out_ref, *, chunk):
    local = picks_ref[...] - base_ref[0]
    upper = local >> 7
    lower = local & (LANES - 1)
    grads = grad_ref[...]
    total = jnp.zeros(local.shape, F32)
    for start in range(0, table_ref.shape[0], chunk):
        products = lax.dot_general(
            grads, table_ref[pl.ds(start, chunk), :], NT, preferred_element_type=F32
        )
        for lane in range(0, chunk, LANES):
            found = jnp.take_along_axis(products[:, lane : lane + LANES], lower, axis=1)
            total = jnp.where(upper == (start + lane) // LANES, found, total)
    out_ref[...] = total


def picked_products(base, picks, grads, table, rows=256, chunk=1024):
    amount, width = grads.shape
    total = table.shape[0]
    return pl.pallas_call(
        functools.partial(picked_body, chunk=chunk),
        grid=(amount // rows,),
        in_specs=[
            pl.BlockSpec(memory_space=pltpu.SMEM),
            pl.BlockSpec((rows, PICKS), lambda i: (i, 0)),
            pl.BlockSpec((rows, width), lambda i: (i, 0)),
            pl.BlockSpec((total, width), lambda i: (0, 0)),
        ],
        out_specs=pl.BlockSpec((rows, PICKS), lambda i: (i, 0)),
        out_shape=jax.ShapeDtypeStruct((amount, PICKS), F32),
        compiler_params=params(48),
        cost_estimate=pl.CostEstimate(
            flops=8 * amount * total * width, bytes_accessed=amount * width * 4, transcendentals=0
        ),
        name="picked_products",
    )(base, picks, grads, table)


def bag_body(
    base_ref, picks_ref, weight_ref, table_ref, out_ref, keep_ref, held, upper, lower, weights,
    *, chunk, unroll
):
    rows = picks_ref.shape[0]
    groups = table_ref.shape[0] // LANES
    local = picks_ref[...] - base_ref[0]
    upper[...] = (local >> 7).astype(F32)
    lower[...] = (local & (LANES - 1)).astype(F32)
    weights[...] = weight_ref[...].astype(F32)
    group_ids = lax.broadcasted_iota(jnp.int32, (groups, LANES), 0).astype(F32).astype(BF16)
    lane_ids = lax.broadcasted_iota(jnp.int32, (LANES, LANES), 0).astype(F32).astype(BF16)
    zero = jnp.zeros((), BF16)
    one = jnp.ones((), BF16)

    def spread_row(ref, token, count):
        row = jnp.broadcast_to(ref[pl.ds(token, 1), :], (16, LANES)).astype(BF16)
        return jnp.concatenate([row] * (count // 16), axis=0)

    def some_tokens(step, carried):
        for slot in range(unroll):
            token = step * unroll + slot
            first = jnp.where(
                group_ids == spread_row(upper, token, groups),
                spread_row(weights, token, groups),
                zero,
            )
            second = jnp.where(lane_ids == spread_row(lower, token, LANES), one, zero)
            held[pl.ds(token, groups, stride=rows), :] = lax.dot_general(
                first, second, NT, preferred_element_type=F32
            )
        return carried

    lax.fori_loop(0, rows // unroll, some_tokens, 0)
    total = jnp.zeros(out_ref.shape, F32)
    for start in range(0, table_ref.shape[0], chunk):
        parts = [
            held[pl.ds(group * rows, rows), :].astype(BF16)
            for group in range(start // LANES, (start + chunk) // LANES)
        ]
        block = jnp.concatenate(parts, axis=1)
        keep_ref[:, pl.ds(start, chunk)] = block
        total = total + jnp.dot(
            block, table_ref[pl.ds(start, chunk), :], preferred_element_type=F32
        )
    out_ref[...] = total.astype(out_ref.dtype)


def bag_sums(base, picks, weights, table, rows=256, chunk=1024, unroll=32):
    amount = picks.shape[0]
    total, width = table.shape
    return pl.pallas_call(
        functools.partial(bag_body, chunk=chunk, unroll=unroll),
        grid=(amount // rows,),
        in_specs=[
            pl.BlockSpec(memory_space=pltpu.SMEM),
            pl.BlockSpec((rows, PICKS), lambda i: (i, 0)),
            pl.BlockSpec((rows, PICKS), lambda i: (i, 0)),
            pl.BlockSpec((total, width), lambda i: (0, 0)),
        ],
        out_specs=[
            pl.BlockSpec((rows, width), lambda i: (i, 0)),
            pl.BlockSpec((rows, total), lambda i: (i, 0)),
        ],
        out_shape=[
            jax.ShapeDtypeStruct((amount, width), BF16),
            jax.ShapeDtypeStruct((amount, total), BF16),
        ],
        scratch_shapes=[pltpu.VMEM((total // LANES * rows, LANES), F32)]
        + [pltpu.VMEM((rows, LANES), F32)] * 3,
        compiler_params=params(56),
        cost_estimate=pl.CostEstimate(
            flops=12 * amount * total * width, bytes_accessed=amount * total * 2, transcendentals=0
        ),
        name="bag_sums",
    )(base, picks, weights, table)


def unit_indices(picks, number):
    return jnp.where(number % 2 == 0, picks >> 8, picks & (NKEYS - 1))


def scores_body(column_ref, picks_ref, query_ref, keys_ref, out_ref, *, units):
    picks = picks_ref[...]
    lanes = lax.broadcasted_iota(jnp.int32, picks.shape, 1)
    total = jnp.zeros(picks.shape, F32)
    for unit in range(units):
        number = column_ref[0] * units + unit
        index = unit_indices(picks, number)
        scores = lax.dot_general(
            query_ref[:, unit * NKEYS : (unit + 1) * NKEYS],
            keys_ref[unit],
            NT,
            preferred_element_type=F32,
        )
        lower = index & (LANES - 1)
        low_part = jnp.take_along_axis(scores[:, :LANES], lower, axis=1)
        high_part = jnp.take_along_axis(scores[:, LANES:], lower, axis=1)
        found = jnp.where(index < LANES, low_part, high_part)
        total = total + jnp.where(lanes // TOPK == number // 2, found, 0.0)
    out_ref[...] = total


def pick_scores(column, picks, queries, keys, rows=256):
    amount = picks.shape[0]
    units = keys.shape[0]
    return pl.pallas_call(
        functools.partial(scores_body, units=units),
        grid=(amount // rows,),
        in_specs=[
            pl.BlockSpec(memory_space=pltpu.SMEM),
            pl.BlockSpec((rows, PICKS), lambda i: (i, 0)),
            pl.BlockSpec((rows, units * NKEYS), lambda i: (i, 0)),
            pl.BlockSpec(keys.shape, lambda i: (0, 0, 0)),
        ],
        out_specs=pl.BlockSpec((rows, PICKS), lambda i: (i, 0)),
        out_shape=jax.ShapeDtypeStruct((amount, PICKS), F32),
        compiler_params=params(32),
        name="pick_scores",
    )(column, picks, queries, keys)


def spread_body(
    column_ref, picks_ref, grad_ref, query_ref, keys_ref, out_ref, sum_ref, held_index, held_grad,
    *, units
):
    rows = picks_ref.shape[0]
    held_grad[...] = grad_ref[...].astype(F32).T

    @pl.when(pl.program_id(0) == 0)
    def clear():
        sum_ref[...] = jnp.zeros_like(sum_ref)

    key_ids = lax.broadcasted_iota(jnp.int32, (NKEYS, rows), 0)
    for unit in range(units):
        number = column_ref[0] * units + unit
        first = (number // 2) * TOPK
        held_index[...] = unit_indices(picks_ref[...], number).T
        table = jnp.zeros((NKEYS, rows), F32)
        for slot in range(TOPK):
            index = held_index[pl.ds(first + slot, 1), :]
            grad = held_grad[pl.ds(first + slot, 1), :]
            table = table + jnp.where(key_ids == index, grad, 0.0)
        table = table.astype(BF16)
        span = slice(unit * NKEYS, (unit + 1) * NKEYS)
        out_ref[:, span] = lax.dot_general(
            table, keys_ref[unit], TN, preferred_element_type=F32
        ).astype(BF16)
        sum_ref[unit] += jnp.dot(table, query_ref[:, span], preferred_element_type=F32)


def spread_grads(column, picks, grads, queries, keys, rows=128):
    amount = picks.shape[0]
    units = keys.shape[0]
    return pl.pallas_call(
        functools.partial(spread_body, units=units),
        grid=(amount // rows,),
        in_specs=[
            pl.BlockSpec(memory_space=pltpu.SMEM),
            pl.BlockSpec((rows, PICKS), lambda i: (i, 0)),
            pl.BlockSpec((rows, PICKS), lambda i: (i, 0)),
            pl.BlockSpec((rows, units * NKEYS), lambda i: (i, 0)),
            pl.BlockSpec(keys.shape, lambda i: (0, 0, 0)),
        ],
        out_specs=[
            pl.BlockSpec((rows, units * NKEYS), lambda i: (i, 0)),
            pl.BlockSpec(keys.shape, lambda i: (0, 0, 0)),
        ],
        out_shape=[
            jax.ShapeDtypeStruct((amount, units * NKEYS), BF16),
            jax.ShapeDtypeStruct(keys.shape, F32),
        ],
        scratch_shapes=[pltpu.VMEM((PICKS, rows), jnp.int32), pltpu.VMEM((PICKS, rows), F32)],
        compiler_params=params(32),
        name="spread_grads",
    )(column, picks, grads, queries, keys)


def swap_narrow(block, bit):
    size = lax.axis_size("narrow")
    return lax.ppermute(block, "narrow", [(i, i ^ bit) for i in range(size)])


def swap_wide(block, bit):
    size = lax.axis_size("wide")
    return lax.ppermute(block, "wide", [(i, i ^ bit) for i in range(size)])


def gather_by_swaps(block, axis, bits):
    size = lax.axis_size(axis)
    me = lax.axis_index(axis)
    held = {0: block}
    for bit in bits:
        moved = {}
        for offset, part in held.items():
            moved[offset ^ bit] = lax.ppermute(part, axis, [(i, i ^ bit) for i in range(size)])
        held.update(moved)
    stacked = jnp.stack([held[offset] for offset in range(size)])
    return [lax.dynamic_index_in_dim(stacked, me ^ number, 0, False) for number in range(size)]


def bits_down(size):
    return [1 << level for level in reversed(range(size.bit_length() - 1))]


def gather_narrow(block):
    return jnp.concatenate(
        gather_by_swaps(block, "narrow", bits_down(lax.axis_size("narrow"))), axis=1
    )


def gather_wide(block):
    return lax.all_gather(block, "wide")


def sum_wide(block):
    return lax.psum_scatter(block, "wide", scatter_dimension=0)


def lane_blocks(block):
    return jnp.concatenate(
        [block[..., start : start + LANES] for start in range(0, block.shape[-1], LANES)], axis=-2
    )


def join_lanes(blocks, rows):
    count = blocks.shape[-2] // rows
    return jnp.concatenate(
        [blocks[..., part * rows : (part + 1) * rows, :] for part in range(count)], axis=-1
    )


def pack(blocks):
    return jnp.concatenate([lane_blocks(block) for block in blocks], axis=-2)


def unpack(packed, shapes):
    result = []
    start = 0
    for rows, columns in shapes:
        stop = start + rows * columns // LANES
        result.append(join_lanes(packed[..., start:stop, :], rows))
        start = stop
    return result


def per_device(
    inputs,
    segments,
    attn_gain,
    qkv_weight,
    out_weight,
    memory_gain,
    query_weight,
    sub_keys,
    gate_weight,
    memory_values,
    memory_out,
    picks,
    cotangent,
):
    length, width = inputs.shape
    shards = lax.axis_size("wide")
    column = lax.axis_index("narrow")
    column_ref = column.astype(jnp.int32).reshape(1)
    shard_rows = memory_values.shape[0]
    base = (lax.axis_index("wide") * shard_rows).astype(jnp.int32).reshape(1)
    units = sub_keys.shape[0]
    part = qkv_weight.shape[0]
    model = part * shards
    key_part = sub_keys.shape[1]

    rows_one = gather_narrow(inputs).astype(F32)
    first_shapes = [(3 * part, width), (2 * part // LANES, LANES)]
    first_pack = pack(
        [
            jnp.transpose(qkv_weight, (1, 0, 2)).reshape(3 * part, width),
            jnp.concatenate([attn_gain, memory_gain]).reshape(-1, LANES),
        ]
    )
    qkv_parts, gains = unpack(gather_wide(first_pack), first_shapes)
    qkv_full = [
        qkv_parts[:, j * part : (j + 1) * part].reshape(model, width) for j in range(3)
    ]
    gains = gains.reshape(shards, 2, part).astype(F32)
    gain_one = gains[:, 0].reshape(model)
    gain_two = gains[:, 1].reshape(model)
    second_shapes = [
        (part, width),
        (part, width),
        (part, width),
        (part, units * NKEYS),
        (units * key_part, NKEYS),
    ]
    second_pack = pack(
        [
            out_weight.T,
            memory_out.T,
            gate_weight,
            query_weight.reshape(part, units * NKEYS),
            sub_keys.reshape(units * key_part, NKEYS),
        ]
    )
    second_pack, first_pack = lax.optimization_barrier((second_pack, first_pack))
    out_turned, mixer_turned, gate_full, query_full, keys_full = unpack(
        gather_wide(second_pack), second_shapes
    )
    out_turned = out_turned.reshape(model, width)
    mixer_turned = mixer_turned.reshape(model, width)
    gate_full = gate_full.reshape(model, width)
    query_full = query_full.reshape(model, units * NKEYS)
    keys_full = jnp.transpose(
        keys_full.reshape(shards, units, key_part, NKEYS), (1, 0, 2, 3)
    ).reshape(units, NKEYS, NKEYS)
    out_all = gather_narrow(out_turned)
    upstream = gather_narrow(cotangent)
    all_picks = jnp.concatenate(
        gather_by_swaps(picks.astype(jnp.uint16), "wide", bits_down(shards)[::-1]), axis=0
    ).astype(jnp.int32)

    factor_one, normed = norm_rows(rows_one, gain_one)
    normed = normed.astype(BF16)
    mixture = [
        jnp.dot(normed, qkv_full[j], preferred_element_type=F32).astype(BF16) for j in range(3)
    ]
    head_count = width // HD
    queries, key_rows, value_rows = [
        member.reshape(length, head_count, HD) for member in mixture
    ]
    segment_row = segments[0]
    head_rows, logsum = attend_forward(queries, key_rows, value_rows, segment_row)
    head_all = gather_narrow(head_rows)
    hidden = rows_one + lax.dot_general(head_all, out_all, NT, preferred_element_type=F32)
    factor_two, second = norm_rows(hidden, gain_two)
    second = second.astype(BF16)

    gate_value = jnp.dot(second, gate_full, preferred_element_type=F32)
    gate_act = jax.nn.silu(gate_value)
    product_grad = jnp.dot(upstream, mixer_turned, preferred_element_type=F32)
    memory_grad = (product_grad * gate_act).astype(BF16)
    all_grads = gather_wide(memory_grad).reshape(shards * length, width)

    memory_query = jnp.dot(second, query_full, preferred_element_type=F32).astype(BF16)
    own_scores = pick_scores(column_ref, picks, memory_query, keys_full)
    for bit in bits_down(lax.axis_size("narrow")):
        own_scores = own_scores + swap_narrow(own_scores, bit)
    mem_scores = own_scores.reshape(length, PKH, TOPK)
    score_peak = jnp.max(mem_scores, axis=-1, keepdims=True)
    raised = jnp.exp(mem_scores - score_peak)
    mem_probs = raised / jnp.sum(raised, axis=-1, keepdims=True)
    pick_weights = mem_probs.astype(BF16).reshape(length, PICKS)
    pick_weights, memory_grad = lax.optimization_barrier((pick_weights, memory_grad))
    all_weights = gather_wide(pick_weights).reshape(shards * length, PICKS)

    pick_part = picked_products(base, all_picks, all_grads, memory_values).astype(BF16)
    all_weights, pick_part = lax.optimization_barrier((all_weights, pick_part))
    memory_part, tables = bag_sums(base, all_picks, all_weights, memory_values)
    pick_own = sum_wide(pick_part.reshape(shards, length, PICKS)).astype(F32)
    memory_part, pick_own = lax.optimization_barrier((memory_part, pick_own))
    memory = sum_wide(memory_part.reshape(shards, length, width)).astype(F32)
    tables, pick_own = lax.optimization_barrier((tables, pick_own))
    values_grad = lax.dot_general(tables, all_grads, TN, preferred_element_type=F32)

    for bit in bits_down(lax.axis_size("narrow")):
        pick_own = pick_own + swap_narrow(pick_own, bit)
    pick_grad = pick_own.reshape(length, PKH, TOPK)
    centre = jnp.sum(mem_probs * pick_grad, axis=-1, keepdims=True)
    score_grad = (mem_probs * (pick_grad - centre)).astype(BF16).reshape(length, PICKS)
    memory_query_grad, key_grad = spread_grads(
        column_ref, picks, score_grad, memory_query, keys_full
    )

    product = (gate_act * memory).astype(BF16)
    sigmoid = jax.nn.sigmoid(gate_value)
    gate_rows_grad = (
        product_grad * memory * sigmoid * (1.0 + gate_value * (1.0 - sigmoid))
    ).astype(BF16)
    second_part = lax.dot_general(gate_rows_grad, gate_full, NT, preferred_element_type=F32)
    second_part = second_part + lax.dot_general(
        memory_query_grad, query_full, NT, preferred_element_type=F32
    )
    second_grad = lax.psum(second_part.astype(BF16), "narrow").astype(F32)

    mixer_part = lax.dot_general(product, mixer_turned, NT, preferred_element_type=F32)
    mixer_part = mixer_part.astype(BF16)
    mixer_part, second_grad = lax.optimization_barrier((mixer_part, second_grad))
    mixer_sum = lax.psum_scatter(mixer_part, "narrow", scatter_dimension=1, tiled=True).astype(F32)
    own_hidden = lax.dynamic_slice_in_dim(hidden, column * width, width, 1)
    outputs = (own_hidden + mixer_sum).astype(BF16)

    through_two, gain_two_part = norm_back(hidden, factor_two, gain_two, second_grad)
    hidden_grad = upstream.astype(F32) + through_two
    branch_grad = hidden_grad.astype(BF16)
    heads_grad = jnp.dot(branch_grad, out_turned, preferred_element_type=F32)
    heads_grad = heads_grad.astype(BF16).reshape(length, head_count, HD)

    mixer_grad = lax.dot_general(upstream, product, TN, preferred_element_type=F32)
    query_grad = lax.dot_general(second, memory_query_grad, TN, preferred_element_type=F32)
    gate_grad = lax.dot_general(second, gate_rows_grad, TN, preferred_element_type=F32)
    key_grad = jnp.transpose(
        key_grad.astype(BF16).reshape(units, shards, key_part, NKEYS), (1, 0, 2, 3)
    ).reshape(shards, units * key_part, NKEYS)

    def by_shard(block):
        return block.astype(BF16).reshape(shards, part, block.shape[1])

    early_pack = pack([by_shard(mixer_grad), by_shard(gate_grad), by_shard(query_grad), key_grad])
    early_pack, heads_grad = lax.optimization_barrier((early_pack, heads_grad))
    early_sums = sum_wide(early_pack).astype(F32)
    mixer_sums, gate_sums, query_sums, key_sums = unpack(early_sums, second_shapes[1:])

    query_back, key_back, value_back = attend_backward(
        queries, key_rows, value_rows, segment_row, logsum, heads_grad
    )
    mixed_grad = [
        member.reshape(length, width).astype(BF16)
        for member in (query_back, key_back, value_back)
    ]
    normed_part = sum(
        lax.dot_general(mixed_grad[j], qkv_full[j], NT, preferred_element_type=F32)
        for j in range(3)
    ).astype(BF16)
    normed_grad = lax.psum(normed_part, "narrow").astype(F32)
    out_grad = lax.dot_general(branch_grad, head_rows, TN, preferred_element_type=F32)
    qkv_grad = [
        lax.dot_general(normed, mixed_grad[j], TN, preferred_element_type=F32) for j in range(3)
    ]
    through_one, gain_one_part = norm_back(rows_one, factor_one, gain_one, normed_grad)
    input_full = hidden_grad + through_one
    input_grad = lax.dynamic_slice_in_dim(input_full, column * width, width, 1)
    gain_parts = jnp.concatenate(
        [gain_one_part.reshape(shards, 1, part), gain_two_part.reshape(shards, 1, part)], axis=1
    ).astype(BF16).reshape(shards, -1, LANES)
    late_pack = pack([by_shard(block) for block in qkv_grad] + [by_shard(out_grad), gain_parts])
    late_sums = sum_wide(late_pack).astype(F32)
    late_shapes = [(part, width)] * 4 + [(2 * part // LANES, LANES)]
    query_sum, key_sum, value_sum, out_sum, gain_sums = unpack(late_sums, late_shapes)
    gain_sums = gain_sums.reshape(2, part)
    return (
        outputs,
        input_grad,
        gain_sums[0],
        jnp.stack([query_sum, key_sum, value_sum], axis=1),
        out_sum.T,
        gain_sums[1],
        query_sums.reshape(part, units, NKEYS),
        key_sums.reshape(units, key_part, NKEYS),
        gate_sums,
        values_grad,
        mixer_sums.T,
    )


def solution(mesh):
    return jax.shard_map(
        per_device,
        mesh=mesh,
        in_specs=(
            P("wide", "narrow"),
            P("wide", None),
            P("wide"),
            P("wide", None, "narrow"),
            P("narrow", "wide"),
            P("wide"),
            P("wide", "narrow", None),
            P("narrow", "wide", None),
            P("wide", "narrow"),
            P("wide", "narrow"),
            P("narrow", "wide"),
            P("wide", None),
            P("wide", "narrow"),
        ),
        out_specs=(
            P("wide", "narrow"),
            P("wide", "narrow"),
            P("wide"),
            P("wide", None, "narrow"),
            P("narrow", "wide"),
            P("wide"),
            P("wide", "narrow", None),
            P("narrow", "wide", None),
            P("wide", "narrow"),
            P("wide", "narrow"),
            P("narrow", "wide"),
        ),
        check_vma=False,
    )
```

```python
import functools

import jax
import jax.numpy as jnp
from jax import lax
from jax.experimental import pallas as pl
from jax.experimental.pallas import tpu as pltpu
from jax.sharding import PartitionSpec as P

HD = 64
PKH = 4
NKEYS = 256
TOPK = 32
PICKS = 128
LANES = 128


EPSILON = 1e-06
MASKED = -1e30
BF16 = jnp.bfloat16
F32 = jnp.float32
NT = (((1,), (1,)), ((), ()))
TN = (((0,), (0,)), ((), ()))


def norm_rows(activations, gain_row):
    factor = lax.rsqrt(jnp.mean(activations * activations, axis=-1, keepdims=True) + EPSILON)
    return (factor, activations * factor * gain_row)


def masked_scores(query_block, key_rows, segment_block, segment_row, offset):
    block_rows = query_block.shape[0]
    positions = jnp.arange(key_rows.shape[0], dtype=jnp.int32)
    scores = jnp.einsum("qhd,khd->hqk", query_block, key_rows, preferred_element_type=jnp.float32)
    scores = scores * query_block.shape[2] ** (-0.5)
    allowed = (positions[None, :] <= (offset + positions[:block_rows])[:, None]) & (
        segment_block[:, None] == segment_row[None, :]
    )
    return jnp.where(allowed[None], scores, MASKED)


def attend_forward(queries, key_rows, value_rows, segment_row):
    length = queries.shape[0]
    block_rows = min(512, length)

    def one_block(number):
        offset = number * block_rows
        query_block = lax.dynamic_slice_in_dim(queries, offset, block_rows, 0)
        segment_block = lax.dynamic_slice_in_dim(segment_row, offset, block_rows, 0)
        scores = masked_scores(query_block, key_rows, segment_block, segment_row, offset)
        row_peak = jnp.max(scores, axis=-1, keepdims=True)
        raised = jnp.exp(scores - row_peak)
        totals = jnp.sum(raised, axis=-1, keepdims=True)
        attention = (raised / totals).astype(jnp.bfloat16)
        mixture = jnp.einsum(
            "hqk,khd->qhd", attention, value_rows, preferred_element_type=jnp.float32
        )
        return (mixture.astype(jnp.bfloat16), (row_peak + jnp.log(totals))[:, :, 0])

    outputs, logsum = lax.map(one_block, jnp.arange(length // block_rows, dtype=jnp.int32))
    head_width = queries.shape[1] * queries.shape[2]
    logsum = jnp.transpose(logsum, (1, 0, 2)).reshape(queries.shape[1], length)
    return (outputs.reshape(length, head_width), logsum)


def attend_backward(queries, key_rows, value_rows, segment_row, logsum, heads_grad):
    length = queries.shape[0]
    block_rows = min(512, length)
    factor = queries.shape[2] ** (-0.5)

    def one_block(running, number):
        key_sum, value_sum = running
        offset = number * block_rows
        query_block = lax.dynamic_slice_in_dim(queries, offset, block_rows, 0)
        segment_block = lax.dynamic_slice_in_dim(segment_row, offset, block_rows, 0)
        grad_block = lax.dynamic_slice_in_dim(heads_grad, offset, block_rows, 0)
        logsum_block = lax.dynamic_slice_in_dim(logsum, offset, block_rows, 1)
        scores = masked_scores(query_block, key_rows, segment_block, segment_row, offset)
        attention = jnp.exp(scores - logsum_block[:, :, None])
        prob_grad = jnp.einsum(
            "qhd,khd->hqk", grad_block, value_rows, preferred_element_type=jnp.float32
        )
        centre = jnp.sum(attention * prob_grad, axis=-1, keepdims=True)
        score_grad = (attention * (prob_grad - centre)).astype(jnp.bfloat16)
        query_grad = (
            jnp.einsum("hqk,khd->qhd", score_grad, key_rows, preferred_element_type=jnp.float32)
            * factor
        )
        key_sum = (
            key_sum
            + jnp.einsum(
                "hqk,qhd->khd", score_grad, query_block, preferred_element_type=jnp.float32
            )
            * factor
        )
        value_sum = value_sum + jnp.einsum(
            "hqk,qhd->khd",
            attention.astype(jnp.bfloat16),
            grad_block,
            preferred_element_type=jnp.float32,
        )
        return ((key_sum, value_sum), query_grad)

    empty_sum = jnp.zeros(key_rows.shape, jnp.float32)
    carried, query_parts = lax.scan(
        one_block, (empty_sum, empty_sum), jnp.arange(length // block_rows, dtype=jnp.int32)
    )
    return (query_parts.reshape(queries.shape), carried[0], carried[1])


SLOTS = 32


def params(mib):
    return pltpu.CompilerParams(vmem_limit_bytes=mib << 20)


def lane_numbers(shape):
    return lax.broadcasted_iota(jnp.int32, shape, len(shape) - 1)


def count_local(local, total):
    inside = (local >= 0) & (local < total)
    square = (LANES, LANES)
    upto = lax.broadcasted_iota(jnp.int32, square, 0) <= lax.broadcasted_iota(jnp.int32, square, 1)
    return jnp.dot(
        jnp.where(inside, 1.0, 0.0).astype(BF16),
        jnp.where(upto, 1.0, 0.0).astype(BF16),
        preferred_element_type=F32,
    )


def rounds_of(counts):
    most = jnp.max(counts[:, LANES - 1 :]).astype(jnp.int32)
    return (most + (SLOTS - 1)) // SLOTS


def compact(counts, members, start):
    target = ((lane_numbers(counts.shape) & (SLOTS - 1)) + (start + 1)).astype(F32)
    place = jnp.zeros(counts.shape, jnp.int32)
    step = LANES // 2
    while step:
        seen = jnp.take_along_axis(counts, place + (step - 1), axis=1)
        place = jnp.where(seen < target, place + step, place)
        step //= 2
    valid = target <= counts[:, LANES - 1 :]
    return valid, [jnp.take_along_axis(member, place, axis=1) for member in members]


def group_masks():
    own = lax.broadcasted_iota(jnp.int32, (8, LANES), 0)
    lane = lane_numbers((8, LANES)) // SLOTS
    per = LANES // SLOTS
    return [own == lane + per * block for block in range(8 // per)]


def lane_table(low, masks):
    ids = lax.broadcasted_iota(jnp.int32, (NKEYS, LANES), 0).astype(F32).astype(BF16)
    parts = []
    for mask in masks:
        row = jnp.sum(jnp.where(mask, low, 0.0), axis=0, keepdims=True)
        row = jnp.broadcast_to(row, (16, LANES)).astype(BF16)
        row = jnp.concatenate([row] * (NKEYS // 16), axis=0)
        parts.append(jnp.where(ids == row, jnp.ones((), BF16), jnp.zeros((), BF16)))
    return jnp.concatenate(parts, axis=1)


def bag_body(
    base_ref, picks_ref, weight_ref, table_ref, out_ref, keep_ref, counts, locals_, high, low,
    weights, *, chunk, unroll
):
    rows = picks_ref.shape[0]
    total = table_ref.shape[0]
    groups = total // NKEYS
    local = picks_ref[...] - base_ref[0]
    counts[...] = count_local(local, total)
    locals_[...] = local
    masks = group_masks()

    def eight(token):
        span = pl.ds(token, 8)
        own_high = high[span, :]
        weight = weights[span, :]
        weight = jnp.concatenate([weight, weight], axis=0).astype(BF16)
        zero = jnp.zeros((), BF16)
        parts = []
        for mask in masks:
            own = jnp.where(mask, own_high, -1.0)
            pair = jnp.concatenate([own, own - 1.0], axis=0).astype(BF16)
            rows_of = [
                jnp.where(pair == jnp.array(group, BF16), weight, zero)
                for group in range(0, groups, 2)
            ]
            parts.append(jnp.concatenate(rows_of, axis=0))
        return lax.dot_general(
            jnp.concatenate(parts, axis=1),
            lane_table(low[span, :], masks),
            NT,
            preferred_element_type=F32,
        )

    def one_round(number, first):
        members = [locals_[...], weight_ref[...].astype(F32)]
        valid, (found, weight) = compact(counts[...], members, number * SLOTS)
        high[...] = jnp.where(valid, found >> 8, -1).astype(F32)
        low[...] = (found & (NKEYS - 1)).astype(F32)
        weights[...] = weight

        def some_tokens(step, carried):
            for slot in range(unroll):
                token = pl.multiple_of((step * unroll + slot) * 16, 16)
                top = eight(token)
                bottom = eight(token + 8)
                for group in range(groups):
                    part = slice(group * 8, group * 8 + 8)
                    block = jnp.concatenate([top[part], bottom[part]], axis=0).astype(BF16)
                    span = (pl.ds(token, 16), slice(group * NKEYS, (group + 1) * NKEYS))
                    keep_ref[span] = block if first else keep_ref[span] + block
            return carried

        lax.fori_loop(0, rows // (16 * unroll), some_tokens, 0)

    def more(number, carried):
        one_round(number, False)
        return carried

    one_round(0, True)
    lax.fori_loop(1, rounds_of(counts[...]), more, 0)
    result = jnp.zeros(out_ref.shape, F32)
    for start in range(0, total, chunk):
        result = result + jnp.dot(
            keep_ref[:, pl.ds(start, chunk)],
            table_ref[pl.ds(start, chunk), :],
            preferred_element_type=F32,
        )
    out_ref[...] = result.astype(out_ref.dtype)


def bag_sums(base, picks, weights, table, rows=256, chunk=1024, unroll=8):
    amount = picks.shape[0]
    total, width = table.shape
    return pl.pallas_call(
        functools.partial(bag_body, chunk=chunk, unroll=unroll),
        grid=(amount // rows,),
        in_specs=[
            pl.BlockSpec(memory_space=pltpu.SMEM),
            pl.BlockSpec((rows, PICKS), lambda i: (i, 0)),
            pl.BlockSpec((rows, PICKS), lambda i: (i, 0)),
            pl.BlockSpec((total, width), lambda i: (0, 0)),
        ],
        out_specs=[
            pl.BlockSpec((rows, width), lambda i: (i, 0)),
            pl.BlockSpec((rows, total), lambda i: (i, 0)),
        ],
        out_shape=[
            jax.ShapeDtypeStruct((amount, width), BF16),
            jax.ShapeDtypeStruct((amount, total), BF16),
        ],
        scratch_shapes=[
            pltpu.VMEM((rows, LANES), F32),
            pltpu.VMEM((rows, LANES), jnp.int32),
            pltpu.VMEM((rows, LANES), F32),
            pltpu.VMEM((rows, LANES), F32),
            pltpu.VMEM((rows, LANES), F32),
        ],
        compiler_params=params(56),
        cost_estimate=pl.CostEstimate(
            flops=9 * amount * total * width, bytes_accessed=amount * total * 2, transcendentals=0
        ),
        name="bag_sums",
    )(base, picks, weights, table)


def picked_body(
    base_ref, picks_ref, grad_ref, table_ref, out_ref, counts, locals_, high, low, found_at, held,
    *, unroll
):
    rows = picks_ref.shape[0]
    total = table_ref.shape[1]
    groups = total // NKEYS
    local = picks_ref[...] - base_ref[0]
    counts[...] = count_local(local, total)
    locals_[...] = local
    masks = group_masks()
    grads = grad_ref[...]
    for group in range(groups):
        held[group] = jnp.dot(
            grads,
            table_ref[:, group * NKEYS : (group + 1) * NKEYS],
            preferred_element_type=F32,
        )

    def eight(token):
        span = pl.ds(token, 8)
        left = jnp.concatenate([held[group, span, :] for group in range(groups)], axis=0)
        seen = jnp.dot(
            left.astype(BF16), lane_table(low[span, :], masks), preferred_element_type=F32
        )
        own_high = high[span, :]
        result = jnp.zeros((8, LANES), F32)
        for block, mask in enumerate(masks):
            own = jnp.where(mask, own_high, -1.0)
            for group in range(groups):
                part = seen[group * 8 : group * 8 + 8, block * LANES : (block + 1) * LANES]
                result = jnp.where(own == float(group), part, result)
        found_at[span, :] = result

    def one_round(number, first):
        valid, (found,) = compact(counts[...], [locals_[...]], number * SLOTS)
        high[...] = jnp.where(valid, found >> 8, -1).astype(F32)
        low[...] = (found & (NKEYS - 1)).astype(F32)

        def some_tokens(step, carried):
            for slot in range(unroll):
                eight(pl.multiple_of((step * unroll + slot) * 8, 8))
            return carried

        lax.fori_loop(0, rows // (8 * unroll), some_tokens, 0)
        slot = counts[...].astype(jnp.int32) - (1 + number * SLOTS)
        inside = (locals_[...] >= 0) & (locals_[...] < total)
        here = (slot >= 0) & (slot < SLOTS) & inside
        token = lax.broadcasted_iota(jnp.int32, slot.shape, 0) & (LANES // SLOTS - 1)
        lane = token * SLOTS + jnp.clip(slot, 0, SLOTS - 1)
        value = jnp.take_along_axis(found_at[...], lane, axis=1)
        before = jnp.zeros(value.shape, F32) if first else out_ref[...].astype(F32)
        out_ref[...] = jnp.where(here, value, before).astype(out_ref.dtype)

    def more(number, carried):
        one_round(number, False)
        return carried

    one_round(0, True)
    lax.fori_loop(1, rounds_of(counts[...]), more, 0)


def picked_products(base, picks, grads, table, rows=256, unroll=16):
    amount, width = grads.shape
    total = table.shape[1]
    return pl.pallas_call(
        functools.partial(picked_body, unroll=unroll),
        grid=(amount // rows,),
        in_specs=[
            pl.BlockSpec(memory_space=pltpu.SMEM),
            pl.BlockSpec((rows, PICKS), lambda i: (i, 0)),
            pl.BlockSpec((rows, width), lambda i: (i, 0)),
            pl.BlockSpec((width, total), lambda i: (0, 0)),
        ],
        out_specs=pl.BlockSpec((rows, PICKS), lambda i: (i, 0)),
        out_shape=jax.ShapeDtypeStruct((amount, PICKS), BF16),
        scratch_shapes=[
            pltpu.VMEM((rows, LANES), F32),
            pltpu.VMEM((rows, LANES), jnp.int32),
            pltpu.VMEM((rows, LANES), F32),
            pltpu.VMEM((rows, LANES), F32),
            pltpu.VMEM((rows, LANES), F32),
            pltpu.VMEM((total // NKEYS, rows, NKEYS), F32),
        ],
        compiler_params=params(56),
        cost_estimate=pl.CostEstimate(
            flops=7 * amount * total * width, bytes_accessed=amount * width * 4, transcendentals=0
        ),
        name="picked_products",
    )(base, picks, grads, table)


def unit_indices(picks, number):
    return jnp.where(number % 2 == 0, picks >> 8, picks & (NKEYS - 1))


def scores_body(column_ref, picks_ref, query_ref, keys_ref, out_ref, *, units):
    picks = picks_ref[...]
    lanes = lax.broadcasted_iota(jnp.int32, picks.shape, 1)
    total = jnp.zeros(picks.shape, F32)
    for unit in range(units):
        number = column_ref[0] * units + unit
        index = unit_indices(picks, number)
        scores = lax.dot_general(
            query_ref[:, unit * NKEYS : (unit + 1) * NKEYS],
            keys_ref[unit],
            NT,
            preferred_element_type=F32,
        )
        lower = index & (LANES - 1)
        low_part = jnp.take_along_axis(scores[:, :LANES], lower, axis=1)
        high_part = jnp.take_along_axis(scores[:, LANES:], lower, axis=1)
        found = jnp.where(index < LANES, low_part, high_part)
        total = total + jnp.where(lanes // TOPK == number // 2, found, 0.0)
    out_ref[...] = total


def pick_scores(column, picks, queries, keys, rows=256):
    amount = picks.shape[0]
    units = keys.shape[0]
    return pl.pallas_call(
        functools.partial(scores_body, units=units),
        grid=(amount // rows,),
        in_specs=[
            pl.BlockSpec(memory_space=pltpu.SMEM),
            pl.BlockSpec((rows, PICKS), lambda i: (i, 0)),
            pl.BlockSpec((rows, units * NKEYS), lambda i: (i, 0)),
            pl.BlockSpec(keys.shape, lambda i: (0, 0, 0)),
        ],
        out_specs=pl.BlockSpec((rows, PICKS), lambda i: (i, 0)),
        out_shape=jax.ShapeDtypeStruct((amount, PICKS), F32),
        compiler_params=params(32),
        name="pick_scores",
    )(column, picks, queries, keys)


def spread_body(
    column_ref, picks_ref, grad_ref, query_ref, keys_ref, out_ref, sum_ref, held_index, held_grad,
    *, units
):
    rows = picks_ref.shape[0]
    held_grad[...] = grad_ref[...].astype(F32).T

    @pl.when(pl.program_id(0) == 0)
    def clear():
        sum_ref[...] = jnp.zeros_like(sum_ref)

    key_ids = lax.broadcasted_iota(jnp.int32, (NKEYS, rows), 0)
    for unit in range(units):
        number = column_ref[0] * units + unit
        first = (number // 2) * TOPK
        held_index[...] = unit_indices(picks_ref[...], number).T
        table = jnp.zeros((NKEYS, rows), F32)
        for slot in range(TOPK):
            index = held_index[pl.ds(first + slot, 1), :]
            grad = held_grad[pl.ds(first + slot, 1), :]
            table = table + jnp.where(key_ids == index, grad, 0.0)
        table = table.astype(BF16)
        span = slice(unit * NKEYS, (unit + 1) * NKEYS)
        out_ref[:, span] = lax.dot_general(
            table, keys_ref[unit], TN, preferred_element_type=F32
        ).astype(BF16)
        sum_ref[unit] += jnp.dot(table, query_ref[:, span], preferred_element_type=F32)


def spread_grads(column, picks, grads, queries, keys, rows=128):
    amount = picks.shape[0]
    units = keys.shape[0]
    return pl.pallas_call(
        functools.partial(spread_body, units=units),
        grid=(amount // rows,),
        in_specs=[
            pl.BlockSpec(memory_space=pltpu.SMEM),
            pl.BlockSpec((rows, PICKS), lambda i: (i, 0)),
            pl.BlockSpec((rows, PICKS), lambda i: (i, 0)),
            pl.BlockSpec((rows, units * NKEYS), lambda i: (i, 0)),
            pl.BlockSpec(keys.shape, lambda i: (0, 0, 0)),
        ],
        out_specs=[
            pl.BlockSpec((rows, units * NKEYS), lambda i: (i, 0)),
            pl.BlockSpec(keys.shape, lambda i: (0, 0, 0)),
        ],
        out_shape=[
            jax.ShapeDtypeStruct((amount, units * NKEYS), BF16),
            jax.ShapeDtypeStruct(keys.shape, F32),
        ],
        scratch_shapes=[pltpu.VMEM((PICKS, rows), jnp.int32), pltpu.VMEM((PICKS, rows), F32)],
        compiler_params=params(32),
        name="spread_grads",
    )(column, picks, grads, queries, keys)


def swap_narrow(block, bit):
    size = lax.axis_size("narrow")
    return lax.ppermute(block, "narrow", [(i, i ^ bit) for i in range(size)])


def gather_by_swaps(block, axis, bits):
    size = lax.axis_size(axis)
    me = lax.axis_index(axis)
    held = {0: block}
    for bit in bits:
        moved = {}
        for offset, part in held.items():
            moved[offset ^ bit] = lax.ppermute(part, axis, [(i, i ^ bit) for i in range(size)])
        held.update(moved)
    stacked = jnp.stack([held[offset] for offset in range(size)])
    return [lax.dynamic_index_in_dim(stacked, me ^ number, 0, False) for number in range(size)]


def sum_by_swaps(block, axis):
    for bit in bits_down(lax.axis_size(axis)):
        block = block + lax.ppermute(
            block, axis, [(i, i ^ bit) for i in range(lax.axis_size(axis))]
        )
    return block


def scatter_narrow(block):
    size = lax.axis_size("narrow")
    me = lax.axis_index("narrow")
    width = block.shape[1] // size
    parts = jnp.stack([block[:, n * width : (n + 1) * width] for n in range(size)])
    held = [lax.dynamic_index_in_dim(parts, me ^ offset, 0, False) for offset in range(size)]
    for bit in bits_down(size)[::-1]:
        arrived = {
            offset: swap_narrow(held[offset ^ bit].astype(BF16), bit)
            for offset in range(size)
            if not offset & (2 * bit - 1)
        }
        held = {
            offset: held[offset].astype(F32) + value.astype(F32)
            for offset, value in arrived.items()
        }
    return held[0]


def bits_down(size):
    return [1 << level for level in reversed(range(size.bit_length() - 1))]


def gather_narrow(block):
    return jnp.concatenate(
        gather_by_swaps(block, "narrow", bits_down(lax.axis_size("narrow"))), axis=1
    )


def gather_wide(block):
    return lax.all_gather(block, "wide")


def sum_wide(block):
    return lax.psum_scatter(block, "wide", scatter_dimension=0)


def lane_blocks(block):
    return jnp.concatenate(
        [block[..., start : start + LANES] for start in range(0, block.shape[-1], LANES)], axis=-2
    )


def join_lanes(blocks, rows):
    count = blocks.shape[-2] // rows
    return jnp.concatenate(
        [blocks[..., part * rows : (part + 1) * rows, :] for part in range(count)], axis=-1
    )


def pack(blocks):
    return jnp.concatenate([lane_blocks(block) for block in blocks], axis=-2)


def unpack(packed, shapes):
    result = []
    start = 0
    for rows, columns in shapes:
        stop = start + rows * columns // LANES
        result.append(join_lanes(packed[..., start:stop, :], rows))
        start = stop
    return result


def per_device(
    inputs,
    segments,
    attn_gain,
    qkv_weight,
    out_weight,
    memory_gain,
    query_weight,
    sub_keys,
    gate_weight,
    memory_values,
    memory_out,
    picks,
    cotangent,
):
    length, width = inputs.shape
    shards = lax.axis_size("wide")
    column = lax.axis_index("narrow")
    column_ref = column.astype(jnp.int32).reshape(1)
    shard_rows = memory_values.shape[0]
    base = (lax.axis_index("wide") * shard_rows).astype(jnp.int32).reshape(1)
    units = sub_keys.shape[0]
    part = qkv_weight.shape[0]
    model = part * shards
    key_part = sub_keys.shape[1]

    rows_one = gather_narrow(inputs).astype(F32)
    first_shapes = [(3 * part, width), (part, width), (2 * part // LANES, LANES)]
    first_pack = pack(
        [
            jnp.transpose(qkv_weight, (1, 0, 2)).reshape(3 * part, width),
            out_weight.T,
            jnp.concatenate([attn_gain, memory_gain]).reshape(-1, LANES),
        ]
    )
    qkv_parts, out_turned, gains = unpack(gather_wide(first_pack), first_shapes)
    qkv_full = [
        qkv_parts[:, j * part : (j + 1) * part].reshape(model, width) for j in range(3)
    ]
    gains = gains.reshape(shards, 2, part).astype(F32)
    gain_one = gains[:, 0].reshape(model)
    gain_two = gains[:, 1].reshape(model)
    second_shapes = [
        (part, width),
        (part, width),
        (part, units * NKEYS),
        (units * key_part, NKEYS),
    ]
    second_pack = pack(
        [
            memory_out.T,
            gate_weight,
            query_weight.reshape(part, units * NKEYS),
            sub_keys.reshape(units * key_part, NKEYS),
        ]
    )
    second_pack, first_pack = lax.optimization_barrier((second_pack, first_pack))
    mixer_turned, gate_full, query_full, keys_full = unpack(
        gather_wide(second_pack), second_shapes
    )
    out_turned = out_turned.reshape(model, width)
    mixer_turned = mixer_turned.reshape(model, width)
    gate_full = gate_full.reshape(model, width)
    query_full = query_full.reshape(model, units * NKEYS)
    keys_full = jnp.transpose(
        keys_full.reshape(shards, units, key_part, NKEYS), (1, 0, 2, 3)
    ).reshape(units, NKEYS, NKEYS)
    out_all = gather_narrow(out_turned)
    upstream = gather_narrow(cotangent)
    all_picks = jnp.concatenate(
        gather_by_swaps(picks.astype(jnp.uint16), "wide", bits_down(shards)[::-1]), axis=0
    ).astype(jnp.int32)

    factor_one, normed = norm_rows(rows_one, gain_one)
    normed = normed.astype(BF16)
    mixture = [
        jnp.dot(normed, qkv_full[j], preferred_element_type=F32).astype(BF16) for j in range(3)
    ]
    head_count = width // HD
    queries, key_rows, value_rows = [
        member.reshape(length, head_count, HD) for member in mixture
    ]
    segment_row = segments[0]
    head_rows, logsum = attend_forward(queries, key_rows, value_rows, segment_row)
    head_all = gather_narrow(head_rows)
    hidden = rows_one + lax.dot_general(head_all, out_all, NT, preferred_element_type=F32)
    factor_two, second = norm_rows(hidden, gain_two)
    second = second.astype(BF16)

    gate_value = jnp.dot(second, gate_full, preferred_element_type=F32)
    gate_act = jax.nn.silu(gate_value)
    product_grad = jnp.dot(upstream, mixer_turned, preferred_element_type=F32)
    memory_grad = (product_grad * gate_act).astype(BF16)
    all_grads = gather_wide(memory_grad).reshape(shards * length, width)

    memory_query = jnp.dot(second, query_full, preferred_element_type=F32).astype(BF16)
    own_scores = pick_scores(column_ref, picks, memory_query, keys_full)
    mem_scores = sum_by_swaps(own_scores, "narrow").reshape(length, PKH, TOPK)
    score_peak = jnp.max(mem_scores, axis=-1, keepdims=True)
    raised = jnp.exp(mem_scores - score_peak)
    mem_probs = raised / jnp.sum(raised, axis=-1, keepdims=True)
    pick_weights = mem_probs.astype(BF16).reshape(length, PICKS)
    pick_weights, memory_grad = lax.optimization_barrier((pick_weights, memory_grad))
    all_weights = gather_wide(pick_weights).reshape(shards * length, PICKS)

    pick_part = picked_products(base, all_picks, all_grads, memory_values.T)
    all_weights, pick_part = lax.optimization_barrier((all_weights, pick_part))
    memory_part, tables = bag_sums(base, all_picks, all_weights, memory_values)
    pick_own = sum_wide(pick_part.reshape(shards, length, PICKS)).astype(F32)
    memory_part, pick_own = lax.optimization_barrier((memory_part, pick_own))
    memory = sum_wide(memory_part.reshape(shards, length, width)).astype(F32)
    tables, pick_own = lax.optimization_barrier((tables, pick_own))
    values_grad = lax.dot_general(tables, all_grads, TN, preferred_element_type=F32)

    pick_grad = sum_by_swaps(pick_own, "narrow").reshape(length, PKH, TOPK)
    centre = jnp.sum(mem_probs * pick_grad, axis=-1, keepdims=True)
    score_grad = (mem_probs * (pick_grad - centre)).astype(BF16).reshape(length, PICKS)
    memory_query_grad, key_grad = spread_grads(
        column_ref, picks, score_grad, memory_query, keys_full
    )

    product = (gate_act * memory).astype(BF16)
    sigmoid = jax.nn.sigmoid(gate_value)
    gate_rows_grad = (
        product_grad * memory * sigmoid * (1.0 + gate_value * (1.0 - sigmoid))
    ).astype(BF16)
    second_part = lax.dot_general(gate_rows_grad, gate_full, NT, preferred_element_type=F32)
    second_part = second_part + lax.dot_general(
        memory_query_grad, query_full, NT, preferred_element_type=F32
    )
    turned = second_part * gain_two
    inner_part = jnp.sum(turned * hidden, axis=-1)
    gain_two_part = jnp.sum(second_part * hidden * factor_two, axis=0)
    tiny = sum_by_swaps(jnp.concatenate([inner_part, gain_two_part]), "narrow")
    inner_two = tiny[:length, None] / model
    gain_two_part = tiny[length:]
    own_second_grad = scatter_narrow(second_part)

    def own_columns(block):
        return lax.dynamic_slice_in_dim(block, column * width, width, block.ndim - 1)

    own_hidden = own_columns(hidden)
    own_hidden_grad = (
        cotangent.astype(F32)
        + factor_two * own_columns(gain_two) * own_second_grad
        - own_hidden * (factor_two * factor_two * factor_two) * inner_two
    )
    branch_grad = gather_narrow(own_hidden_grad.astype(BF16))

    mixer_part = lax.dot_general(product, mixer_turned, NT, preferred_element_type=F32)
    mixer_part, branch_grad = lax.optimization_barrier((mixer_part, branch_grad))
    outputs = (own_hidden + scatter_narrow(mixer_part)).astype(BF16)

    heads_grad = jnp.dot(branch_grad, out_turned, preferred_element_type=F32)
    heads_grad = heads_grad.astype(BF16).reshape(length, head_count, HD)

    mixer_grad = lax.dot_general(upstream, product, TN, preferred_element_type=F32)
    query_grad = lax.dot_general(second, memory_query_grad, TN, preferred_element_type=F32)
    gate_grad = lax.dot_general(second, gate_rows_grad, TN, preferred_element_type=F32)
    key_grad = jnp.transpose(
        key_grad.astype(BF16).reshape(units, shards, key_part, NKEYS), (1, 0, 2, 3)
    ).reshape(shards, units * key_part, NKEYS)

    def by_shard(block):
        return block.astype(BF16).reshape(shards, part, block.shape[1])

    early_pack = pack([by_shard(mixer_grad), by_shard(gate_grad), by_shard(query_grad), key_grad])
    early_pack, heads_grad = lax.optimization_barrier((early_pack, heads_grad))
    early_sums = sum_wide(early_pack).astype(F32)
    mixer_sums, gate_sums, query_sums, key_sums = unpack(early_sums, second_shapes)

    query_back, key_back, value_back = attend_backward(
        queries, key_rows, value_rows, segment_row, logsum, heads_grad
    )
    mixed_grad = [
        member.reshape(length, width).astype(BF16)
        for member in (query_back, key_back, value_back)
    ]
    normed_part = sum(
        lax.dot_general(mixed_grad[j], qkv_full[j], NT, preferred_element_type=F32)
        for j in range(3)
    )
    out_grad = lax.dot_general(branch_grad, head_rows, TN, preferred_element_type=F32)
    qkv_grad = [
        lax.dot_general(normed, mixed_grad[j], TN, preferred_element_type=F32) for j in range(3)
    ]
    inner_part = jnp.sum(normed_part * gain_one * rows_one, axis=-1)
    gain_one_part = jnp.sum(normed_part * rows_one * factor_one, axis=0)
    tiny = sum_by_swaps(jnp.concatenate([inner_part, gain_one_part]), "narrow")
    inner_one = tiny[:length, None] / model
    gain_one_part = tiny[length:]
    own_normed_grad = scatter_narrow(normed_part)
    input_grad = (
        own_hidden_grad
        + factor_one * own_columns(gain_one) * own_normed_grad
        - inputs.astype(F32) * (factor_one * factor_one * factor_one) * inner_one
    )
    gain_parts = jnp.concatenate(
        [gain_one_part.reshape(shards, 1, part), gain_two_part.reshape(shards, 1, part)], axis=1
    ).astype(BF16).reshape(shards, -1, LANES)
    late_pack = pack([by_shard(block) for block in qkv_grad] + [by_shard(out_grad), gain_parts])
    late_sums = sum_wide(late_pack).astype(F32)
    late_shapes = [(part, width)] * 4 + [(2 * part // LANES, LANES)]
    query_sum, key_sum, value_sum, out_sum, gain_sums = unpack(late_sums, late_shapes)
    gain_sums = gain_sums.reshape(2, part)
    return (
        outputs,
        input_grad,
        gain_sums[0],
        jnp.stack([query_sum, key_sum, value_sum], axis=1),
        out_sum.T,
        gain_sums[1],
        query_sums.reshape(part, units, NKEYS),
        key_sums.reshape(units, key_part, NKEYS),
        gate_sums,
        values_grad,
        mixer_sums.T,
    )


def solution(mesh):
    return jax.shard_map(
        per_device,
        mesh=mesh,
        in_specs=(
            P("wide", "narrow"),
            P("wide", None),
            P("wide"),
            P("wide", None, "narrow"),
            P("narrow", "wide"),
            P("wide"),
            P("wide", "narrow", None),
            P("narrow", "wide", None),
            P("wide", "narrow"),
            P("wide", "narrow"),
            P("narrow", "wide"),
            P("wide", None),
            P("wide", "narrow"),
        ),
        out_specs=(
            P("wide", "narrow"),
            P("wide", "narrow"),
            P("wide"),
            P("wide", None, "narrow"),
            P("narrow", "wide"),
            P("wide"),
            P("wide", "narrow", None),
            P("narrow", "wide", None),
            P("wide", "narrow"),
            P("wide", "narrow"),
            P("narrow", "wide"),
        ),
        check_vma=False,
    )
```

```python
import functools

import jax
import jax.numpy as jnp
from jax import lax
from jax.experimental import pallas as pl
from jax.experimental.pallas import tpu as pltpu
from jax.sharding import PartitionSpec as P

HD = 64
PKH = 4
NKEYS = 256
TOPK = 32
PICKS = 128
DOCS = 3
DOC_MOST = 512
LANES = 128
PARTS = 2


EPSILON = 1e-06
MASKED = -1e30
BF16 = jnp.bfloat16
F32 = jnp.float32
NT = (((1,), (1,)), ((), ()))
TN = (((0,), (0,)), ((), ()))


def norm_rows(activations, gain_row):
    factor = lax.rsqrt(jnp.mean(activations * activations, axis=-1, keepdims=True) + EPSILON)
    return (factor, activations * factor * gain_row)


def document_starts(segment_row):
    starts = jnp.zeros(segment_row.shape, jnp.int32)
    for number in range(1, DOCS):
        before = jnp.sum((segment_row == number - 1).astype(jnp.int32))
        starts = starts + jnp.where(segment_row >= number, before, 0)
    return starts


def key_window(block, rows):
    first = max(0, (block * rows - (DOC_MOST - 1)) // rows * rows)
    return first, (block + 1) * rows


def head_lanes(shape, head, axis):
    return lax.broadcasted_iota(jnp.int32, shape, axis) // HD == head


def turned_probs(keys, queries, starts, first, offset):
    scores = lax.dot_general(keys, queries, NT, preferred_element_type=F32) * HD ** (-0.5)
    key_ids = lax.broadcasted_iota(jnp.int32, scores.shape, 0) + first
    query_ids = lax.broadcasted_iota(jnp.int32, scores.shape, 1) + offset
    allowed = (key_ids >= starts) & (key_ids <= query_ids)
    scores = jnp.where(allowed, scores, MASKED)
    raised = jnp.exp(scores - jnp.max(scores, axis=0, keepdims=True))
    return raised * (1.0 / jnp.sum(raised, axis=0, keepdims=True))


def attend_body(start_ref, query_ref, key_ref, value_ref, out_ref, *, rows):
    length = query_ref.shape[0]
    values_turned = value_ref[...].T
    for block in range(length // rows):
        first, last = key_window(block, rows)
        span = slice(block * rows, last)
        queries = query_ref[span, :]
        mixture = jnp.zeros((LANES, rows), F32)
        for head in range(LANES // HD):
            own = jnp.where(head_lanes(queries.shape, head, 1), queries, jnp.zeros((), BF16))
            probs = turned_probs(
                key_ref[first:last, :], own, start_ref[:, span], first, block * rows
            )
            part = jnp.dot(
                values_turned[:, first:last], probs.astype(BF16), preferred_element_type=F32
            )
            mixture = jnp.where(head_lanes(part.shape, head, 0), part, mixture)
        out_ref[span, :] = mixture.T.astype(BF16)


def attend_forward(starts, queries, key_rows, value_rows, rows=256):
    length, width = queries.shape
    column = pl.BlockSpec((length, LANES), lambda i: (0, i))
    return pl.pallas_call(
        functools.partial(attend_body, rows=rows),
        grid=(width // LANES,),
        in_specs=[pl.BlockSpec((1, length), lambda i: (0, 0)), column, column, column],
        out_specs=column,
        out_shape=jax.ShapeDtypeStruct((length, width), BF16),
        compiler_params=params(32),
        cost_estimate=pl.CostEstimate(
            flops=16 * length * length * width, bytes_accessed=8 * length * width, transcendentals=0
        ),
        name="attend_forward",
    )(starts, queries, key_rows, value_rows)


def attend_back_body(
    start_ref, query_ref, key_ref, value_ref, grad_ref, dq_ref, dk_ref, dv_ref, key_sum, value_sum,
    *, rows
):
    length = query_ref.shape[0]
    keys_turned = key_ref[...].T
    key_sum[...] = jnp.zeros_like(key_sum)
    value_sum[...] = jnp.zeros_like(value_sum)
    zero = jnp.zeros((), BF16)
    factor = HD ** (-0.5)
    for block in range(length // rows):
        first, last = key_window(block, rows)
        span = slice(block * rows, last)
        window = slice(first, last)
        queries = query_ref[span, :]
        grads = grad_ref[span, :]
        query_sum = jnp.zeros((LANES, rows), F32)
        for head in range(LANES // HD):
            mask = head_lanes(queries.shape, head, 1)
            own = jnp.where(mask, queries, zero)
            own_grads = jnp.where(mask, grads, zero)
            probs = turned_probs(key_ref[window, :], own, start_ref[:, span], first, block * rows)
            prob_grad = lax.dot_general(
                value_ref[window, :], own_grads, NT, preferred_element_type=F32
            )
            centre = jnp.sum(probs * prob_grad, axis=0, keepdims=True)
            score_grad = (probs * (prob_grad - centre)).astype(BF16)
            part = jnp.dot(keys_turned[:, window], score_grad, preferred_element_type=F32)
            query_sum = jnp.where(head_lanes(part.shape, head, 0), part, query_sum)
            key_sum[window, :] += jnp.dot(score_grad, own, preferred_element_type=F32)
            value_sum[window, :] += jnp.dot(
                probs.astype(BF16), own_grads, preferred_element_type=F32
            )
        dq_ref[span, :] = (query_sum.T * factor).astype(BF16)
    dk_ref[...] = (key_sum[...] * factor).astype(BF16)
    dv_ref[...] = value_sum[...].astype(BF16)


def attend_backward(starts, queries, key_rows, value_rows, heads_grad, rows=256):
    length, width = queries.shape
    column = pl.BlockSpec((length, LANES), lambda i: (0, i))
    return pl.pallas_call(
        functools.partial(attend_back_body, rows=rows),
        grid=(width // LANES,),
        in_specs=[pl.BlockSpec((1, length), lambda i: (0, 0))] + [column] * 4,
        out_specs=[column] * 3,
        out_shape=[jax.ShapeDtypeStruct((length, width), BF16)] * 3,
        scratch_shapes=[pltpu.VMEM((length, LANES), F32)] * 2,
        compiler_params=params(40),
        cost_estimate=pl.CostEstimate(
            flops=40 * length * length * width,
            bytes_accessed=14 * length * width,
            transcendentals=0,
        ),
        name="attend_backward",
    )(starts, queries, key_rows, value_rows, heads_grad)


SLOTS = 32


def params(mib):
    return pltpu.CompilerParams(vmem_limit_bytes=mib << 20)


def lane_numbers(shape):
    return lax.broadcasted_iota(jnp.int32, shape, len(shape) - 1)


def count_local(local, total):
    inside = (local >= 0) & (local < total)
    square = (LANES, LANES)
    upto = lax.broadcasted_iota(jnp.int32, square, 0) <= lax.broadcasted_iota(jnp.int32, square, 1)
    return jnp.dot(
        jnp.where(inside, 1.0, 0.0).astype(BF16),
        jnp.where(upto, 1.0, 0.0).astype(BF16),
        preferred_element_type=F32,
    )


def rounds_of(counts):
    most = jnp.max(counts[:, LANES - 1 :]).astype(jnp.int32)
    return (most + (SLOTS - 1)) // SLOTS


def compact(counts, members, start):
    target = ((lane_numbers(counts.shape) & (SLOTS - 1)) + (start + 1)).astype(F32)
    place = jnp.zeros(counts.shape, jnp.int32)
    step = LANES // 2
    while step:
        seen = jnp.take_along_axis(counts, place + (step - 1), axis=1)
        place = jnp.where(seen < target, place + step, place)
        step //= 2
    valid = target <= counts[:, LANES - 1 :]
    return valid, [jnp.take_along_axis(member, place, axis=1) for member in members]


def group_masks():
    own = lax.broadcasted_iota(jnp.int32, (8, LANES), 0)
    lane = lane_numbers((8, LANES)) // SLOTS
    per = LANES // SLOTS
    return [own == lane + per * block for block in range(8 // per)]


def lane_table(low, masks):
    ids = lax.broadcasted_iota(jnp.int32, (NKEYS, LANES), 0).astype(F32).astype(BF16)
    parts = []
    for mask in masks:
        row = jnp.sum(jnp.where(mask, low, 0.0), axis=0, keepdims=True)
        row = jnp.broadcast_to(row, (16, LANES)).astype(BF16)
        row = jnp.concatenate([row] * (NKEYS // 16), axis=0)
        parts.append(jnp.where(ids == row, jnp.ones((), BF16), jnp.zeros((), BF16)))
    return jnp.concatenate(parts, axis=1)


def bag_body(
    base_ref, picks_ref, weight_ref, table_ref, before_ref, out_ref, keep_ref, counts, locals_,
    high, low, weights, *, chunk, unroll
):
    del before_ref
    rows = picks_ref.shape[0]
    total = table_ref.shape[0]
    groups = total // NKEYS
    local = picks_ref[...] - base_ref[0]
    counts[...] = count_local(local, total)
    locals_[...] = local
    masks = group_masks()

    def eight(token):
        span = pl.ds(token, 8)
        own_high = high[span, :]
        weight = weights[span, :]
        weight = jnp.concatenate([weight, weight], axis=0).astype(BF16)
        zero = jnp.zeros((), BF16)
        parts = []
        for mask in masks:
            own = jnp.where(mask, own_high, -1.0)
            pair = jnp.concatenate([own, own - 1.0], axis=0).astype(BF16)
            rows_of = [
                jnp.where(pair == jnp.array(group, BF16), weight, zero)
                for group in range(0, groups, 2)
            ]
            parts.append(jnp.concatenate(rows_of, axis=0))
        return lax.dot_general(
            jnp.concatenate(parts, axis=1),
            lane_table(low[span, :], masks),
            NT,
            preferred_element_type=F32,
        )

    def one_round(number, first):
        members = [locals_[...], weight_ref[...].astype(F32)]
        valid, (found, weight) = compact(counts[...], members, number * SLOTS)
        high[...] = jnp.where(valid, found >> 8, -1).astype(F32)
        low[...] = (found & (NKEYS - 1)).astype(F32)
        weights[...] = weight

        def some_tokens(step, carried):
            for slot in range(unroll):
                token = pl.multiple_of((step * unroll + slot) * 16, 16)
                top = eight(token)
                bottom = eight(token + 8)
                for group in range(groups):
                    part = slice(group * 8, group * 8 + 8)
                    block = jnp.concatenate([top[part], bottom[part]], axis=0).astype(BF16)
                    span = (pl.ds(token, 16), slice(group * NKEYS, (group + 1) * NKEYS))
                    keep_ref[span] = block if first else keep_ref[span] + block
            return carried

        lax.fori_loop(0, rows // (16 * unroll), some_tokens, 0)

    def more(number, carried):
        one_round(number, False)
        return carried

    one_round(0, True)
    lax.fori_loop(1, rounds_of(counts[...]), more, 0)
    result = jnp.zeros(out_ref.shape, F32)
    for start in range(0, total, chunk):
        result = result + jnp.dot(
            keep_ref[:, pl.ds(start, chunk)],
            table_ref[pl.ds(start, chunk), :],
            preferred_element_type=F32,
        )
    out_ref[...] = result.astype(out_ref.dtype)


def bag_sums(base, picks, weights, table, before, part, parts, shards, rows=256, chunk=1024,
             unroll=8):
    amount = picks.shape[0]
    total, width = table.shape
    whole = amount // shards // rows
    count = whole // parts

    def place(i):
        return (i // count * whole + part * count + i % count, 0)

    kept = jax.ShapeDtypeStruct((amount, total), BF16)
    return pl.pallas_call(
        functools.partial(bag_body, chunk=chunk, unroll=unroll),
        grid=(shards * count,),
        in_specs=[
            pl.BlockSpec(memory_space=pltpu.SMEM),
            pl.BlockSpec((rows, PICKS), place),
            pl.BlockSpec((rows, PICKS), place),
            pl.BlockSpec((total, width), lambda i: (0, 0)),
            pl.BlockSpec(memory_space=pl.ANY),
        ],
        out_specs=[
            pl.BlockSpec((rows, width), lambda i: (i, 0)),
            pl.BlockSpec((rows, total), place),
        ],
        out_shape=[jax.ShapeDtypeStruct((amount // parts, width), BF16), kept],
        scratch_shapes=[
            pltpu.VMEM((rows, LANES), F32),
            pltpu.VMEM((rows, LANES), jnp.int32),
            pltpu.VMEM((rows, LANES), F32),
            pltpu.VMEM((rows, LANES), F32),
            pltpu.VMEM((rows, LANES), F32),
        ],
        input_output_aliases={} if before is None else {4: 1},
        compiler_params=params(56),
        cost_estimate=pl.CostEstimate(
            flops=9 * amount * total * width // parts,
            bytes_accessed=amount * total * 2 // parts,
            transcendentals=0,
        ),
        name="bag_sums",
    )(base, picks, weights, table, base if before is None else before)


def picked_body(
    base_ref, picks_ref, grad_ref, table_ref, out_ref, counts, locals_, high, low, found_at, held,
    *, unroll
):
    rows = picks_ref.shape[0]
    total = table_ref.shape[1]
    groups = total // NKEYS
    local = picks_ref[...] - base_ref[0]
    counts[...] = count_local(local, total)
    locals_[...] = local
    masks = group_masks()
    grads = grad_ref[...]
    for group in range(groups):
        held[group] = jnp.dot(
            grads,
            table_ref[:, group * NKEYS : (group + 1) * NKEYS],
            preferred_element_type=F32,
        )

    def eight(token):
        span = pl.ds(token, 8)
        left = jnp.concatenate([held[group, span, :] for group in range(groups)], axis=0)
        seen = jnp.dot(
            left.astype(BF16), lane_table(low[span, :], masks), preferred_element_type=F32
        )
        own_high = high[span, :]
        result = jnp.zeros((8, LANES), F32)
        for block, mask in enumerate(masks):
            own = jnp.where(mask, own_high, -1.0)
            for group in range(groups):
                part = seen[group * 8 : group * 8 + 8, block * LANES : (block + 1) * LANES]
                result = jnp.where(own == float(group), part, result)
        found_at[span, :] = result

    def one_round(number, first):
        valid, (found,) = compact(counts[...], [locals_[...]], number * SLOTS)
        high[...] = jnp.where(valid, found >> 8, -1).astype(F32)
        low[...] = (found & (NKEYS - 1)).astype(F32)

        def some_tokens(step, carried):
            for slot in range(unroll):
                eight(pl.multiple_of((step * unroll + slot) * 8, 8))
            return carried

        lax.fori_loop(0, rows // (8 * unroll), some_tokens, 0)
        slot = counts[...].astype(jnp.int32) - (1 + number * SLOTS)
        inside = (locals_[...] >= 0) & (locals_[...] < total)
        here = (slot >= 0) & (slot < SLOTS) & inside
        token = lax.broadcasted_iota(jnp.int32, slot.shape, 0) & (LANES // SLOTS - 1)
        lane = token * SLOTS + jnp.clip(slot, 0, SLOTS - 1)
        value = jnp.take_along_axis(found_at[...], lane, axis=1)
        before = jnp.zeros(value.shape, F32) if first else out_ref[...].astype(F32)
        out_ref[...] = jnp.where(here, value, before).astype(out_ref.dtype)

    def more(number, carried):
        one_round(number, False)
        return carried

    one_round(0, True)
    lax.fori_loop(1, rounds_of(counts[...]), more, 0)


def picked_products(base, picks, grads, table, rows=256, unroll=16):
    amount, width = grads.shape
    total = table.shape[1]
    return pl.pallas_call(
        functools.partial(picked_body, unroll=unroll),
        grid=(amount // rows,),
        in_specs=[
            pl.BlockSpec(memory_space=pltpu.SMEM),
            pl.BlockSpec((rows, PICKS), lambda i: (i, 0)),
            pl.BlockSpec((rows, width), lambda i: (i, 0)),
            pl.BlockSpec((width, total), lambda i: (0, 0)),
        ],
        out_specs=pl.BlockSpec((rows, PICKS), lambda i: (i, 0)),
        out_shape=jax.ShapeDtypeStruct((amount, PICKS), BF16),
        scratch_shapes=[
            pltpu.VMEM((rows, LANES), F32),
            pltpu.VMEM((rows, LANES), jnp.int32),
            pltpu.VMEM((rows, LANES), F32),
            pltpu.VMEM((rows, LANES), F32),
            pltpu.VMEM((rows, LANES), F32),
            pltpu.VMEM((total // NKEYS, rows, NKEYS), F32),
        ],
        compiler_params=params(56),
        cost_estimate=pl.CostEstimate(
            flops=7 * amount * total * width, bytes_accessed=amount * width * 4, transcendentals=0
        ),
        name="picked_products",
    )(base, picks, grads, table)


def unit_indices(picks, number):
    return jnp.where(number % 2 == 0, picks >> 8, picks & (NKEYS - 1))


def scores_body(column_ref, picks_ref, query_ref, keys_ref, out_ref, *, units):
    picks = picks_ref[...]
    lanes = lax.broadcasted_iota(jnp.int32, picks.shape, 1)
    total = jnp.zeros(picks.shape, F32)
    for unit in range(units):
        number = column_ref[0] * units + unit
        index = unit_indices(picks, number)
        scores = lax.dot_general(
            query_ref[:, unit * NKEYS : (unit + 1) * NKEYS],
            keys_ref[unit],
            NT,
            preferred_element_type=F32,
        )
        lower = index & (LANES - 1)
        low_part = jnp.take_along_axis(scores[:, :LANES], lower, axis=1)
        high_part = jnp.take_along_axis(scores[:, LANES:], lower, axis=1)
        found = jnp.where(index < LANES, low_part, high_part)
        total = total + jnp.where(lanes // TOPK == number // 2, found, 0.0)
    out_ref[...] = total


def pick_scores(column, picks, queries, keys, rows=256):
    amount = picks.shape[0]
    units = keys.shape[0]
    return pl.pallas_call(
        functools.partial(scores_body, units=units),
        grid=(amount // rows,),
        in_specs=[
            pl.BlockSpec(memory_space=pltpu.SMEM),
            pl.BlockSpec((rows, PICKS), lambda i: (i, 0)),
            pl.BlockSpec((rows, units * NKEYS), lambda i: (i, 0)),
            pl.BlockSpec(keys.shape, lambda i: (0, 0, 0)),
        ],
        out_specs=pl.BlockSpec((rows, PICKS), lambda i: (i, 0)),
        out_shape=jax.ShapeDtypeStruct((amount, PICKS), F32),
        compiler_params=params(32),
        name="pick_scores",
    )(column, picks, queries, keys)


def spread_body(
    column_ref, picks_ref, grad_ref, query_ref, keys_ref, out_ref, sum_ref, held_index, held_grad,
    *, units
):
    rows = picks_ref.shape[0]
    held_grad[...] = grad_ref[...].astype(F32).T

    @pl.when(pl.program_id(0) == 0)
    def clear():
        sum_ref[...] = jnp.zeros_like(sum_ref)

    key_ids = lax.broadcasted_iota(jnp.int32, (NKEYS, rows), 0)
    for unit in range(units):
        number = column_ref[0] * units + unit
        first = (number // 2) * TOPK
        held_index[...] = unit_indices(picks_ref[...], number).T
        table = jnp.zeros((NKEYS, rows), F32)
        for slot in range(TOPK):
            index = held_index[pl.ds(first + slot, 1), :]
            grad = held_grad[pl.ds(first + slot, 1), :]
            table = table + jnp.where(key_ids == index, grad, 0.0)
        table = table.astype(BF16)
        span = slice(unit * NKEYS, (unit + 1) * NKEYS)
        out_ref[:, span] = lax.dot_general(
            table, keys_ref[unit], TN, preferred_element_type=F32
        ).astype(BF16)
        sum_ref[unit] += jnp.dot(table, query_ref[:, span], preferred_element_type=F32)


def spread_grads(column, picks, grads, queries, keys, rows=128):
    amount = picks.shape[0]
    units = keys.shape[0]
    return pl.pallas_call(
        functools.partial(spread_body, units=units),
        grid=(amount // rows,),
        in_specs=[
            pl.BlockSpec(memory_space=pltpu.SMEM),
            pl.BlockSpec((rows, PICKS), lambda i: (i, 0)),
            pl.BlockSpec((rows, PICKS), lambda i: (i, 0)),
            pl.BlockSpec((rows, units * NKEYS), lambda i: (i, 0)),
            pl.BlockSpec(keys.shape, lambda i: (0, 0, 0)),
        ],
        out_specs=[
            pl.BlockSpec((rows, units * NKEYS), lambda i: (i, 0)),
            pl.BlockSpec(keys.shape, lambda i: (0, 0, 0)),
        ],
        out_shape=[
            jax.ShapeDtypeStruct((amount, units * NKEYS), BF16),
            jax.ShapeDtypeStruct(keys.shape, F32),
        ],
        scratch_shapes=[pltpu.VMEM((PICKS, rows), jnp.int32), pltpu.VMEM((PICKS, rows), F32)],
        compiler_params=params(32),
        name="spread_grads",
    )(column, picks, grads, queries, keys)


def swap_narrow(block, bit):
    size = lax.axis_size("narrow")
    return lax.ppermute(block, "narrow", [(i, i ^ bit) for i in range(size)])


def swap_all(held, axis, bit):
    pairs = [(i, i ^ bit) for i in range(lax.axis_size(axis))]
    moved = {offset ^ bit: lax.ppermute(part, axis, pairs) for offset, part in held.items()}
    return {**held, **moved}


def in_order(held, axis):
    me = lax.axis_index(axis)
    size = lax.axis_size(axis)
    stacked = jnp.stack([held[offset] for offset in range(size)])
    return [lax.dynamic_index_in_dim(stacked, me ^ number, 0, False) for number in range(size)]


def gather_by_swaps(block, axis, bits):
    held = {0: block}
    for bit in bits:
        held = swap_all(held, axis, bit)
    return in_order(held, axis)


def sum_by_swaps(block, axis):
    for bit in bits_down(lax.axis_size(axis)):
        block = block + lax.ppermute(
            block, axis, [(i, i ^ bit) for i in range(lax.axis_size(axis))]
        )
    return block


def scatter_narrow(block):
    size = lax.axis_size("narrow")
    me = lax.axis_index("narrow")
    width = block.shape[1] // size
    parts = jnp.stack([block[:, n * width : (n + 1) * width] for n in range(size)])
    held = [lax.dynamic_index_in_dim(parts, me ^ offset, 0, False) for offset in range(size)]
    for bit in bits_down(size)[::-1]:
        arrived = {
            offset: swap_narrow(held[offset ^ bit].astype(BF16), bit)
            for offset in range(size)
            if not offset & (2 * bit - 1)
        }
        held = {
            offset: held[offset].astype(F32) + value.astype(F32)
            for offset, value in arrived.items()
        }
    return held[0]


def bits_down(size):
    return [1 << level for level in reversed(range(size.bit_length() - 1))]


def gather_narrow(block):
    return jnp.concatenate(
        gather_by_swaps(block, "narrow", bits_down(lax.axis_size("narrow"))), axis=1
    )


def gather_wide(block):
    return lax.all_gather(block, "wide")


def sum_wide(block):
    return lax.psum_scatter(block, "wide", scatter_dimension=0)


def lane_blocks(block):
    return jnp.concatenate(
        [block[..., start : start + LANES] for start in range(0, block.shape[-1], LANES)], axis=-2
    )


def join_lanes(blocks, rows):
    count = blocks.shape[-2] // rows
    return jnp.concatenate(
        [blocks[..., part * rows : (part + 1) * rows, :] for part in range(count)], axis=-1
    )


def pack(blocks):
    return jnp.concatenate([lane_blocks(block) for block in blocks], axis=-2)


def unpack(packed, shapes):
    result = []
    start = 0
    for rows, columns in shapes:
        stop = start + rows * columns // LANES
        result.append(join_lanes(packed[..., start:stop, :], rows))
        start = stop
    return result


def per_device(
    inputs,
    segments,
    attn_gain,
    qkv_weight,
    out_weight,
    memory_gain,
    query_weight,
    sub_keys,
    gate_weight,
    memory_values,
    memory_out,
    picks,
    cotangent,
):
    length, width = inputs.shape
    shards = lax.axis_size("wide")
    column = lax.axis_index("narrow")
    column_ref = column.astype(jnp.int32).reshape(1)
    shard_rows = memory_values.shape[0]
    base = (lax.axis_index("wide") * shard_rows).astype(jnp.int32).reshape(1)
    units = sub_keys.shape[0]
    part = qkv_weight.shape[0]
    model = part * shards
    key_part = sub_keys.shape[1]

    rows_one = gather_narrow(inputs).astype(F32)
    first_shapes = [(3 * part, width), (part, width), (2 * part // LANES, LANES)]
    first_pack = pack(
        [
            jnp.transpose(qkv_weight, (1, 0, 2)).reshape(3 * part, width),
            out_weight.T,
            jnp.concatenate([attn_gain, memory_gain]).reshape(-1, LANES),
        ]
    )
    qkv_parts, out_turned, gains = unpack(gather_wide(first_pack), first_shapes)
    qkv_full = [
        qkv_parts[:, j * part : (j + 1) * part].reshape(model, width) for j in range(3)
    ]
    gains = gains.reshape(shards, 2, part).astype(F32)
    gain_one = gains[:, 0].reshape(model)
    gain_two = gains[:, 1].reshape(model)
    second_shapes = [
        (part, width),
        (part, width),
        (part, units * NKEYS),
        (units * key_part, NKEYS),
    ]
    second_pack = pack(
        [
            memory_out.T,
            gate_weight,
            query_weight.reshape(part, units * NKEYS),
            sub_keys.reshape(units * key_part, NKEYS),
        ]
    )
    second_pack, first_pack = lax.optimization_barrier((second_pack, first_pack))
    mixer_turned, gate_full, query_full, keys_full = unpack(
        gather_wide(second_pack), second_shapes
    )
    out_turned = out_turned.reshape(model, width)
    mixer_turned = mixer_turned.reshape(model, width)
    gate_full = gate_full.reshape(model, width)
    query_full = query_full.reshape(model, units * NKEYS)
    keys_full = jnp.transpose(
        keys_full.reshape(shards, units, key_part, NKEYS), (1, 0, 2, 3)
    ).reshape(units, NKEYS, NKEYS)
    out_all = gather_narrow(out_turned)
    upstream = gather_narrow(cotangent)
    moving = {0: picks.astype(jnp.uint16)}
    bits = bits_down(shards)
    moving = swap_all(moving, "wide", bits[0])
    rows_one, moving = lax.optimization_barrier((rows_one, moving))
    for bit in bits[1:-1]:
        moving = swap_all(moving, "wide", bit)

    factor_one, normed = norm_rows(rows_one, gain_one)
    normed = normed.astype(BF16)
    normed, moving = lax.optimization_barrier((normed, moving))
    moving = swap_all(moving, "wide", bits[-1])
    queries, key_rows, value_rows = [
        jnp.dot(normed, qkv_full[j], preferred_element_type=F32).astype(BF16) for j in range(3)
    ]
    starts = document_starts(segments)
    head_rows = attend_forward(starts, queries, key_rows, value_rows)
    head_all = gather_narrow(head_rows)
    hidden = rows_one + lax.dot_general(head_all, out_all, NT, preferred_element_type=F32)
    factor_two, second = norm_rows(hidden, gain_two)
    second = second.astype(BF16)
    second, moving = lax.optimization_barrier((second, moving))
    all_picks = jnp.concatenate(in_order(moving, "wide"), axis=0).astype(jnp.int32)

    gate_value = jnp.dot(second, gate_full, preferred_element_type=F32)
    gate_act = jax.nn.silu(gate_value)
    product_grad = jnp.dot(upstream, mixer_turned, preferred_element_type=F32)
    memory_grad = (product_grad * gate_act).astype(BF16)
    all_grads = gather_wide(memory_grad).reshape(shards * length, width)

    memory_query = jnp.dot(second, query_full, preferred_element_type=F32).astype(BF16)
    own_scores = pick_scores(column_ref, picks, memory_query, keys_full)
    mem_scores = sum_by_swaps(own_scores, "narrow").reshape(length, PKH, TOPK)
    score_peak = jnp.max(mem_scores, axis=-1, keepdims=True)
    raised = jnp.exp(mem_scores - score_peak)
    mem_probs = raised / jnp.sum(raised, axis=-1, keepdims=True)
    pick_weights = mem_probs.astype(BF16).reshape(length, PICKS)
    pick_weights, memory_grad = lax.optimization_barrier((pick_weights, memory_grad))
    all_weights = gather_wide(pick_weights).reshape(shards * length, PICKS)

    pick_part = picked_products(base, all_picks, all_grads, memory_values.T)
    all_weights, pick_part = lax.optimization_barrier((all_weights, pick_part))
    pick_own = sum_wide(pick_part.reshape(shards, length, PICKS)).astype(F32)
    tables = None
    memory_parts = []
    for number in range(PARTS):
        part_sums, tables = bag_sums(
            base, all_picks, all_weights, memory_values, tables, number, PARTS, shards
        )
        part_sums, pick_own = lax.optimization_barrier((part_sums, pick_own))
        memory_parts.append(sum_wide(part_sums.reshape(shards, length // PARTS, width)))
    values_grad = lax.dot_general(tables, all_grads, TN, preferred_element_type=F32)
    memory_parts, values_grad = lax.optimization_barrier((memory_parts, values_grad))
    memory = jnp.concatenate(memory_parts, axis=0).astype(F32)

    pick_grad = sum_by_swaps(pick_own, "narrow").reshape(length, PKH, TOPK)
    centre = jnp.sum(mem_probs * pick_grad, axis=-1, keepdims=True)
    score_grad = (mem_probs * (pick_grad - centre)).astype(BF16).reshape(length, PICKS)
    memory_query_grad, key_grad = spread_grads(
        column_ref, picks, score_grad, memory_query, keys_full
    )

    product = (gate_act * memory).astype(BF16)
    sigmoid = jax.nn.sigmoid(gate_value)
    gate_rows_grad = (
        product_grad * memory * sigmoid * (1.0 + gate_value * (1.0 - sigmoid))
    ).astype(BF16)
    second_part = lax.dot_general(gate_rows_grad, gate_full, NT, preferred_element_type=F32)
    second_part = second_part + lax.dot_general(
        memory_query_grad, query_full, NT, preferred_element_type=F32
    )
    turned = second_part * gain_two
    inner_part = jnp.sum(turned * hidden, axis=-1)
    gain_two_part = jnp.sum(second_part * hidden * factor_two, axis=0)
    tiny = sum_by_swaps(jnp.concatenate([inner_part, gain_two_part]), "narrow")
    inner_two = tiny[:length, None] / model
    gain_two_part = tiny[length:]
    own_second_grad = scatter_narrow(second_part)

    def own_columns(block):
        return lax.dynamic_slice_in_dim(block, column * width, width, block.ndim - 1)

    own_hidden = own_columns(hidden)
    own_hidden_grad = (
        cotangent.astype(F32)
        + factor_two * own_columns(gain_two) * own_second_grad
        - own_hidden * (factor_two * factor_two * factor_two) * inner_two
    )
    branch_grad = gather_narrow(own_hidden_grad.astype(BF16))

    mixer_part = lax.dot_general(product, mixer_turned, NT, preferred_element_type=F32)
    mixer_part, branch_grad = lax.optimization_barrier((mixer_part, branch_grad))
    outputs = (own_hidden + scatter_narrow(mixer_part)).astype(BF16)

    heads_grad = jnp.dot(branch_grad, out_turned, preferred_element_type=F32)
    heads_grad = heads_grad.astype(BF16)

    mixer_grad = lax.dot_general(upstream, product, TN, preferred_element_type=F32)
    query_grad = lax.dot_general(second, memory_query_grad, TN, preferred_element_type=F32)
    gate_grad = lax.dot_general(second, gate_rows_grad, TN, preferred_element_type=F32)
    key_grad = jnp.transpose(
        key_grad.astype(BF16).reshape(units, shards, key_part, NKEYS), (1, 0, 2, 3)
    ).reshape(shards, units * key_part, NKEYS)

    def by_shard(block):
        return block.astype(BF16).reshape(shards, part, block.shape[1])

    mixed_grad = attend_backward(starts, queries, key_rows, value_rows, heads_grad)
    normed_part = sum(
        lax.dot_general(mixed_grad[j], qkv_full[j], NT, preferred_element_type=F32)
        for j in range(3)
    )
    out_grad = lax.dot_general(branch_grad, head_rows, TN, preferred_element_type=F32)
    qkv_grad = [
        lax.dot_general(normed, mixed_grad[j], TN, preferred_element_type=F32) for j in range(3)
    ]
    inner_part = jnp.sum(normed_part * gain_one * rows_one, axis=-1)
    gain_one_part = jnp.sum(normed_part * rows_one * factor_one, axis=0)
    tiny = sum_by_swaps(jnp.concatenate([inner_part, gain_one_part]), "narrow")
    inner_one = tiny[:length, None] / model
    gain_one_part = tiny[length:]
    own_normed_grad = scatter_narrow(normed_part)
    input_grad = (
        own_hidden_grad
        + factor_one * own_columns(gain_one) * own_normed_grad
        - inputs.astype(F32) * (factor_one * factor_one * factor_one) * inner_one
    )
    gain_parts = jnp.concatenate(
        [gain_one_part.reshape(shards, 1, part), gain_two_part.reshape(shards, 1, part)], axis=1
    ).astype(BF16).reshape(shards, -1, LANES)
    all_grads_pack = pack(
        [by_shard(block) for block in qkv_grad + [out_grad, mixer_grad, gate_grad, query_grad]]
        + [key_grad, gain_parts]
    )
    sums = sum_wide(all_grads_pack).astype(F32)
    sum_shapes = [(part, width)] * 4 + second_shapes + [(2 * part // LANES, LANES)]
    (
        query_sum, key_sum, value_sum, out_sum, mixer_sums, gate_sums, query_sums, key_sums,
        gain_sums,
    ) = unpack(sums, sum_shapes)
    gain_sums = gain_sums.reshape(2, part)
    return (
        outputs,
        input_grad,
        gain_sums[0],
        jnp.stack([query_sum, key_sum, value_sum], axis=1),
        out_sum.T,
        gain_sums[1],
        query_sums.reshape(part, units, NKEYS),
        key_sums.reshape(units, key_part, NKEYS),
        gate_sums,
        values_grad,
        mixer_sums.T,
    )


def solution(mesh):
    return jax.shard_map(
        per_device,
        mesh=mesh,
        in_specs=(
            P("wide", "narrow"),
            P("wide", None),
            P("wide"),
            P("wide", None, "narrow"),
            P("narrow", "wide"),
            P("wide"),
            P("wide", "narrow", None),
            P("narrow", "wide", None),
            P("wide", "narrow"),
            P("wide", "narrow"),
            P("narrow", "wide"),
            P("wide", None),
            P("wide", "narrow"),
        ),
        out_specs=(
            P("wide", "narrow"),
            P("wide", "narrow"),
            P("wide"),
            P("wide", None, "narrow"),
            P("narrow", "wide"),
            P("wide"),
            P("wide", "narrow", None),
            P("narrow", "wide", None),
            P("wide", "narrow"),
            P("wide", "narrow"),
            P("narrow", "wide"),
        ),
        check_vma=False,
    )
```

```python
import functools

import jax
import jax.numpy as jnp
from jax import lax
from jax.experimental import pallas as pl
from jax.experimental.pallas import tpu as pltpu
from jax.sharding import PartitionSpec as P

HD = 64
PKH = 4
NKEYS = 256
TOPK = 32
PICKS = 128
DOCS = 3
DOC_MOST = 512
LANES = 128
GAIN_ROWS = 16
COVER = 1


EPSILON = 1e-06
MASKED = -1e30
BF16 = jnp.bfloat16
F32 = jnp.float32
NT = (((1,), (1,)), ((), ()))
TN = (((0,), (0,)), ((), ()))


def norm_rows(activations, gain_row):
    factor = lax.rsqrt(jnp.mean(activations * activations, axis=-1, keepdims=True) + EPSILON)
    return (factor, activations * factor * gain_row)


def document_starts(segment_row):
    starts = jnp.zeros(segment_row.shape, jnp.int32)
    for number in range(1, DOCS):
        before = jnp.sum((segment_row == number - 1).astype(jnp.int32))
        starts = starts + jnp.where(segment_row >= number, before, 0)
    return starts


def key_window(block, rows):
    first = max(0, (block * rows - (DOC_MOST - 1)) // rows * rows)
    return first, (block + 1) * rows


def head_lanes(shape, head, axis):
    return lax.broadcasted_iota(jnp.int32, shape, axis) // HD == head


def turned_probs(keys, queries, starts, first, offset):
    scores = lax.dot_general(keys, queries, NT, preferred_element_type=F32) * HD ** (-0.5)
    key_ids = lax.broadcasted_iota(jnp.int32, scores.shape, 0) + first
    query_ids = lax.broadcasted_iota(jnp.int32, scores.shape, 1) + offset
    allowed = (key_ids >= starts) & (key_ids <= query_ids)
    scores = jnp.where(allowed, scores, MASKED)
    raised = jnp.exp(scores - jnp.max(scores, axis=0, keepdims=True))
    return raised * (1.0 / jnp.sum(raised, axis=0, keepdims=True))


def attend_body(start_ref, query_ref, key_ref, value_ref, out_ref, *, rows):
    length = query_ref.shape[0]
    values_turned = value_ref[...].T
    for block in range(length // rows):
        first, last = key_window(block, rows)
        span = slice(block * rows, last)
        queries = query_ref[span, :]
        mixture = jnp.zeros((LANES, rows), F32)
        for head in range(LANES // HD):
            own = jnp.where(head_lanes(queries.shape, head, 1), queries, jnp.zeros((), BF16))
            probs = turned_probs(
                key_ref[first:last, :], own, start_ref[:, span], first, block * rows
            )
            part = jnp.dot(
                values_turned[:, first:last], probs.astype(BF16), preferred_element_type=F32
            )
            mixture = jnp.where(head_lanes(part.shape, head, 0), part, mixture)
        out_ref[span, :] = mixture.T.astype(BF16)


def attend_forward(starts, queries, key_rows, value_rows, rows=256):
    length, width = queries.shape
    column = pl.BlockSpec((length, LANES), lambda i: (0, i))
    return pl.pallas_call(
        functools.partial(attend_body, rows=rows),
        grid=(width // LANES,),
        in_specs=[pl.BlockSpec((1, length), lambda i: (0, 0)), column, column, column],
        out_specs=column,
        out_shape=jax.ShapeDtypeStruct((length, width), BF16),
        compiler_params=params(32),
        cost_estimate=pl.CostEstimate(
            flops=16 * length * length * width, bytes_accessed=8 * length * width, transcendentals=0
        ),
        name="attend_forward",
    )(starts, queries, key_rows, value_rows)


def attend_back_body(
    start_ref, query_ref, key_ref, value_ref, grad_ref, dq_ref, dk_ref, dv_ref, key_sum, value_sum,
    *, rows
):
    length = query_ref.shape[0]
    keys_turned = key_ref[...].T
    key_sum[...] = jnp.zeros_like(key_sum)
    value_sum[...] = jnp.zeros_like(value_sum)
    zero = jnp.zeros((), BF16)
    factor = HD ** (-0.5)
    for block in range(length // rows):
        first, last = key_window(block, rows)
        span = slice(block * rows, last)
        window = slice(first, last)
        queries = query_ref[span, :]
        grads = grad_ref[span, :]
        query_sum = jnp.zeros((LANES, rows), F32)
        for head in range(LANES // HD):
            mask = head_lanes(queries.shape, head, 1)
            own = jnp.where(mask, queries, zero)
            own_grads = jnp.where(mask, grads, zero)
            probs = turned_probs(key_ref[window, :], own, start_ref[:, span], first, block * rows)
            prob_grad = lax.dot_general(
                value_ref[window, :], own_grads, NT, preferred_element_type=F32
            )
            centre = jnp.sum(probs * prob_grad, axis=0, keepdims=True)
            score_grad = (probs * (prob_grad - centre)).astype(BF16)
            part = jnp.dot(keys_turned[:, window], score_grad, preferred_element_type=F32)
            query_sum = jnp.where(head_lanes(part.shape, head, 0), part, query_sum)
            key_sum[window, :] += jnp.dot(score_grad, own, preferred_element_type=F32)
            value_sum[window, :] += jnp.dot(
                probs.astype(BF16), own_grads, preferred_element_type=F32
            )
        dq_ref[span, :] = (query_sum.T * factor).astype(BF16)
    dk_ref[...] = (key_sum[...] * factor).astype(BF16)
    dv_ref[...] = value_sum[...].astype(BF16)


def attend_backward(starts, queries, key_rows, value_rows, heads_grad, rows=256):
    length, width = queries.shape
    column = pl.BlockSpec((length, LANES), lambda i: (0, i))
    return pl.pallas_call(
        functools.partial(attend_back_body, rows=rows),
        grid=(width // LANES,),
        in_specs=[pl.BlockSpec((1, length), lambda i: (0, 0))] + [column] * 4,
        out_specs=[column] * 3,
        out_shape=[jax.ShapeDtypeStruct((length, width), BF16)] * 3,
        scratch_shapes=[pltpu.VMEM((length, LANES), F32)] * 2,
        compiler_params=params(40),
        cost_estimate=pl.CostEstimate(
            flops=COVER * length * length * width,
            bytes_accessed=14 * length * width,
            transcendentals=0,
        ),
        name="attend_backward",
    )(starts, queries, key_rows, value_rows, heads_grad)


SLOTS = 32


def params(mib):
    return pltpu.CompilerParams(vmem_limit_bytes=mib << 20)


def lane_numbers(shape):
    return lax.broadcasted_iota(jnp.int32, shape, len(shape) - 1)


def count_local(local, total):
    inside = (local >= 0) & (local < total)
    square = (LANES, LANES)
    upto = lax.broadcasted_iota(jnp.int32, square, 0) <= lax.broadcasted_iota(jnp.int32, square, 1)
    return jnp.dot(
        jnp.where(inside, 1.0, 0.0).astype(BF16),
        jnp.where(upto, 1.0, 0.0).astype(BF16),
        preferred_element_type=F32,
    )


def rounds_of(counts):
    most = jnp.max(counts[:, LANES - 1 :]).astype(jnp.int32)
    return (most + (SLOTS - 1)) // SLOTS


def search(counts, start):
    target = ((lane_numbers(counts.shape) & (SLOTS - 1)) + (start + 1)).astype(F32)
    place = jnp.zeros(counts.shape, jnp.int32)
    step = LANES // 2
    while step:
        seen = jnp.take_along_axis(counts, place + (step - 1), axis=1)
        place = jnp.where(seen < target, place + step, place)
        step //= 2
    return target <= counts[:, LANES - 1 :], place


def place_of(counts, local, number):
    valid, place = search(counts, number * SLOTS)
    return place, jnp.where(valid, jnp.take_along_axis(local, place, axis=1), -1)


def locate_body(base_ref, picks_ref, count_ref, place_ref, found_ref, *, total):
    local = picks_ref[...] - base_ref[0]
    counts = count_local(local, total)
    valid, place = search(counts, 0)
    count_ref[...] = counts
    place_ref[...] = place
    found_ref[...] = jnp.where(valid, jnp.take_along_axis(local, place, axis=1), -1)


def locate(base, picks, total, rows=512):
    block = pl.BlockSpec((rows, PICKS), lambda i: (i, 0))
    amount = picks.shape[0]
    return pl.pallas_call(
        functools.partial(locate_body, total=total),
        grid=(amount // rows,),
        in_specs=[pl.BlockSpec(memory_space=pltpu.SMEM), block],
        out_specs=[block] * 3,
        out_shape=[
            jax.ShapeDtypeStruct((amount, PICKS), F32),
            jax.ShapeDtypeStruct((amount, PICKS), jnp.int32),
            jax.ShapeDtypeStruct((amount, PICKS), jnp.int32),
        ],
        compiler_params=params(32),
        cost_estimate=pl.CostEstimate(
            flops=amount * PICKS * 20000, bytes_accessed=amount * PICKS * 16, transcendentals=0
        ),
        name="locate",
    )(base, picks)


def group_masks():
    own = lax.broadcasted_iota(jnp.int32, (8, LANES), 0)
    lane = lane_numbers((8, LANES)) // SLOTS
    per = LANES // SLOTS
    return [own == lane + per * block for block in range(8 // per)]


def lane_table(low, masks):
    ids = lax.broadcasted_iota(jnp.int32, (NKEYS, LANES), 0).astype(F32).astype(BF16)
    parts = []
    for mask in masks:
        row = jnp.sum(jnp.where(mask, low, 0.0), axis=0, keepdims=True)
        row = jnp.broadcast_to(row, (16, LANES)).astype(BF16)
        row = jnp.concatenate([row] * (NKEYS // 16), axis=0)
        parts.append(jnp.where(ids == row, jnp.ones((), BF16), jnp.zeros((), BF16)))
    return jnp.concatenate(parts, axis=1)


def bag_body(
    base_ref, picks_ref, count_ref, place_ref, found_ref, weight_ref, table_ref, out_ref, keep_ref,
    high, low, weights, *, chunk, unroll
):
    rows = picks_ref.shape[0]
    total = table_ref.shape[0]
    groups = total // NKEYS
    masks = group_masks()

    def eight(token):
        span = pl.ds(token, 8)
        own_high = high[span, :]
        weight = weights[span, :]
        weight = jnp.concatenate([weight, weight], axis=0).astype(BF16)
        zero = jnp.zeros((), BF16)
        parts = []
        for mask in masks:
            own = jnp.where(mask, own_high, -1.0)
            pair = jnp.concatenate([own, own - 1.0], axis=0).astype(BF16)
            rows_of = [
                jnp.where(pair == jnp.array(group, BF16), weight, zero)
                for group in range(0, groups, 2)
            ]
            parts.append(jnp.concatenate(rows_of, axis=0))
        return lax.dot_general(
            jnp.concatenate(parts, axis=1),
            lane_table(low[span, :], masks),
            NT,
            preferred_element_type=F32,
        )

    def one_round(place, found, first):
        high[...] = (found >> 8).astype(F32)
        low[...] = (found & (NKEYS - 1)).astype(F32)
        weights[...] = jnp.take_along_axis(weight_ref[...].astype(F32), place, axis=1)

        def some_tokens(step, carried):
            for slot in range(unroll):
                token = pl.multiple_of((step * unroll + slot) * 16, 16)
                top = eight(token)
                bottom = eight(token + 8)
                for group in range(groups):
                    part = slice(group * 8, group * 8 + 8)
                    block = jnp.concatenate([top[part], bottom[part]], axis=0).astype(BF16)
                    span = (pl.ds(token, 16), slice(group * NKEYS, (group + 1) * NKEYS))
                    keep_ref[span] = block if first else keep_ref[span] + block
            return carried

        lax.fori_loop(0, rows // (16 * unroll), some_tokens, 0)

    def more(number, carried):
        local = picks_ref[...] - base_ref[0]
        one_round(*place_of(count_ref[...], local, number), False)
        return carried

    one_round(place_ref[...], found_ref[...], True)
    lax.fori_loop(1, rounds_of(count_ref[...]), more, 0)
    result = jnp.zeros(out_ref.shape, F32)
    for start in range(0, total, chunk):
        result = result + jnp.dot(
            keep_ref[:, pl.ds(start, chunk)],
            table_ref[pl.ds(start, chunk), :],
            preferred_element_type=F32,
        )
    out_ref[...] = result.astype(out_ref.dtype)


def bag_sums(base, picks, located, weights, table, rows=256, chunk=1024, unroll=16):
    amount = picks.shape[0]
    total, width = table.shape
    block = pl.BlockSpec((rows, PICKS), lambda i: (i, 0))
    return pl.pallas_call(
        functools.partial(bag_body, chunk=chunk, unroll=unroll),
        grid=(amount // rows,),
        in_specs=[pl.BlockSpec(memory_space=pltpu.SMEM)]
        + [block] * 5
        + [pl.BlockSpec((total, width), lambda i: (0, 0))],
        out_specs=[
            pl.BlockSpec((rows, width), lambda i: (i, 0)),
            pl.BlockSpec((rows, total), lambda i: (i, 0)),
        ],
        out_shape=[
            jax.ShapeDtypeStruct((amount, width), BF16),
            jax.ShapeDtypeStruct((amount, total), BF16),
        ],
        scratch_shapes=[pltpu.VMEM((rows, LANES), F32)] * 3,
        compiler_params=params(56),
        cost_estimate=pl.CostEstimate(
            flops=9 * amount * total * width, bytes_accessed=amount * total * 2, transcendentals=0
        ),
        name="bag_sums",
    )(base, picks, *located, weights, table)


def picked_body(
    base_ref, picks_ref, count_ref, found_ref, grad_ref, table_ref, out_ref, high, low, found_at,
    held, *, unroll
):
    rows = picks_ref.shape[0]
    total = table_ref.shape[1]
    groups = total // NKEYS
    masks = group_masks()
    grads = grad_ref[...]
    for group in range(groups):
        held[group] = jnp.dot(
            grads,
            table_ref[:, group * NKEYS : (group + 1) * NKEYS],
            preferred_element_type=F32,
        )

    def eight(token):
        span = pl.ds(token, 8)
        left = jnp.concatenate([held[group, span, :] for group in range(groups)], axis=0)
        seen = jnp.dot(
            left.astype(BF16), lane_table(low[span, :], masks), preferred_element_type=F32
        )
        own_high = high[span, :]
        result = jnp.zeros((8, LANES), F32)
        for block, mask in enumerate(masks):
            own = jnp.where(mask, own_high, -1.0)
            for group in range(groups):
                part = seen[group * 8 : group * 8 + 8, block * LANES : (block + 1) * LANES]
                result = jnp.where(own == float(group), part, result)
        found_at[span, :] = result

    def one_round(number, found, first):
        high[...] = (found >> 8).astype(F32)
        low[...] = (found & (NKEYS - 1)).astype(F32)

        def some_tokens(step, carried):
            for slot in range(unroll):
                eight(pl.multiple_of((step * unroll + slot) * 8, 8))
            return carried

        lax.fori_loop(0, rows // (8 * unroll), some_tokens, 0)
        slot = count_ref[...].astype(jnp.int32) - (1 + number * SLOTS)
        local = picks_ref[...] - base_ref[0]
        inside = (local >= 0) & (local < total)
        here = (slot >= 0) & (slot < SLOTS) & inside
        token = lax.broadcasted_iota(jnp.int32, slot.shape, 0) & (LANES // SLOTS - 1)
        lane = token * SLOTS + jnp.clip(slot, 0, SLOTS - 1)
        value = jnp.take_along_axis(found_at[...], lane, axis=1)
        before = jnp.zeros(value.shape, F32) if first else out_ref[...].astype(F32)
        out_ref[...] = jnp.where(here, value, before).astype(out_ref.dtype)

    def more(number, carried):
        local = picks_ref[...] - base_ref[0]
        one_round(number, place_of(count_ref[...], local, number)[1], False)
        return carried

    one_round(0, found_ref[...], True)
    lax.fori_loop(1, rounds_of(count_ref[...]), more, 0)


def picked_products(base, picks, located, grads, table, rows=256, unroll=32):
    amount, width = grads.shape
    total = table.shape[1]
    return pl.pallas_call(
        functools.partial(picked_body, unroll=unroll),
        grid=(amount // rows,),
        in_specs=[
            pl.BlockSpec(memory_space=pltpu.SMEM),
            pl.BlockSpec((rows, PICKS), lambda i: (i, 0)),
            pl.BlockSpec((rows, PICKS), lambda i: (i, 0)),
            pl.BlockSpec((rows, PICKS), lambda i: (i, 0)),
            pl.BlockSpec((rows, width), lambda i: (i, 0)),
            pl.BlockSpec((width, total), lambda i: (0, 0)),
        ],
        out_specs=pl.BlockSpec((rows, PICKS), lambda i: (i, 0)),
        out_shape=jax.ShapeDtypeStruct((amount, PICKS), BF16),
        scratch_shapes=[
            pltpu.VMEM((rows, LANES), F32),
            pltpu.VMEM((rows, LANES), F32),
            pltpu.VMEM((rows, LANES), F32),
            pltpu.VMEM((total // NKEYS, rows, NKEYS), F32),
        ],
        compiler_params=params(56),
        cost_estimate=pl.CostEstimate(
            flops=7 * amount * total * width, bytes_accessed=amount * width * 4, transcendentals=0
        ),
        name="picked_products",
    )(base, picks, located[0], located[2], grads, table)


def gather_lanes(block, index):
    return jnp.take_along_axis(block, index, axis=1)


def over_head(block, merge):
    lanes = lane_numbers(block.shape)
    step = 1
    while step < TOPK:
        block = merge(block, gather_lanes(block, lanes ^ step))
        step *= 2
    return block


def softmax_body(score_ref, prob_ref, weight_ref):
    scores = score_ref[...]
    raised = jnp.exp(scores - over_head(scores, jnp.maximum))
    probs = raised / over_head(raised, jnp.add)
    prob_ref[...] = probs
    weight_ref[...] = probs.astype(BF16)


def pick_softmax(scores, rows=256):
    block = pl.BlockSpec((rows, PICKS), lambda i: (i, 0))
    amount = scores.shape[0]
    return pl.pallas_call(
        softmax_body,
        grid=(amount // rows,),
        in_specs=[block],
        out_specs=[block] * 2,
        out_shape=[
            jax.ShapeDtypeStruct((amount, PICKS), F32),
            jax.ShapeDtypeStruct((amount, PICKS), BF16),
        ],
        compiler_params=params(32),
        name="pick_softmax",
    )(scores)


def store_lanes(out_ref, lead, row, block):
    rows, columns = block.shape
    for start in range(0, columns, LANES):
        out_ref[(*lead, slice(row, row + rows), slice(None))] = block[:, start : start + LANES]
        row += rows
    return row


def load_lanes(ref, lead, row, rows, columns):
    parts = []
    for _ in range(columns // LANES):
        parts.append(ref[(*lead, slice(row, row + rows), slice(None))])
        row += rows
    return jnp.concatenate(parts, axis=1), row


def pack_body(qkv_ref, out_ref, mixer_ref, gate_ref, query_ref, keys_ref, gain_ref, packed_ref):
    row = 0
    for j in range(3):
        row = store_lanes(packed_ref, (), row, qkv_ref[j])
    row = store_lanes(packed_ref, (), row, out_ref[...].T)
    row = store_lanes(packed_ref, (), row, mixer_ref[...].T)
    row = store_lanes(packed_ref, (), row, gate_ref[...])
    for unit in range(query_ref.shape[0]):
        row = store_lanes(packed_ref, (), row, query_ref[unit])
    for unit in range(keys_ref.shape[0]):
        row = store_lanes(packed_ref, (), row, keys_ref[unit])
    store_lanes(packed_ref, (), row, gain_ref[...])


def pack_weights(blocks):
    amount = sum(block.size for block in blocks) // LANES
    return pl.pallas_call(
        pack_body,
        out_shape=jax.ShapeDtypeStruct((amount, LANES), BF16),
        compiler_params=params(32),
        name="pack_weights",
    )(*blocks)


def unpack_body(
    packed_ref, q_ref, k_ref, v_ref, out_ref, mixer_ref, gate_ref, query_ref, keys_ref, gain_ref
):
    row = 0
    for target in (q_ref, k_ref, v_ref, out_ref, mixer_ref, gate_ref):
        target[...], row = load_lanes(packed_ref, (0,), row, *target.shape)
    for unit in range(query_ref.shape[1] // NKEYS):
        span = slice(unit * NKEYS, (unit + 1) * NKEYS)
        query_ref[:, span], row = load_lanes(packed_ref, (0,), row, query_ref.shape[0], NKEYS)
    for unit in range(keys_ref.shape[0]):
        keys_ref[unit], row = load_lanes(packed_ref, (0,), row, keys_ref.shape[1], NKEYS)
    gain_ref[0] = packed_ref[0, row : row + gain_ref.shape[1], :]


def unpack_weights(packed, part, width, units, key_part):
    shards, amount, _ = packed.shape
    model = shards * part

    def rows_of(columns):
        return pl.BlockSpec((part, columns), lambda i: (i, 0))

    return pl.pallas_call(
        unpack_body,
        grid=(shards,),
        in_specs=[pl.BlockSpec((1, amount, LANES), lambda i: (i, 0, 0))],
        out_specs=[rows_of(width)] * 6
        + [
            rows_of(units * NKEYS),
            pl.BlockSpec((units, key_part, NKEYS), lambda i: (0, i, 0)),
            pl.BlockSpec((1, GAIN_ROWS, LANES), lambda i: (i, 0, 0)),
        ],
        out_shape=[jax.ShapeDtypeStruct((model, width), BF16)] * 6
        + [
            jax.ShapeDtypeStruct((model, units * NKEYS), BF16),
            jax.ShapeDtypeStruct((units, shards * key_part, NKEYS), BF16),
            jax.ShapeDtypeStruct((shards, GAIN_ROWS, LANES), BF16),
        ],
        compiler_params=params(32),
        name="unpack_weights",
    )(packed)


def grads_body(*refs, pairs, part, units):
    lefts, rights, rest = refs[:pairs], refs[pairs : 2 * pairs], refs[2 * pairs :]
    packed_ref = rest[-1]
    per = LANES // part
    rows = [0] * per
    for left, right in zip(lefts, rights):
        grad = lax.dot_general(left[...], right[...], TN, preferred_element_type=F32).astype(BF16)
        for number in range(per):
            own = grad[number * part : (number + 1) * part]
            rows[number] = store_lanes(packed_ref, (number,), rows[number], own)
    if units:
        key_ref = rest[0]
        key_part = key_ref.shape[1] // per
        for number in range(per):
            for unit in range(units):
                own = key_ref[unit, number * key_part : (number + 1) * key_part, :].astype(BF16)
                rows[number] = store_lanes(packed_ref, (number,), rows[number], own)


def pack_grads(lefts, rights, part, key_grad=None):
    length, model = lefts[0].shape
    shards = model // part
    per = LANES // part
    amount = part * sum(right.shape[1] for right in rights) // LANES
    units = 0
    extra, extra_specs = [], []
    if key_grad is not None:
        units, keys, _ = key_grad.shape
        amount += key_grad.size // shards // LANES
        extra = [key_grad]
        extra_specs = [pl.BlockSpec((units, keys // shards * per, NKEYS), lambda i: (0, i, 0))]
    return pl.pallas_call(
        functools.partial(grads_body, pairs=len(lefts), part=part, units=units),
        grid=(shards // per,),
        in_specs=[pl.BlockSpec((length, LANES), lambda i: (0, i))] * len(lefts)
        + [pl.BlockSpec(right.shape, lambda i: (0, 0)) for right in rights]
        + extra_specs,
        out_specs=pl.BlockSpec((per, amount, LANES), lambda i: (i, 0, 0)),
        out_shape=jax.ShapeDtypeStruct((shards, amount, LANES), BF16),
        compiler_params=params(48),
        name="pack_grads",
    )(*lefts, *rights, *extra)


def unpack_grads_body(
    early_ref, late_ref, qkv_ref, out_ref, mixer_ref, gate_ref, query_ref, keys_ref
):
    part, width = gate_ref.shape
    row = 0
    for j in range(3):
        block, row = load_lanes(late_ref, (), row, part, width)
        qkv_ref[j] = block.astype(F32)
    block, row = load_lanes(late_ref, (), row, part, width)
    out_ref[...] = block.astype(F32).T
    row = 0
    block, row = load_lanes(early_ref, (), row, part, width)
    mixer_ref[...] = block.astype(F32).T
    block, row = load_lanes(early_ref, (), row, part, width)
    gate_ref[...] = block.astype(F32)
    for unit in range(query_ref.shape[0]):
        block, row = load_lanes(early_ref, (), row, part, NKEYS)
        query_ref[unit] = block.astype(F32)
    for unit in range(keys_ref.shape[0]):
        block, row = load_lanes(early_ref, (), row, keys_ref.shape[1], NKEYS)
        keys_ref[unit] = block.astype(F32)


def unpack_grads(early, late, part, width, units, key_part):
    shapes = [
        (3, part, width),
        (width, part),
        (width, part),
        (part, width),
        (units, part, NKEYS),
        (units, key_part, NKEYS),
    ]
    return pl.pallas_call(
        unpack_grads_body,
        out_shape=[jax.ShapeDtypeStruct(shape, F32) for shape in shapes],
        compiler_params=params(32),
        name="unpack_grads",
    )(early, late)


def unit_indices(picks, number):
    return jnp.where(number % 2 == 0, picks >> 8, picks & (NKEYS - 1))


def scores_body(column_ref, picks_ref, query_ref, keys_ref, out_ref, *, units):
    picks = picks_ref[...]
    lanes = lax.broadcasted_iota(jnp.int32, picks.shape, 1)
    total = jnp.zeros(picks.shape, F32)
    for unit in range(units):
        number = column_ref[0] * units + unit
        index = unit_indices(picks, number)
        scores = lax.dot_general(
            query_ref[:, unit * NKEYS : (unit + 1) * NKEYS],
            keys_ref[unit],
            NT,
            preferred_element_type=F32,
        )
        lower = index & (LANES - 1)
        low_part = jnp.take_along_axis(scores[:, :LANES], lower, axis=1)
        high_part = jnp.take_along_axis(scores[:, LANES:], lower, axis=1)
        found = jnp.where(index < LANES, low_part, high_part)
        total = total + jnp.where(lanes // TOPK == number // 2, found, 0.0)
    out_ref[...] = total


def pick_scores(column, picks, queries, keys, rows=256):
    amount = picks.shape[0]
    units = keys.shape[0]
    return pl.pallas_call(
        functools.partial(scores_body, units=units),
        grid=(amount // rows,),
        in_specs=[
            pl.BlockSpec(memory_space=pltpu.SMEM),
            pl.BlockSpec((rows, PICKS), lambda i: (i, 0)),
            pl.BlockSpec((rows, units * NKEYS), lambda i: (i, 0)),
            pl.BlockSpec(keys.shape, lambda i: (0, 0, 0)),
        ],
        out_specs=pl.BlockSpec((rows, PICKS), lambda i: (i, 0)),
        out_shape=jax.ShapeDtypeStruct((amount, PICKS), F32),
        compiler_params=params(32),
        name="pick_scores",
    )(column, picks, queries, keys)


def spread_body(
    column_ref, picks_ref, prob_ref, grad_ref, query_ref, keys_ref, out_ref, sum_ref, held_index,
    held_grad, *, units
):
    rows = picks_ref.shape[0]
    probs = prob_ref[...]
    pick_grad = grad_ref[...]
    centre = over_head(probs * pick_grad, jnp.add)
    held_grad[...] = (probs * (pick_grad - centre)).astype(BF16).astype(F32).T

    @pl.when(pl.program_id(0) == 0)
    def clear():
        sum_ref[...] = jnp.zeros_like(sum_ref)

    key_ids = lax.broadcasted_iota(jnp.int32, (NKEYS, rows), 0)
    for unit in range(units):
        number = column_ref[0] * units + unit
        first = (number // 2) * TOPK
        held_index[...] = unit_indices(picks_ref[...], number).T
        table = jnp.zeros((NKEYS, rows), F32)
        for slot in range(TOPK):
            index = held_index[pl.ds(first + slot, 1), :]
            grad = held_grad[pl.ds(first + slot, 1), :]
            table = table + jnp.where(key_ids == index, grad, 0.0)
        table = table.astype(BF16)
        span = slice(unit * NKEYS, (unit + 1) * NKEYS)
        out_ref[:, span] = lax.dot_general(
            table, keys_ref[unit], TN, preferred_element_type=F32
        ).astype(BF16)
        sum_ref[unit] += jnp.dot(table, query_ref[:, span], preferred_element_type=F32)


def spread_grads(column, picks, probs, grads, queries, keys, rows=128):
    amount = picks.shape[0]
    units = keys.shape[0]
    return pl.pallas_call(
        functools.partial(spread_body, units=units),
        grid=(amount // rows,),
        in_specs=[
            pl.BlockSpec(memory_space=pltpu.SMEM),
            pl.BlockSpec((rows, PICKS), lambda i: (i, 0)),
            pl.BlockSpec((rows, PICKS), lambda i: (i, 0)),
            pl.BlockSpec((rows, PICKS), lambda i: (i, 0)),
            pl.BlockSpec((rows, units * NKEYS), lambda i: (i, 0)),
            pl.BlockSpec(keys.shape, lambda i: (0, 0, 0)),
        ],
        out_specs=[
            pl.BlockSpec((rows, units * NKEYS), lambda i: (i, 0)),
            pl.BlockSpec(keys.shape, lambda i: (0, 0, 0)),
        ],
        out_shape=[
            jax.ShapeDtypeStruct((amount, units * NKEYS), BF16),
            jax.ShapeDtypeStruct(keys.shape, F32),
        ],
        scratch_shapes=[pltpu.VMEM((PICKS, rows), jnp.int32), pltpu.VMEM((PICKS, rows), F32)],
        compiler_params=params(32),
        name="spread_grads",
    )(column, picks, probs, grads, queries, keys)


def swap_narrow(block, bit):
    size = lax.axis_size("narrow")
    return lax.ppermute(block, "narrow", [(i, i ^ bit) for i in range(size)])


def swap_all(held, axis, bit):
    pairs = [(i, i ^ bit) for i in range(lax.axis_size(axis))]
    moved = {offset ^ bit: lax.ppermute(part, axis, pairs) for offset, part in held.items()}
    return {**held, **moved}


def in_order(held, axis):
    me = lax.axis_index(axis)
    size = lax.axis_size(axis)
    stacked = jnp.stack([held[offset] for offset in range(size)])
    return [lax.dynamic_index_in_dim(stacked, me ^ number, 0, False) for number in range(size)]


def gather_by_swaps(block, axis, bits):
    held = {0: block}
    for bit in bits:
        held = swap_all(held, axis, bit)
    return in_order(held, axis)


def sum_by_swaps(block, axis):
    for bit in bits_down(lax.axis_size(axis)):
        block = block + lax.ppermute(
            block, axis, [(i, i ^ bit) for i in range(lax.axis_size(axis))]
        )
    return block


def scatter_narrow(block):
    size = lax.axis_size("narrow")
    me = lax.axis_index("narrow")
    width = block.shape[1] // size
    parts = jnp.stack([block[:, n * width : (n + 1) * width] for n in range(size)])
    held = [lax.dynamic_index_in_dim(parts, me ^ offset, 0, False) for offset in range(size)]
    for bit in bits_down(size)[::-1]:
        arrived = {
            offset: swap_narrow(held[offset ^ bit].astype(BF16), bit)
            for offset in range(size)
            if not offset & (2 * bit - 1)
        }
        held = {
            offset: held[offset].astype(F32) + value.astype(F32)
            for offset, value in arrived.items()
        }
    return held[0]


def bits_down(size):
    return [1 << level for level in reversed(range(size.bit_length() - 1))]


def gather_narrow(block):
    return jnp.concatenate(
        gather_by_swaps(block, "narrow", bits_down(lax.axis_size("narrow"))), axis=1
    )


def gather_wide(block):
    return lax.all_gather(block, "wide")


def sum_wide(block):
    return lax.psum_scatter(block, "wide", scatter_dimension=0)


def per_device(
    inputs,
    segments,
    attn_gain,
    qkv_weight,
    out_weight,
    memory_gain,
    query_weight,
    sub_keys,
    gate_weight,
    memory_values,
    memory_out,
    picks,
    cotangent,
):
    length, width = inputs.shape
    shards = lax.axis_size("wide")
    column = lax.axis_index("narrow")
    column_ref = column.astype(jnp.int32).reshape(1)
    shard_rows = memory_values.shape[0]
    base = (lax.axis_index("wide") * shard_rows).astype(jnp.int32).reshape(1)
    units = sub_keys.shape[0]
    part = qkv_weight.shape[0]
    model = part * shards
    key_part = sub_keys.shape[1]

    rows_one = gather_narrow(inputs).astype(F32)
    gains = jnp.concatenate([attn_gain, memory_gain]).reshape(-1, LANES)
    gains = jnp.pad(gains, ((0, GAIN_ROWS - gains.shape[0]), (0, 0)))
    packed = gather_wide(
        pack_weights(
            [
                jnp.transpose(qkv_weight, (1, 0, 2)),
                out_weight,
                memory_out,
                gate_weight,
                jnp.transpose(query_weight, (1, 0, 2)),
                sub_keys,
                gains,
            ]
        )
    )
    (
        query_matrix, key_matrix, value_matrix, out_turned, mixer_turned, gate_full, query_full,
        keys_full, gains,
    ) = unpack_weights(packed, part, width, units, key_part)
    qkv_full = [query_matrix, key_matrix, value_matrix]
    gains = gains.reshape(shards, -1)[:, : 2 * part].reshape(shards, 2, part).astype(F32)
    gain_one = gains[:, 0].reshape(model)
    gain_two = gains[:, 1].reshape(model)
    out_all = gather_narrow(out_turned)
    upstream = gather_narrow(cotangent)
    half = length // 2
    pairs = picks[:half] | (picks[half:] << 16)
    pairs, packed = lax.optimization_barrier((pairs, packed))
    pairs = gather_wide(pairs)
    all_picks = jnp.concatenate([pairs & 0xFFFF, (pairs >> 16) & 0xFFFF], axis=1)
    all_picks = all_picks.reshape(shards * length, PICKS)
    located = locate(base, all_picks, shard_rows)

    factor_one, normed = norm_rows(rows_one, gain_one)
    normed = normed.astype(BF16)
    queries, key_rows, value_rows = [
        jnp.dot(normed, qkv_full[j], preferred_element_type=F32).astype(BF16) for j in range(3)
    ]
    starts = document_starts(segments)
    head_rows = attend_forward(starts, queries, key_rows, value_rows)
    head_all = gather_narrow(head_rows)
    hidden = rows_one + lax.dot_general(head_all, out_all, NT, preferred_element_type=F32)
    factor_two, second = norm_rows(hidden, gain_two)
    second = second.astype(BF16)

    gate_value = jnp.dot(second, gate_full, preferred_element_type=F32)
    gate_act = jax.nn.silu(gate_value)
    product_grad = jnp.dot(upstream, mixer_turned, preferred_element_type=F32)
    memory_grad = (product_grad * gate_act).astype(BF16)
    all_grads = gather_wide(memory_grad).reshape(shards * length, width)

    memory_query = jnp.dot(second, query_full, preferred_element_type=F32).astype(BF16)
    own_scores = pick_scores(column_ref, picks, memory_query, keys_full)
    mem_probs, pick_weights = pick_softmax(sum_by_swaps(own_scores, "narrow"))
    pick_weights, memory_grad = lax.optimization_barrier((pick_weights, memory_grad))
    all_weights = gather_wide(pick_weights).reshape(shards * length, PICKS)

    pick_part = picked_products(base, all_picks, located, all_grads, memory_values.T)
    all_weights, pick_part = lax.optimization_barrier((all_weights, pick_part))
    pick_own = sum_wide(pick_part.reshape(shards, length, PICKS)).astype(F32)
    memory_part, tables = bag_sums(base, all_picks, located, all_weights, memory_values)
    memory_part, pick_own = lax.optimization_barrier((memory_part, pick_own))
    memory_own = sum_wide(memory_part.reshape(shards, length, width))
    values_grad = lax.dot_general(tables, all_grads, TN, preferred_element_type=F32)
    memory_own, values_grad = lax.optimization_barrier((memory_own, values_grad))
    memory = memory_own.astype(F32)

    pick_grad = sum_by_swaps(pick_own, "narrow")
    memory_query_grad, key_grad = spread_grads(
        column_ref, picks, mem_probs, pick_grad, memory_query, keys_full
    )

    product = (gate_act * memory).astype(BF16)
    sigmoid = jax.nn.sigmoid(gate_value)
    gate_rows_grad = (
        product_grad * memory * sigmoid * (1.0 + gate_value * (1.0 - sigmoid))
    ).astype(BF16)
    early_pack = pack_grads(
        [upstream, second, second],
        [product, gate_rows_grad, memory_query_grad],
        part,
        key_grad,
    )
    early_pack, gate_rows_grad = lax.optimization_barrier((early_pack, gate_rows_grad))
    early_sums = sum_wide(early_pack)
    second_part = lax.dot_general(gate_rows_grad, gate_full, NT, preferred_element_type=F32)
    second_part = second_part + lax.dot_general(
        memory_query_grad, query_full, NT, preferred_element_type=F32
    )
    turned = second_part * gain_two
    inner_part = jnp.sum(turned * hidden, axis=-1)
    gain_two_part = jnp.sum(second_part * hidden * factor_two, axis=0)
    tiny = sum_by_swaps(jnp.concatenate([inner_part, gain_two_part]), "narrow")
    inner_two = tiny[:length, None] / model
    gain_two_part = tiny[length:]
    own_second_grad = scatter_narrow(second_part)

    def own_columns(block):
        return lax.dynamic_slice_in_dim(block, column * width, width, block.ndim - 1)

    own_hidden = own_columns(hidden)
    own_hidden_grad = (
        cotangent.astype(F32)
        + factor_two * own_columns(gain_two) * own_second_grad
        - own_hidden * (factor_two * factor_two * factor_two) * inner_two
    )
    branch_grad = gather_narrow(own_hidden_grad.astype(BF16))

    mixer_part = lax.dot_general(product, mixer_turned, NT, preferred_element_type=F32)
    mixer_part, branch_grad = lax.optimization_barrier((mixer_part, branch_grad))
    outputs = (own_hidden + scatter_narrow(mixer_part)).astype(BF16)

    heads_grad = jnp.dot(branch_grad, out_turned, preferred_element_type=F32)
    heads_grad = heads_grad.astype(BF16)

    mixed_grad = attend_backward(starts, queries, key_rows, value_rows, heads_grad)
    normed_part = sum(
        lax.dot_general(mixed_grad[j], qkv_full[j], NT, preferred_element_type=F32)
        for j in range(3)
    )
    late_pack = pack_grads(
        [normed, normed, normed, branch_grad], [*mixed_grad, head_rows], part
    )
    late_pack, early_sums = lax.optimization_barrier((late_pack, early_sums))
    late_sums = sum_wide(late_pack)
    inner_part = jnp.sum(normed_part * gain_one * rows_one, axis=-1)
    gain_one_part = jnp.sum(normed_part * rows_one * factor_one, axis=0)
    tiny = sum_by_swaps(jnp.concatenate([inner_part, gain_one_part]), "narrow")
    inner_one = tiny[:length, None] / model
    gain_one_part = tiny[length:]
    own_normed_grad = scatter_narrow(normed_part)
    input_grad = (
        own_hidden_grad
        + factor_one * own_columns(gain_one) * own_normed_grad
        - inputs.astype(F32) * (factor_one * factor_one * factor_one) * inner_one
    )
    gain_sums = sum_by_swaps(jnp.stack([gain_one_part, gain_two_part]), "wide")
    gain_sums = lax.dynamic_slice_in_dim(gain_sums, lax.axis_index("wide") * part, part, 1)
    qkv_sum, out_sum, mixer_sum, gate_sum, query_sum, key_sum = unpack_grads(
        early_sums, late_sums, part, width, units, key_part
    )
    return (
        outputs,
        input_grad,
        gain_sums[0],
        jnp.transpose(qkv_sum, (1, 0, 2)),
        out_sum,
        gain_sums[1],
        jnp.transpose(query_sum, (1, 0, 2)),
        key_sum,
        gate_sum,
        values_grad,
        mixer_sum,
    )


def solution(mesh):
    return jax.shard_map(
        per_device,
        mesh=mesh,
        in_specs=(
            P("wide", "narrow"),
            P("wide", None),
            P("wide"),
            P("wide", None, "narrow"),
            P("narrow", "wide"),
            P("wide"),
            P("wide", "narrow", None),
            P("narrow", "wide", None),
            P("wide", "narrow"),
            P("wide", "narrow"),
            P("narrow", "wide"),
            P("wide", None),
            P("wide", "narrow"),
        ),
        out_specs=(
            P("wide", "narrow"),
            P("wide", "narrow"),
            P("wide"),
            P("wide", None, "narrow"),
            P("narrow", "wide"),
            P("wide"),
            P("wide", "narrow", None),
            P("narrow", "wide", None),
            P("wide", "narrow"),
            P("wide", "narrow"),
            P("narrow", "wide"),
        ),
        check_vma=False,
    )
```

```python
import functools

import jax
import jax.numpy as jnp
from jax import lax
from jax.experimental import pallas as pl
from jax.experimental.pallas import tpu as pltpu
from jax.sharding import PartitionSpec as P

HD = 64
PKH = 4
NKEYS = 256
TOPK = 32
PICKS = 128
DOCS = 3
DOC_MOST = 512
LANES = 128
ROWS = 512
GAIN_ROWS = 16
COVER = 1


EPSILON = 1e-06
MASKED = -1e30
BF16 = jnp.bfloat16
F32 = jnp.float32
NT = (((1,), (1,)), ((), ()))
TN = (((0,), (0,)), ((), ()))


def norm_rows(activations, gain_row):
    factor = lax.rsqrt(jnp.mean(activations * activations, axis=-1, keepdims=True) + EPSILON)
    return (factor, activations * factor * gain_row)


def document_starts(segment_row):
    starts = jnp.zeros(segment_row.shape, jnp.int32)
    for number in range(1, DOCS):
        before = jnp.sum((segment_row == number - 1).astype(jnp.int32))
        starts = starts + jnp.where(segment_row >= number, before, 0)
    return starts


def key_window(block, rows):
    first = max(0, (block * rows - (DOC_MOST - 1)) // rows * rows)
    return first, (block + 1) * rows


def head_lanes(shape, head, axis):
    return lax.broadcasted_iota(jnp.int32, shape, axis) // HD == head


def turned_probs(keys, queries, starts, first, offset):
    scores = lax.dot_general(keys, queries, NT, preferred_element_type=F32) * HD ** (-0.5)
    key_ids = lax.broadcasted_iota(jnp.int32, scores.shape, 0) + first
    query_ids = lax.broadcasted_iota(jnp.int32, scores.shape, 1) + offset
    allowed = (key_ids >= starts) & (key_ids <= query_ids)
    scores = jnp.where(allowed, scores, MASKED)
    raised = jnp.exp(scores - jnp.max(scores, axis=0, keepdims=True))
    return raised * (1.0 / jnp.sum(raised, axis=0, keepdims=True))


def attend_body(start_ref, query_ref, key_ref, value_ref, out_ref, *, rows):
    length = query_ref.shape[0]
    values_turned = value_ref[...].T
    for block in range(length // rows):
        first, last = key_window(block, rows)
        span = slice(block * rows, last)
        queries = query_ref[span, :]
        mixture = jnp.zeros((LANES, rows), F32)
        for head in range(LANES // HD):
            own = jnp.where(head_lanes(queries.shape, head, 1), queries, jnp.zeros((), BF16))
            probs = turned_probs(
                key_ref[first:last, :], own, start_ref[:, span], first, block * rows
            )
            part = jnp.dot(
                values_turned[:, first:last], probs.astype(BF16), preferred_element_type=F32
            )
            mixture = jnp.where(head_lanes(part.shape, head, 0), part, mixture)
        out_ref[span, :] = mixture.T.astype(BF16)


def attend_forward(starts, queries, key_rows, value_rows, rows=256):
    length, width = queries.shape
    column = pl.BlockSpec((length, LANES), lambda i: (0, i))
    return pl.pallas_call(
        functools.partial(attend_body, rows=rows),
        grid=(width // LANES,),
        in_specs=[pl.BlockSpec((1, length), lambda i: (0, 0)), column, column, column],
        out_specs=column,
        out_shape=jax.ShapeDtypeStruct((length, width), BF16),
        compiler_params=params(32),
        cost_estimate=pl.CostEstimate(
            flops=16 * length * length * width, bytes_accessed=8 * length * width, transcendentals=0
        ),
        name="attend_forward",
    )(starts, queries, key_rows, value_rows)


def attend_back_body(
    start_ref, query_ref, key_ref, value_ref, grad_ref, dq_ref, dk_ref, dv_ref, key_sum, value_sum,
    *, rows
):
    length = query_ref.shape[0]
    keys_turned = key_ref[...].T
    key_sum[...] = jnp.zeros_like(key_sum)
    value_sum[...] = jnp.zeros_like(value_sum)
    zero = jnp.zeros((), BF16)
    factor = HD ** (-0.5)
    for block in range(length // rows):
        first, last = key_window(block, rows)
        span = slice(block * rows, last)
        window = slice(first, last)
        queries = query_ref[span, :]
        grads = grad_ref[span, :]
        query_sum = jnp.zeros((LANES, rows), F32)
        for head in range(LANES // HD):
            mask = head_lanes(queries.shape, head, 1)
            own = jnp.where(mask, queries, zero)
            own_grads = jnp.where(mask, grads, zero)
            probs = turned_probs(key_ref[window, :], own, start_ref[:, span], first, block * rows)
            prob_grad = lax.dot_general(
                value_ref[window, :], own_grads, NT, preferred_element_type=F32
            )
            centre = jnp.sum(probs * prob_grad, axis=0, keepdims=True)
            score_grad = (probs * (prob_grad - centre)).astype(BF16)
            part = jnp.dot(keys_turned[:, window], score_grad, preferred_element_type=F32)
            query_sum = jnp.where(head_lanes(part.shape, head, 0), part, query_sum)
            key_sum[window, :] += jnp.dot(score_grad, own, preferred_element_type=F32)
            value_sum[window, :] += jnp.dot(
                probs.astype(BF16), own_grads, preferred_element_type=F32
            )
        dq_ref[span, :] = (query_sum.T * factor).astype(BF16)
    dk_ref[...] = (key_sum[...] * factor).astype(BF16)
    dv_ref[...] = value_sum[...].astype(BF16)


def attend_backward(starts, queries, key_rows, value_rows, heads_grad, rows=256):
    length, width = queries.shape
    column = pl.BlockSpec((length, LANES), lambda i: (0, i))
    return pl.pallas_call(
        functools.partial(attend_back_body, rows=rows),
        grid=(width // LANES,),
        in_specs=[pl.BlockSpec((1, length), lambda i: (0, 0))] + [column] * 4,
        out_specs=[column] * 3,
        out_shape=[jax.ShapeDtypeStruct((length, width), BF16)] * 3,
        scratch_shapes=[pltpu.VMEM((length, LANES), F32)] * 2,
        compiler_params=params(40),
        cost_estimate=pl.CostEstimate(
            flops=COVER * length * length * width,
            bytes_accessed=14 * length * width,
            transcendentals=0,
        ),
        name="attend_backward",
    )(starts, queries, key_rows, value_rows, heads_grad)


SLOTS = 32


def params(mib):
    return pltpu.CompilerParams(vmem_limit_bytes=mib << 20)


def lane_numbers(shape):
    return lax.broadcasted_iota(jnp.int32, shape, len(shape) - 1)


def count_local(local, total):
    inside = (local >= 0) & (local < total)
    square = (LANES, LANES)
    upto = lax.broadcasted_iota(jnp.int32, square, 0) <= lax.broadcasted_iota(jnp.int32, square, 1)
    return jnp.dot(
        jnp.where(inside, 1.0, 0.0).astype(BF16),
        jnp.where(upto, 1.0, 0.0).astype(BF16),
        preferred_element_type=F32,
    )


def rounds_of(counts):
    most = jnp.max(counts[:, LANES - 1 :]).astype(jnp.int32)
    return (most + (SLOTS - 1)) // SLOTS


def search(counts, start):
    target = ((lane_numbers(counts.shape) & (SLOTS - 1)) + (start + 1)).astype(F32)
    place = jnp.zeros(counts.shape, jnp.int32)
    step = LANES // 2
    while step:
        seen = jnp.take_along_axis(counts, place + (step - 1), axis=1)
        place = jnp.where(seen < target, place + step, place)
        step //= 2
    return target <= counts[:, LANES - 1 :], place


def place_of(counts, local, number):
    valid, place = search(counts, number * SLOTS)
    return place, jnp.where(valid, jnp.take_along_axis(local, place, axis=1), -1)


def locate_body(base_ref, picks_ref, out_ref, *, total):
    local = picks_ref[...] - base_ref[0]
    counts = count_local(local, total)
    valid, place = search(counts, 0)
    found = jnp.where(valid, jnp.take_along_axis(local, place, axis=1) + 1, 0)
    inside = jnp.where((local >= 0) & (local < total), 1, 0)
    out_ref[...] = found | (place << 16) | (counts.astype(jnp.int32) << 23) | (inside << 31)


def found_in(located):
    return (located & 0xFFFF) - 1


def place_in(located):
    return (located >> 16) & (LANES - 1)


def count_in(located):
    return (located >> 23) & (2 * LANES - 1)


def locate(base, picks, total, rows=512):
    block = pl.BlockSpec((rows, PICKS), lambda i: (i, 0))
    amount = picks.shape[0]
    return pl.pallas_call(
        functools.partial(locate_body, total=total),
        grid=(amount // rows,),
        in_specs=[pl.BlockSpec(memory_space=pltpu.SMEM), block],
        out_specs=block,
        out_shape=pltpu.HBM((amount, PICKS), jnp.int32),
        compiler_params=params(32),
        cost_estimate=pl.CostEstimate(
            flops=amount * PICKS * 20000, bytes_accessed=amount * PICKS * 16, transcendentals=0
        ),
        name="locate",
    )(base, picks)


def group_masks():
    own = lax.broadcasted_iota(jnp.int32, (8, LANES), 0)
    lane = lane_numbers((8, LANES)) // SLOTS
    per = LANES // SLOTS
    return [own == lane + per * block for block in range(8 // per)]


def lane_table(low, masks):
    ids = lax.broadcasted_iota(jnp.int32, (NKEYS, LANES), 0).astype(F32).astype(BF16)
    parts = []
    for mask in masks:
        row = jnp.sum(jnp.where(mask, low, 0.0), axis=0, keepdims=True)
        row = jnp.broadcast_to(row, (16, LANES)).astype(BF16)
        row = jnp.concatenate([row] * (NKEYS // 16), axis=0)
        parts.append(jnp.where(ids == row, jnp.ones((), BF16), jnp.zeros((), BF16)))
    return jnp.concatenate(parts, axis=1)


def token_places(picks, shards, before):
    own = before is None
    length = picks.shape[0] if own else picks.shape[0] // shards
    blocks = length // ROWS

    def place(i, where):
        shard = where[1] if own else lax.rem(where[1] + 1 + i // blocks, shards)
        return (shard * blocks + i % blocks, 0)

    block = pl.BlockSpec((ROWS, PICKS), (lambda i, where: (i, 0)) if own else place)
    return (blocks if own else (shards - 1) * blocks), block, place, length


def bag_body(
    base_ref, picks_ref, located_ref, weight_ref, table_ref, out_ref, keep_ref, high, low, weights,
    *, chunk, unroll
):
    rows = picks_ref.shape[0]
    total = table_ref.shape[0]
    groups = total // NKEYS
    masks = group_masks()

    def eight(token):
        span = pl.ds(token, 8)
        own_high = high[span, :]
        weight = weights[span, :]
        weight = jnp.concatenate([weight, weight], axis=0).astype(BF16)
        zero = jnp.zeros((), BF16)
        parts = []
        for mask in masks:
            own = jnp.where(mask, own_high, -1.0)
            pair = jnp.concatenate([own, own - 1.0], axis=0).astype(BF16)
            rows_of = [
                jnp.where(pair == jnp.array(group, BF16), weight, zero)
                for group in range(0, groups, 2)
            ]
            parts.append(jnp.concatenate(rows_of, axis=0))
        return lax.dot_general(
            jnp.concatenate(parts, axis=1),
            lane_table(low[span, :], masks),
            NT,
            preferred_element_type=F32,
        )

    def one_round(place, found, first):
        high[...] = (found >> 8).astype(F32)
        low[...] = (found & (NKEYS - 1)).astype(F32)
        weights[...] = jnp.take_along_axis(weight_ref[...].astype(F32), place, axis=1)

        def some_tokens(step, carried):
            for slot in range(unroll):
                token = pl.multiple_of((step * unroll + slot) * 16, 16)
                top = eight(token)
                bottom = eight(token + 8)
                for group in range(groups):
                    part = slice(group * 8, group * 8 + 8)
                    block = jnp.concatenate([top[part], bottom[part]], axis=0).astype(BF16)
                    span = (pl.ds(token, 16), slice(group * NKEYS, (group + 1) * NKEYS))
                    keep_ref[span] = block if first else keep_ref[span] + block
            return carried

        lax.fori_loop(0, rows // (16 * unroll), some_tokens, 0)

    def more(number, carried):
        local = picks_ref[...] - base_ref[0]
        one_round(*place_of(counts, local, number), False)
        return carried

    located = located_ref[...]
    counts = count_in(located).astype(F32)
    one_round(place_in(located), found_in(located), True)
    lax.fori_loop(1, rounds_of(counts), more, 0)
    result = jnp.zeros(out_ref.shape, F32)
    for start in range(0, total, chunk):
        result = result + jnp.dot(
            keep_ref[:, pl.ds(start, chunk)],
            table_ref[pl.ds(start, chunk), :],
            preferred_element_type=F32,
        )
    out_ref[...] = result.astype(out_ref.dtype)


def bag_sums(base, picks, located, weights, table, chunk=1024, unroll=32):
    amount = picks.shape[0]
    total, width = table.shape
    block = pl.BlockSpec((ROWS, PICKS), lambda i: (i, 0))
    return pl.pallas_call(
        functools.partial(bag_body, chunk=chunk, unroll=unroll),
        grid=(amount // ROWS,),
        in_specs=[pl.BlockSpec(memory_space=pltpu.SMEM)]
        + [block] * 3
        + [pl.BlockSpec((total, width), lambda i: (0, 0))],
        out_specs=[
            pl.BlockSpec((ROWS, width), lambda i: (i, 0)),
            pl.BlockSpec((ROWS, total), lambda i: (i, 0)),
        ],
        out_shape=[
            jax.ShapeDtypeStruct((amount, width), BF16),
            jax.ShapeDtypeStruct((amount, total), BF16),
        ],
        scratch_shapes=[pltpu.VMEM((ROWS, LANES), F32)] * 3,
        compiler_params=params(56),
        cost_estimate=pl.CostEstimate(
            flops=9 * amount * total * width, bytes_accessed=amount * total * 2, transcendentals=0
        ),
        name="bag_sums",
    )(base, picks, located, weights, table)


def picked_body(
    base_ref, picks_ref, located_ref, grad_ref, table_ref, *rest, unroll
):
    out_ref, high, low, found_at, held = rest[-5:]
    rows = picks_ref.shape[0]
    total = table_ref.shape[1]
    groups = total // NKEYS
    masks = group_masks()
    located = located_ref[...]
    grads = grad_ref[...]
    for group in range(groups):
        held[group] = jnp.dot(
            grads,
            table_ref[:, group * NKEYS : (group + 1) * NKEYS],
            preferred_element_type=F32,
        )

    def eight(token):
        span = pl.ds(token, 8)
        left = jnp.concatenate([held[group, span, :] for group in range(groups)], axis=0)
        seen = jnp.dot(
            left.astype(BF16), lane_table(low[span, :], masks), preferred_element_type=F32
        )
        own_high = high[span, :]
        result = jnp.zeros((8, LANES), F32)
        for block, mask in enumerate(masks):
            own = jnp.where(mask, own_high, -1.0)
            for group in range(groups):
                part = seen[group * 8 : group * 8 + 8, block * LANES : (block + 1) * LANES]
                result = jnp.where(own == float(group), part, result)
        found_at[span, :] = result

    def one_round(number, found, first):
        high[...] = (found >> 8).astype(F32)
        low[...] = (found & (NKEYS - 1)).astype(F32)

        def some_tokens(step, carried):
            for slot in range(unroll):
                eight(pl.multiple_of((step * unroll + slot) * 8, 8))
            return carried

        lax.fori_loop(0, rows // (8 * unroll), some_tokens, 0)
        slot = count_in(located) - (1 + number * SLOTS)
        here = (slot >= 0) & (slot < SLOTS) & (located < 0)
        token = lax.broadcasted_iota(jnp.int32, slot.shape, 0) & (LANES // SLOTS - 1)
        lane = token * SLOTS + jnp.clip(slot, 0, SLOTS - 1)
        value = jnp.take_along_axis(found_at[...], lane, axis=1)
        before = jnp.zeros(value.shape, F32) if first else out_ref[...].astype(F32)
        out_ref[...] = jnp.where(here, value, before).astype(out_ref.dtype)

    def more(number, carried):
        local = picks_ref[...] - base_ref[0]
        one_round(number, place_of(counts, local, number)[1], False)
        return carried

    counts = count_in(located).astype(F32)
    one_round(0, found_in(located), True)
    lax.fori_loop(1, rounds_of(counts), more, 0)


def picked_products(where, picks, located, grads, table, shards, before=None, unroll=64):
    width, total = table.shape
    count, block, place, length = token_places(picks, shards, before)
    grad_map = block.index_map
    return pl.pallas_call(
        functools.partial(picked_body, unroll=unroll),
        grid_spec=pltpu.PrefetchScalarGridSpec(
            num_scalar_prefetch=1,
            grid=(count,),
            in_specs=[block] * 2
            + [
                pl.BlockSpec((ROWS, width), grad_map),
                pl.BlockSpec((width, total), lambda i, where: (0, 0)),
            ]
            + [pl.BlockSpec(memory_space=pl.ANY)] * (0 if before is None else 1),
            out_specs=pl.BlockSpec((ROWS, PICKS), place),
            scratch_shapes=[pltpu.VMEM((ROWS, LANES), F32)] * 3
            + [pltpu.VMEM((total // NKEYS, ROWS, NKEYS), F32)],
        ),
        out_shape=jax.ShapeDtypeStruct((length * shards, PICKS), BF16),
        input_output_aliases={} if before is None else {5: 0},
        compiler_params=params(56),
        cost_estimate=pl.CostEstimate(
            flops=7 * count * ROWS * total * width,
            bytes_accessed=count * ROWS * width * 4,
            transcendentals=0,
        ),
        name="picked_products",
    )(where, picks, located, grads, table, *(() if before is None else (before,)))


def gather_lanes(block, index):
    return jnp.take_along_axis(block, index, axis=1)


def over_head(block, merge):
    lanes = lane_numbers(block.shape)
    step = 1
    while step < TOPK:
        block = merge(block, gather_lanes(block, lanes ^ step))
        step *= 2
    return block


def softmax_body(score_ref, prob_ref, weight_ref):
    scores = score_ref[...]
    raised = jnp.exp(scores - over_head(scores, jnp.maximum))
    probs = raised / over_head(raised, jnp.add)
    prob_ref[...] = probs
    weight_ref[...] = probs.astype(BF16)


def pick_softmax(scores, rows=256):
    block = pl.BlockSpec((rows, PICKS), lambda i: (i, 0))
    amount = scores.shape[0]
    return pl.pallas_call(
        softmax_body,
        grid=(amount // rows,),
        in_specs=[block],
        out_specs=[block] * 2,
        out_shape=[
            jax.ShapeDtypeStruct((amount, PICKS), F32),
            jax.ShapeDtypeStruct((amount, PICKS), BF16),
        ],
        compiler_params=params(32),
        name="pick_softmax",
    )(scores)


def store_lanes(out_ref, lead, row, block):
    rows, columns = block.shape
    for start in range(0, columns, LANES):
        out_ref[(*lead, slice(row, row + rows), slice(None))] = block[:, start : start + LANES]
        row += rows
    return row


def load_lanes(ref, lead, row, rows, columns):
    parts = []
    for _ in range(columns // LANES):
        parts.append(ref[(*lead, slice(row, row + rows), slice(None))])
        row += rows
    return jnp.concatenate(parts, axis=1), row


def pack_body(
    qkv_ref, out_ref, mixer_ref, gate_ref, query_ref, keys_ref, gain_ref, packed_ref, scores_ref
):
    row = 0
    for j in range(3):
        row = store_lanes(packed_ref, (), row, qkv_ref[j])
    row = store_lanes(packed_ref, (), row, out_ref[...].T)
    row = store_lanes(packed_ref, (), row, mixer_ref[...].T)
    row = store_lanes(packed_ref, (), row, gate_ref[...])
    store_lanes(packed_ref, (), row, gain_ref[...])
    row = 0
    for unit in range(query_ref.shape[0]):
        row = store_lanes(scores_ref, (), row, query_ref[unit])
    for unit in range(keys_ref.shape[0]):
        row = store_lanes(scores_ref, (), row, keys_ref[unit])


def pack_weights(blocks, query, keys, gains):
    first = sum(block.size for block in [*blocks, gains]) // LANES
    second = (query.size + keys.size) // LANES
    return pl.pallas_call(
        pack_body,
        out_shape=[
            jax.ShapeDtypeStruct((first, LANES), BF16),
            jax.ShapeDtypeStruct((second, LANES), BF16),
        ],
        compiler_params=params(32),
        name="pack_weights",
    )(*blocks, query, keys, gains)


def unpack_body(packed_ref, q_ref, k_ref, v_ref, out_ref, mixer_ref, gate_ref, gain_ref):
    row = 0
    for target in (q_ref, k_ref, v_ref, out_ref, mixer_ref, gate_ref):
        target[...], row = load_lanes(packed_ref, (0,), row, *target.shape)
    gain_ref[0] = packed_ref[0, row : row + gain_ref.shape[1], :]


def unpack_weights(packed, part, width):
    shards, amount, _ = packed.shape
    model = shards * part
    return pl.pallas_call(
        unpack_body,
        grid=(shards,),
        in_specs=[pl.BlockSpec((1, amount, LANES), lambda i: (i, 0, 0))],
        out_specs=[pl.BlockSpec((part, width), lambda i: (i, 0))] * 6
        + [pl.BlockSpec((1, GAIN_ROWS, LANES), lambda i: (i, 0, 0))],
        out_shape=[jax.ShapeDtypeStruct((model, width), BF16)] * 6
        + [jax.ShapeDtypeStruct((shards, GAIN_ROWS, LANES), BF16)],
        compiler_params=params(32),
        name="unpack_weights",
    )(packed)


def unpack_scores_body(me_ref, packed_ref, query_ref, keys_ref):
    row = 0
    for unit in range(query_ref.shape[1] // NKEYS):
        span = slice(unit * NKEYS, (unit + 1) * NKEYS)
        query_ref[:, span], row = load_lanes(packed_ref, (0,), row, query_ref.shape[0], NKEYS)
    for unit in range(keys_ref.shape[0]):
        keys_ref[unit], row = load_lanes(packed_ref, (0,), row, keys_ref.shape[1], NKEYS)


def unpack_scores(me, packed, part, units, key_part):
    shards, amount, _ = packed.shape
    return pl.pallas_call(
        unpack_scores_body,
        grid_spec=pltpu.PrefetchScalarGridSpec(
            num_scalar_prefetch=1,
            grid=(shards,),
            in_specs=[pl.BlockSpec((1, amount, LANES), lambda i, me: (i ^ me[0], 0, 0))],
            out_specs=[
                pl.BlockSpec((part, units * NKEYS), lambda i, me: (i, 0)),
                pl.BlockSpec((units, key_part, NKEYS), lambda i, me: (0, i, 0)),
            ],
        ),
        out_shape=[
            jax.ShapeDtypeStruct((shards * part, units * NKEYS), BF16),
            jax.ShapeDtypeStruct((units, shards * key_part, NKEYS), BF16),
        ],
        compiler_params=params(32),
        name="unpack_scores",
    )(me, packed)


def grads_body(me_ref, *refs, pairs, part, units):
    lefts, rights, rest = refs[:pairs], refs[pairs : 2 * pairs], refs[2 * pairs :]
    packed_ref = rest[-1]
    per = LANES // part
    rows = [0] * per
    places = [number ^ (me_ref[0] & (per - 1)) for number in range(per)]
    for left, right in zip(lefts, rights):
        grad = lax.dot_general(left[...], right[...], TN, preferred_element_type=F32).astype(BF16)
        for number in range(per):
            own = grad[number * part : (number + 1) * part]
            rows[number] = store_lanes(packed_ref, (places[number],), rows[number], own)
    if units:
        key_ref = rest[0]
        key_part = key_ref.shape[1] // per
        for number in range(per):
            for unit in range(units):
                own = key_ref[unit, number * key_part : (number + 1) * key_part, :].astype(BF16)
                rows[number] = store_lanes(packed_ref, (places[number],), rows[number], own)


def pack_grads(me, lefts, rights, part, key_grad=None):
    length, model = lefts[0].shape
    shards = model // part
    per = LANES // part
    amount = part * sum(right.shape[1] for right in rights) // LANES
    units = 0
    extra, extra_specs = [], []
    if key_grad is not None:
        units, keys, _ = key_grad.shape
        amount += key_grad.size // shards // LANES
        extra = [key_grad]
        extra_specs = [pl.BlockSpec((units, keys // shards * per, NKEYS), lambda i, me: (0, i, 0))]
    return pl.pallas_call(
        functools.partial(grads_body, pairs=len(lefts), part=part, units=units),
        grid_spec=pltpu.PrefetchScalarGridSpec(
            num_scalar_prefetch=1,
            grid=(shards // per,),
            in_specs=[pl.BlockSpec((length, LANES), lambda i, me: (0, i))] * len(lefts)
            + [pl.BlockSpec(right.shape, lambda i, me: (0, 0)) for right in rights]
            + extra_specs,
            out_specs=pl.BlockSpec((per, amount, LANES), lambda i, me: (i ^ (me[0] // per), 0, 0)),
        ),
        out_shape=jax.ShapeDtypeStruct((shards, amount, LANES), BF16),
        compiler_params=params(48),
        cost_estimate=pl.CostEstimate(
            flops=2 * length * model * sum(right.shape[1] for right in rights),
            bytes_accessed=2 * length * model * len(lefts),
            transcendentals=0,
        ),
        name="pack_grads",
    )(me, *lefts, *rights, *extra)


def unpack_grads_body(
    early_ref, late_ref, qkv_ref, out_ref, mixer_ref, gate_ref, query_ref, keys_ref
):
    part, width = gate_ref.shape
    row = 0
    for j in range(3):
        block, row = load_lanes(late_ref, (), row, part, width)
        qkv_ref[j] = block.astype(F32)
    block, row = load_lanes(late_ref, (), row, part, width)
    out_ref[...] = block.astype(F32).T
    row = 0
    block, row = load_lanes(early_ref, (), row, part, width)
    mixer_ref[...] = block.astype(F32).T
    block, row = load_lanes(early_ref, (), row, part, width)
    gate_ref[...] = block.astype(F32)
    for unit in range(query_ref.shape[0]):
        block, row = load_lanes(early_ref, (), row, part, NKEYS)
        query_ref[unit] = block.astype(F32)
    for unit in range(keys_ref.shape[0]):
        block, row = load_lanes(early_ref, (), row, keys_ref.shape[1], NKEYS)
        keys_ref[unit] = block.astype(F32)


def unpack_grads(early, late, part, width, units, key_part):
    shapes = [
        (3, part, width),
        (width, part),
        (width, part),
        (part, width),
        (units, part, NKEYS),
        (units, key_part, NKEYS),
    ]
    return pl.pallas_call(
        unpack_grads_body,
        out_shape=[jax.ShapeDtypeStruct(shape, F32) for shape in shapes],
        compiler_params=params(32),
        name="unpack_grads",
    )(early, late)


def unit_indices(picks, number):
    return jnp.where(number % 2 == 0, picks >> 8, picks & (NKEYS - 1))


def scores_body(column_ref, picks_ref, query_ref, keys_ref, out_ref, *, units):
    picks = picks_ref[...]
    lanes = lax.broadcasted_iota(jnp.int32, picks.shape, 1)
    total = jnp.zeros(picks.shape, F32)
    for unit in range(units):
        number = column_ref[0] * units + unit
        index = unit_indices(picks, number)
        scores = lax.dot_general(
            query_ref[:, unit * NKEYS : (unit + 1) * NKEYS],
            keys_ref[unit],
            NT,
            preferred_element_type=F32,
        )
        lower = index & (LANES - 1)
        low_part = jnp.take_along_axis(scores[:, :LANES], lower, axis=1)
        high_part = jnp.take_along_axis(scores[:, LANES:], lower, axis=1)
        found = jnp.where(index < LANES, low_part, high_part)
        total = total + jnp.where(lanes // TOPK == number // 2, found, 0.0)
    out_ref[...] = total


def pick_scores(column, picks, queries, keys, rows=256):
    amount = picks.shape[0]
    units = keys.shape[0]
    return pl.pallas_call(
        functools.partial(scores_body, units=units),
        grid=(amount // rows,),
        in_specs=[
            pl.BlockSpec(memory_space=pltpu.SMEM),
            pl.BlockSpec((rows, PICKS), lambda i: (i, 0)),
            pl.BlockSpec((rows, units * NKEYS), lambda i: (i, 0)),
            pl.BlockSpec(keys.shape, lambda i: (0, 0, 0)),
        ],
        out_specs=pl.BlockSpec((rows, PICKS), lambda i: (i, 0)),
        out_shape=jax.ShapeDtypeStruct((amount, PICKS), F32),
        compiler_params=params(32),
        name="pick_scores",
    )(column, picks, queries, keys)


def spread_body(
    column_ref, picks_ref, prob_ref, grad_ref, query_ref, keys_ref, out_ref, sum_ref, held_index,
    held_grad, *, units
):
    rows = picks_ref.shape[0]
    probs = prob_ref[...]
    pick_grad = grad_ref[...]
    centre = over_head(probs * pick_grad, jnp.add)
    held_grad[...] = (probs * (pick_grad - centre)).astype(BF16).astype(F32).T

    @pl.when(pl.program_id(0) == 0)
    def clear():
        sum_ref[...] = jnp.zeros_like(sum_ref)

    key_ids = lax.broadcasted_iota(jnp.int32, (NKEYS, rows), 0)
    for unit in range(units):
        number = column_ref[0] * units + unit
        first = (number // 2) * TOPK
        held_index[...] = unit_indices(picks_ref[...], number).T
        table = jnp.zeros((NKEYS, rows), F32)
        for slot in range(TOPK):
            index = held_index[pl.ds(first + slot, 1), :]
            grad = held_grad[pl.ds(first + slot, 1), :]
            table = table + jnp.where(key_ids == index, grad, 0.0)
        table = table.astype(BF16)
        span = slice(unit * NKEYS, (unit + 1) * NKEYS)
        out_ref[:, span] = lax.dot_general(
            table, keys_ref[unit], TN, preferred_element_type=F32
        ).astype(BF16)
        sum_ref[unit] += jnp.dot(table, query_ref[:, span], preferred_element_type=F32)


def spread_grads(column, picks, probs, grads, queries, keys, rows=128):
    amount = picks.shape[0]
    units = keys.shape[0]
    return pl.pallas_call(
        functools.partial(spread_body, units=units),
        grid=(amount // rows,),
        in_specs=[
            pl.BlockSpec(memory_space=pltpu.SMEM),
            pl.BlockSpec((rows, PICKS), lambda i: (i, 0)),
            pl.BlockSpec((rows, PICKS), lambda i: (i, 0)),
            pl.BlockSpec((rows, PICKS), lambda i: (i, 0)),
            pl.BlockSpec((rows, units * NKEYS), lambda i: (i, 0)),
            pl.BlockSpec(keys.shape, lambda i: (0, 0, 0)),
        ],
        out_specs=[
            pl.BlockSpec((rows, units * NKEYS), lambda i: (i, 0)),
            pl.BlockSpec(keys.shape, lambda i: (0, 0, 0)),
        ],
        out_shape=[
            jax.ShapeDtypeStruct((amount, units * NKEYS), BF16),
            jax.ShapeDtypeStruct(keys.shape, F32),
        ],
        scratch_shapes=[pltpu.VMEM((PICKS, rows), jnp.int32), pltpu.VMEM((PICKS, rows), F32)],
        compiler_params=params(32),
        name="spread_grads",
    )(column, picks, probs, grads, queries, keys)


def swap_narrow(block, bit):
    size = lax.axis_size("narrow")
    return lax.ppermute(block, "narrow", [(i, i ^ bit) for i in range(size)])


def swap_all(held, axis, bit):
    pairs = [(i, i ^ bit) for i in range(lax.axis_size(axis))]
    moved = {offset ^ bit: lax.ppermute(part, axis, pairs) for offset, part in held.items()}
    return {**held, **moved}


def in_order(held, axis):
    me = lax.axis_index(axis)
    size = lax.axis_size(axis)
    stacked = jnp.stack([held[offset] for offset in range(size)])
    return [lax.dynamic_index_in_dim(stacked, me ^ number, 0, False) for number in range(size)]


def gather_by_swaps(block, axis, bits):
    held = {0: block}
    for bit in bits:
        held = swap_all(held, axis, bit)
    return in_order(held, axis)


def sum_by_swaps(block, axis):
    for bit in bits_down(lax.axis_size(axis)):
        block = block + lax.ppermute(
            block, axis, [(i, i ^ bit) for i in range(lax.axis_size(axis))]
        )
    return block


def scatter_narrow(block):
    size = lax.axis_size("narrow")
    me = lax.axis_index("narrow")
    width = block.shape[1] // size
    parts = jnp.stack([block[:, n * width : (n + 1) * width] for n in range(size)])
    held = [lax.dynamic_index_in_dim(parts, me ^ offset, 0, False) for offset in range(size)]
    for bit in bits_down(size)[::-1]:
        arrived = {
            offset: swap_narrow(held[offset ^ bit].astype(BF16), bit)
            for offset in range(size)
            if not offset & (2 * bit - 1)
        }
        held = {
            offset: held[offset].astype(F32) + value.astype(F32)
            for offset, value in arrived.items()
        }
    return held[0]


def bits_down(size):
    return [1 << level for level in reversed(range(size.bit_length() - 1))]


def scatter_by_swaps(blocks, axis, bits, other=None):
    size = lax.axis_size(axis)
    held = {offset: blocks[offset] for offset in range(size)}
    for bit in bits:
        if bit == bits[-1] and other is not None:
            held, other = lax.optimization_barrier((held, other))
        sent = jnp.stack([held[offset] for offset in sorted(held) if offset & bit])
        kept = [offset for offset in sorted(held) if not offset & bit]
        arrived = lax.ppermute(sent.astype(BF16), axis, [(i, i ^ bit) for i in range(size)])
        held = {
            offset: held[offset].astype(F32) + arrived[place].astype(F32)
            for place, offset in enumerate(kept)
        }
    return held[0], other


def gather_narrow(block):
    return jnp.concatenate(
        gather_by_swaps(block, "narrow", bits_down(lax.axis_size("narrow"))), axis=1
    )


def gather_wide(block):
    return lax.all_gather(block, "wide")


def sum_wide(block):
    return lax.psum_scatter(block, "wide", scatter_dimension=0)


def per_device(
    inputs,
    segments,
    attn_gain,
    qkv_weight,
    out_weight,
    memory_gain,
    query_weight,
    sub_keys,
    gate_weight,
    memory_values,
    memory_out,
    picks,
    cotangent,
):
    length, width = inputs.shape
    shards = lax.axis_size("wide")
    column = lax.axis_index("narrow")
    column_ref = column.astype(jnp.int32).reshape(1)
    shard_rows = memory_values.shape[0]
    base = (lax.axis_index("wide") * shard_rows).astype(jnp.int32).reshape(1)
    units = sub_keys.shape[0]
    part = qkv_weight.shape[0]
    model = part * shards
    key_part = sub_keys.shape[1]

    rows_one = gather_narrow(inputs).astype(F32)
    gains = jnp.concatenate([attn_gain, memory_gain]).reshape(-1, LANES)
    gains = jnp.pad(gains, ((0, GAIN_ROWS - gains.shape[0]), (0, 0)))
    packed, scores_packed = pack_weights(
        [
            jnp.transpose(qkv_weight, (1, 0, 2)),
            out_weight,
            memory_out,
            gate_weight,
        ],
        jnp.transpose(query_weight, (1, 0, 2)),
        sub_keys,
        gains,
    )
    packed = gather_wide(packed)
    moving = {0: scores_packed}
    for bit in bits_down(shards):
        moving = swap_all(moving, "wide", bit)
    moving = jnp.stack([moving[offset] for offset in range(shards)])
    table_turned = memory_values.T
    located_own = locate(base, picks, shard_rows)
    packed, moving, table_turned, located_own = lax.optimization_barrier(
        (packed, moving, table_turned, located_own)
    )
    (
        query_matrix, key_matrix, value_matrix, out_turned, mixer_turned, gate_full, gains
    ) = unpack_weights(packed, part, width)
    me_wide = lax.axis_index("wide").astype(jnp.int32).reshape(1)
    query_full, keys_full = unpack_scores(me_wide, moving, part, units, key_part)
    qkv_full = [query_matrix, key_matrix, value_matrix]
    gains = gains.reshape(shards, -1)[:, : 2 * part].reshape(shards, 2, part).astype(F32)
    gain_one = gains[:, 0].reshape(model)
    gain_two = gains[:, 1].reshape(model)
    out_all = gather_narrow(out_turned)
    upstream = gather_narrow(cotangent)
    half = length // 2
    pairs = picks[:half] | (picks[half:] << 16)
    pairs, packed = lax.optimization_barrier((pairs, packed))
    pairs = gather_wide(pairs)
    all_picks = jnp.concatenate([pairs & 0xFFFF, (pairs >> 16) & 0xFFFF], axis=1)
    all_picks = all_picks.reshape(shards * length, PICKS)
    located = locate(base, all_picks, shard_rows)
    where = jnp.concatenate([base, me_wide])

    factor_one, normed = norm_rows(rows_one, gain_one)
    normed = normed.astype(BF16)
    queries, key_rows, value_rows = [
        jnp.dot(normed, qkv_full[j], preferred_element_type=F32).astype(BF16) for j in range(3)
    ]
    starts = document_starts(segments)
    head_rows = attend_forward(starts, queries, key_rows, value_rows)
    head_all = gather_narrow(head_rows)
    hidden = rows_one + lax.dot_general(head_all, out_all, NT, preferred_element_type=F32)
    factor_two, second = norm_rows(hidden, gain_two)
    second = second.astype(BF16)

    gate_value = jnp.dot(second, gate_full, preferred_element_type=F32)
    gate_act = jax.nn.silu(gate_value)
    product_grad = jnp.dot(upstream, mixer_turned, preferred_element_type=F32)
    memory_grad = (product_grad * gate_act).astype(BF16)
    all_grads = gather_wide(memory_grad).reshape(shards * length, width)

    memory_query = jnp.dot(second, query_full, preferred_element_type=F32).astype(BF16)
    own_scores = pick_scores(column_ref, picks, memory_query, keys_full)
    mem_probs, pick_weights = pick_softmax(sum_by_swaps(own_scores, "narrow"))
    pick_weights, memory_grad = lax.optimization_barrier((pick_weights, memory_grad))
    all_weights = gather_wide(pick_weights).reshape(shards * length, PICKS)

    pick_part = picked_products(where, picks, located_own, memory_grad, table_turned, shards)
    pick_part = picked_products(
        where, all_picks, located, all_grads, table_turned, shards, pick_part
    )
    all_weights, pick_part = lax.optimization_barrier((all_weights, pick_part))
    pick_own = sum_wide(pick_part.reshape(shards, length, PICKS)).astype(F32)
    memory_part, tables = bag_sums(base, all_picks, located, all_weights, memory_values)
    memory_part, pick_own = lax.optimization_barrier((memory_part, pick_own))
    memory_own = sum_wide(memory_part.reshape(shards, length, width))
    values_grad = lax.dot_general(tables, all_grads, TN, preferred_element_type=F32)
    memory_own, values_grad = lax.optimization_barrier((memory_own, values_grad))
    memory = memory_own.astype(F32)

    pick_grad = sum_by_swaps(pick_own, "narrow")
    memory_query_grad, key_grad = spread_grads(
        column_ref, picks, mem_probs, pick_grad, memory_query, keys_full
    )

    product = (gate_act * memory).astype(BF16)
    sigmoid = jax.nn.sigmoid(gate_value)
    gate_rows_grad = (
        product_grad * memory * sigmoid * (1.0 + gate_value * (1.0 - sigmoid))
    ).astype(BF16)
    early_pack = pack_grads(
        column_ref * 0,
        [upstream, second, second],
        [product, gate_rows_grad, memory_query_grad],
        part,
        key_grad,
    )
    early_sums = sum_wide(early_pack)
    second_part = lax.dot_general(gate_rows_grad, gate_full, NT, preferred_element_type=F32)
    second_part = second_part + lax.dot_general(
        memory_query_grad, query_full, NT, preferred_element_type=F32
    )
    turned = second_part * gain_two
    inner_part = jnp.sum(turned * hidden, axis=-1)
    gain_two_part = jnp.sum(second_part * hidden * factor_two, axis=0)
    tiny = sum_by_swaps(jnp.concatenate([inner_part, gain_two_part]), "narrow")
    inner_two = tiny[:length, None] / model
    gain_two_part = tiny[length:]
    own_second_grad = scatter_narrow(second_part)

    def own_columns(block):
        return lax.dynamic_slice_in_dim(block, column * width, width, block.ndim - 1)

    own_hidden = own_columns(hidden)
    own_hidden_grad = (
        cotangent.astype(F32)
        + factor_two * own_columns(gain_two) * own_second_grad
        - own_hidden * (factor_two * factor_two * factor_two) * inner_two
    )
    branch_grad = own_hidden_grad.astype(BF16)
    branch_grad, early_pack = lax.optimization_barrier((branch_grad, early_pack))
    branch_grad = gather_narrow(branch_grad)

    mixer_part = lax.dot_general(product, mixer_turned, NT, preferred_element_type=F32)
    mixer_part, branch_grad = lax.optimization_barrier((mixer_part, branch_grad))
    outputs = (own_hidden + scatter_narrow(mixer_part)).astype(BF16)

    heads_grad = jnp.dot(branch_grad, out_turned, preferred_element_type=F32)
    heads_grad = heads_grad.astype(BF16)

    mixed_grad = attend_backward(starts, queries, key_rows, value_rows, heads_grad)
    normed_part = sum(
        lax.dot_general(mixed_grad[j], qkv_full[j], NT, preferred_element_type=F32)
        for j in range(3)
    )
    late_pack = pack_grads(
        me_wide, [normed, normed, normed, branch_grad], [*mixed_grad, head_rows], part
    )
    bits = bits_down(shards)
    cut = late_pack.shape[1] * 5 // 8 // 16 * 16
    upper_sums, early_sums = scatter_by_swaps(late_pack[:, :cut], "wide", bits[::-1], early_sums)
    lower_sums, _ = scatter_by_swaps(late_pack[:, cut:], "wide", bits)
    late_sums = jnp.concatenate([upper_sums, lower_sums], axis=0)
    inner_part = jnp.sum(normed_part * gain_one * rows_one, axis=-1)
    gain_one_part = jnp.sum(normed_part * rows_one * factor_one, axis=0)
    tiny = sum_by_swaps(jnp.concatenate([inner_part, gain_one_part]), "narrow")
    inner_one = tiny[:length, None] / model
    gain_one_part = tiny[length:]
    own_normed_grad = scatter_narrow(normed_part)
    input_grad = (
        own_hidden_grad
        + factor_one * own_columns(gain_one) * own_normed_grad
        - inputs.astype(F32) * (factor_one * factor_one * factor_one) * inner_one
    )
    gain_sums = sum_by_swaps(jnp.stack([gain_one_part, gain_two_part]), "wide")
    gain_sums = lax.dynamic_slice_in_dim(gain_sums, lax.axis_index("wide") * part, part, 1)
    qkv_sum, out_sum, mixer_sum, gate_sum, query_sum, key_sum = unpack_grads(
        early_sums, late_sums, part, width, units, key_part
    )
    return (
        outputs,
        input_grad,
        gain_sums[0],
        jnp.transpose(qkv_sum, (1, 0, 2)),
        out_sum,
        gain_sums[1],
        jnp.transpose(query_sum, (1, 0, 2)),
        key_sum,
        gate_sum,
        values_grad,
        mixer_sum,
    )


def solution(mesh):
    return jax.shard_map(
        per_device,
        mesh=mesh,
        in_specs=(
            P("wide", "narrow"),
            P("wide", None),
            P("wide"),
            P("wide", None, "narrow"),
            P("narrow", "wide"),
            P("wide"),
            P("wide", "narrow", None),
            P("narrow", "wide", None),
            P("wide", "narrow"),
            P("wide", "narrow"),
            P("narrow", "wide"),
            P("wide", None),
            P("wide", "narrow"),
        ),
        out_specs=(
            P("wide", "narrow"),
            P("wide", "narrow"),
            P("wide"),
            P("wide", None, "narrow"),
            P("narrow", "wide"),
            P("wide"),
            P("wide", "narrow", None),
            P("narrow", "wide", None),
            P("wide", "narrow"),
            P("wide", "narrow"),
            P("narrow", "wide"),
        ),
        check_vma=False,
    )
```

```python
import functools

import jax
import jax.numpy as jnp
from jax import lax
from jax.experimental import pallas as pl
from jax.experimental.pallas import tpu as pltpu
from jax.sharding import PartitionSpec as P

HD = 64
PKH = 4
NKEYS = 256
TOPK = 32
PICKS = 128
DOCS = 3
DOC_MOST = 512
LANES = 128
ROWS = 512
GAIN_ROWS = 16
COVER = 1


EPSILON = 1e-06
MASKED = -1e30
BF16 = jnp.bfloat16
F32 = jnp.float32
NT = (((1,), (1,)), ((), ()))
TN = (((0,), (0,)), ((), ()))


def norm_rows(activations, gain_row):
    factor = lax.rsqrt(jnp.mean(activations * activations, axis=-1, keepdims=True) + EPSILON)
    return (factor, activations * factor * gain_row)


def document_starts(segment_row):
    starts = jnp.zeros(segment_row.shape, jnp.int32)
    for number in range(1, DOCS):
        before = jnp.sum((segment_row == number - 1).astype(jnp.int32))
        starts = starts + jnp.where(segment_row >= number, before, 0)
    return starts


def key_window(block, rows):
    first = max(0, (block * rows - (DOC_MOST - 1)) // rows * rows)
    return first, (block + 1) * rows


def head_lanes(shape, head, axis):
    return lax.broadcasted_iota(jnp.int32, shape, axis) // HD == head


def turned_probs(keys, queries, starts, first, offset):
    scores = lax.dot_general(keys, queries, NT, preferred_element_type=F32) * HD ** (-0.5)
    key_ids = lax.broadcasted_iota(jnp.int32, scores.shape, 0) + first
    query_ids = lax.broadcasted_iota(jnp.int32, scores.shape, 1) + offset
    allowed = (key_ids >= starts) & (key_ids <= query_ids)
    scores = jnp.where(allowed, scores, MASKED)
    raised = jnp.exp(scores - jnp.max(scores, axis=0, keepdims=True))
    return raised * (1.0 / jnp.sum(raised, axis=0, keepdims=True))


def attend_body(start_ref, query_ref, key_ref, value_ref, out_ref, *, rows):
    length = query_ref.shape[0]
    values_turned = value_ref[...].T
    for block in range(length // rows):
        first, last = key_window(block, rows)
        span = slice(block * rows, last)
        queries = query_ref[span, :]
        mixture = jnp.zeros((LANES, rows), F32)
        for head in range(LANES // HD):
            own = jnp.where(head_lanes(queries.shape, head, 1), queries, jnp.zeros((), BF16))
            probs = turned_probs(
                key_ref[first:last, :], own, start_ref[:, span], first, block * rows
            )
            part = jnp.dot(
                values_turned[:, first:last], probs.astype(BF16), preferred_element_type=F32
            )
            mixture = jnp.where(head_lanes(part.shape, head, 0), part, mixture)
        out_ref[span, :] = mixture.T.astype(BF16)


def attend_forward(starts, queries, key_rows, value_rows, rows=256):
    length, width = queries.shape
    column = pl.BlockSpec((length, LANES), lambda i: (0, i))
    return pl.pallas_call(
        functools.partial(attend_body, rows=rows),
        grid=(width // LANES,),
        in_specs=[pl.BlockSpec((1, length), lambda i: (0, 0)), column, column, column],
        out_specs=column,
        out_shape=jax.ShapeDtypeStruct((length, width), BF16),
        compiler_params=params(32),
        cost_estimate=pl.CostEstimate(
            flops=16 * length * length * width, bytes_accessed=8 * length * width, transcendentals=0
        ),
        name="attend_forward",
    )(starts, queries, key_rows, value_rows)


def attend_back_body(
    start_ref, query_ref, key_ref, value_ref, grad_ref, dq_ref, dk_ref, dv_ref, key_sum, value_sum,
    *, rows
):
    length = query_ref.shape[0]
    keys_turned = key_ref[...].T
    key_sum[...] = jnp.zeros_like(key_sum)
    value_sum[...] = jnp.zeros_like(value_sum)
    zero = jnp.zeros((), BF16)
    factor = HD ** (-0.5)
    for block in range(length // rows):
        first, last = key_window(block, rows)
        span = slice(block * rows, last)
        window = slice(first, last)
        queries = query_ref[span, :]
        grads = grad_ref[span, :]
        query_sum = jnp.zeros((LANES, rows), F32)
        for head in range(LANES // HD):
            mask = head_lanes(queries.shape, head, 1)
            own = jnp.where(mask, queries, zero)
            own_grads = jnp.where(mask, grads, zero)
            probs = turned_probs(key_ref[window, :], own, start_ref[:, span], first, block * rows)
            prob_grad = lax.dot_general(
                value_ref[window, :], own_grads, NT, preferred_element_type=F32
            )
            centre = jnp.sum(probs * prob_grad, axis=0, keepdims=True)
            score_grad = (probs * (prob_grad - centre)).astype(BF16)
            part = jnp.dot(keys_turned[:, window], score_grad, preferred_element_type=F32)
            query_sum = jnp.where(head_lanes(part.shape, head, 0), part, query_sum)
            key_sum[window, :] += jnp.dot(score_grad, own, preferred_element_type=F32)
            value_sum[window, :] += jnp.dot(
                probs.astype(BF16), own_grads, preferred_element_type=F32
            )
        dq_ref[span, :] = (query_sum.T * factor).astype(BF16)
    dk_ref[...] = (key_sum[...] * factor).astype(BF16)
    dv_ref[...] = value_sum[...].astype(BF16)


def attend_backward(starts, queries, key_rows, value_rows, heads_grad, rows=256):
    length, width = queries.shape
    column = pl.BlockSpec((length, LANES), lambda i: (0, i))
    return pl.pallas_call(
        functools.partial(attend_back_body, rows=rows),
        grid=(width // LANES,),
        in_specs=[pl.BlockSpec((1, length), lambda i: (0, 0))] + [column] * 4,
        out_specs=[column] * 3,
        out_shape=[jax.ShapeDtypeStruct((length, width), BF16)] * 3,
        scratch_shapes=[pltpu.VMEM((length, LANES), F32)] * 2,
        compiler_params=params(40),
        cost_estimate=pl.CostEstimate(
            flops=COVER * length * length * width,
            bytes_accessed=14 * length * width,
            transcendentals=0,
        ),
        name="attend_backward",
    )(starts, queries, key_rows, value_rows, heads_grad)


SLOTS = 32


def params(mib):
    return pltpu.CompilerParams(vmem_limit_bytes=mib << 20)


def lane_numbers(shape):
    return lax.broadcasted_iota(jnp.int32, shape, len(shape) - 1)


def count_local(local, total):
    inside = (local >= 0) & (local < total)
    square = (LANES, LANES)
    upto = lax.broadcasted_iota(jnp.int32, square, 0) <= lax.broadcasted_iota(jnp.int32, square, 1)
    return jnp.dot(
        jnp.where(inside, 1.0, 0.0).astype(BF16),
        jnp.where(upto, 1.0, 0.0).astype(BF16),
        preferred_element_type=F32,
    )


def rounds_of(counts):
    most = jnp.max(counts[:, LANES - 1 :]).astype(jnp.int32)
    return (most + (SLOTS - 1)) // SLOTS


def search(counts, start):
    target = ((lane_numbers(counts.shape) & (SLOTS - 1)) + (start + 1)).astype(F32)
    place = jnp.zeros(counts.shape, jnp.int32)
    step = LANES // 2
    while step:
        seen = jnp.take_along_axis(counts, place + (step - 1), axis=1)
        place = jnp.where(seen < target, place + step, place)
        step //= 2
    return target <= counts[:, LANES - 1 :], place


def place_of(counts, local, number):
    valid, place = search(counts, number * SLOTS)
    return place, jnp.where(valid, jnp.take_along_axis(local, place, axis=1), -1)


def locate_body(base_ref, picks_ref, out_ref, *, total):
    local = picks_ref[...] - base_ref[0]
    counts = count_local(local, total)
    valid, place = search(counts, 0)
    found = jnp.where(valid, jnp.take_along_axis(local, place, axis=1) + 1, 0)
    inside = jnp.where((local >= 0) & (local < total), 1, 0)
    out_ref[...] = found | (place << 16) | (counts.astype(jnp.int32) << 23) | (inside << 31)


def found_in(located):
    return (located & 0xFFFF) - 1


def place_in(located):
    return (located >> 16) & (LANES - 1)


def count_in(located):
    return (located >> 23) & (2 * LANES - 1)


def locate(base, picks, total, rows=512):
    block = pl.BlockSpec((rows, PICKS), lambda i: (i, 0))
    amount = picks.shape[0]
    return pl.pallas_call(
        functools.partial(locate_body, total=total),
        grid=(amount // rows,),
        in_specs=[pl.BlockSpec(memory_space=pltpu.SMEM), block],
        out_specs=block,
        out_shape=pltpu.HBM((amount, PICKS), jnp.int32),
        compiler_params=params(32),
        cost_estimate=pl.CostEstimate(
            flops=amount * PICKS * 20000, bytes_accessed=amount * PICKS * 16, transcendentals=0
        ),
        name="locate",
    )(base, picks)


def group_masks():
    own = lax.broadcasted_iota(jnp.int32, (8, LANES), 0)
    lane = lane_numbers((8, LANES)) // SLOTS
    per = LANES // SLOTS
    return [own == lane + per * block for block in range(8 // per)]


def lane_table(low, masks):
    ids = lax.broadcasted_iota(jnp.int32, (NKEYS, LANES), 0).astype(F32).astype(BF16)
    parts = []
    for mask in masks:
        row = jnp.sum(jnp.where(mask, low, 0.0), axis=0, keepdims=True)
        row = jnp.broadcast_to(row, (16, LANES)).astype(BF16)
        row = jnp.concatenate([row] * (NKEYS // 16), axis=0)
        parts.append(jnp.where(ids == row, jnp.ones((), BF16), jnp.zeros((), BF16)))
    return jnp.concatenate(parts, axis=1)


def token_places(picks, shards, before):
    own = before is None
    length = picks.shape[0] if own else picks.shape[0] // shards
    blocks = length // ROWS

    def place(i, where):
        shard = where[1] if own else lax.rem(where[1] + 1 + i // blocks, shards)
        return (shard * blocks + i % blocks, 0)

    block = pl.BlockSpec((ROWS, PICKS), (lambda i, where: (i, 0)) if own else place)
    return (blocks if own else (shards - 1) * blocks), block, place, length


def bag_body(
    base_ref, picks_ref, located_ref, weight_ref, table_ref, out_ref, keep_ref, high, low, weights,
    *, chunk, unroll
):
    rows = picks_ref.shape[0]
    total = table_ref.shape[0]
    groups = total // NKEYS
    masks = group_masks()

    def eight(token):
        span = pl.ds(token, 8)
        own_high = high[span, :]
        weight = weights[span, :]
        weight = jnp.concatenate([weight, weight], axis=0).astype(BF16)
        zero = jnp.zeros((), BF16)
        parts = []
        for mask in masks:
            own = jnp.where(mask, own_high, -1.0)
            pair = jnp.concatenate([own, own - 1.0], axis=0).astype(BF16)
            rows_of = [
                jnp.where(pair == jnp.array(group, BF16), weight, zero)
                for group in range(0, groups, 2)
            ]
            parts.append(jnp.concatenate(rows_of, axis=0))
        return lax.dot_general(
            jnp.concatenate(parts, axis=1),
            lane_table(low[span, :], masks),
            NT,
            preferred_element_type=F32,
        )

    def one_round(place, found, first):
        high[...] = (found >> 8).astype(F32)
        low[...] = (found & (NKEYS - 1)).astype(F32)
        weights[...] = jnp.take_along_axis(weight_ref[...].astype(F32), place, axis=1)

        def some_tokens(step, carried):
            for slot in range(unroll):
                token = pl.multiple_of((step * unroll + slot) * 16, 16)
                top = eight(token)
                bottom = eight(token + 8)
                for group in range(groups):
                    part = slice(group * 8, group * 8 + 8)
                    block = jnp.concatenate([top[part], bottom[part]], axis=0).astype(BF16)
                    span = (pl.ds(token, 16), slice(group * NKEYS, (group + 1) * NKEYS))
                    keep_ref[span] = block if first else keep_ref[span] + block
            return carried

        lax.fori_loop(0, rows // (16 * unroll), some_tokens, 0)

    def more(number, carried):
        local = picks_ref[...] - base_ref[0]
        one_round(*place_of(counts, local, number), False)
        return carried

    located = located_ref[...]
    counts = count_in(located).astype(F32)
    one_round(place_in(located), found_in(located), True)
    lax.fori_loop(1, rounds_of(counts), more, 0)
    result = jnp.zeros(out_ref.shape, F32)
    for start in range(0, total, chunk):
        result = result + jnp.dot(
            keep_ref[:, pl.ds(start, chunk)],
            table_ref[pl.ds(start, chunk), :],
            preferred_element_type=F32,
        )
    out_ref[...] = result.astype(out_ref.dtype)


def bag_sums(base, picks, located, weights, table, chunk=1024, unroll=32):
    amount = picks.shape[0]
    total, width = table.shape
    block = pl.BlockSpec((ROWS, PICKS), lambda i: (i, 0))
    return pl.pallas_call(
        functools.partial(bag_body, chunk=chunk, unroll=unroll),
        grid=(amount // ROWS,),
        in_specs=[pl.BlockSpec(memory_space=pltpu.SMEM)]
        + [block] * 3
        + [pl.BlockSpec((total, width), lambda i: (0, 0))],
        out_specs=[
            pl.BlockSpec((ROWS, width), lambda i: (i, 0)),
            pl.BlockSpec((ROWS, total), lambda i: (i, 0)),
        ],
        out_shape=[
            jax.ShapeDtypeStruct((amount, width), BF16),
            jax.ShapeDtypeStruct((amount, total), BF16),
        ],
        scratch_shapes=[pltpu.VMEM((ROWS, LANES), F32)] * 3,
        compiler_params=params(56),
        cost_estimate=pl.CostEstimate(
            flops=9 * amount * total * width, bytes_accessed=amount * total * 2, transcendentals=0
        ),
        name="bag_sums",
    )(base, picks, located, weights, table)


def picked_body(
    base_ref, picks_ref, located_ref, grad_ref, table_ref, *rest, unroll
):
    out_ref, high, low, found_at, held = rest[-5:]
    rows = picks_ref.shape[0]
    total = table_ref.shape[1]
    groups = total // NKEYS
    masks = group_masks()
    located = located_ref[...]
    grads = grad_ref[...]
    for group in range(groups):
        held[group] = jnp.dot(
            grads,
            table_ref[:, group * NKEYS : (group + 1) * NKEYS],
            preferred_element_type=F32,
        )

    def eight(token):
        span = pl.ds(token, 8)
        left = jnp.concatenate([held[group, span, :] for group in range(groups)], axis=0)
        seen = jnp.dot(
            left.astype(BF16), lane_table(low[span, :], masks), preferred_element_type=F32
        )
        own_high = high[span, :]
        result = jnp.zeros((8, LANES), F32)
        for block, mask in enumerate(masks):
            own = jnp.where(mask, own_high, -1.0)
            for group in range(groups):
                part = seen[group * 8 : group * 8 + 8, block * LANES : (block + 1) * LANES]
                result = jnp.where(own == float(group), part, result)
        found_at[span, :] = result

    def one_round(number, found, first):
        high[...] = (found >> 8).astype(F32)
        low[...] = (found & (NKEYS - 1)).astype(F32)

        def some_tokens(step, carried):
            for slot in range(unroll):
                eight(pl.multiple_of((step * unroll + slot) * 8, 8))
            return carried

        lax.fori_loop(0, rows // (8 * unroll), some_tokens, 0)
        slot = count_in(located) - (1 + number * SLOTS)
        here = (slot >= 0) & (slot < SLOTS) & (located < 0)
        token = lax.broadcasted_iota(jnp.int32, slot.shape, 0) & (LANES // SLOTS - 1)
        lane = token * SLOTS + jnp.clip(slot, 0, SLOTS - 1)
        value = jnp.take_along_axis(found_at[...], lane, axis=1)
        before = jnp.zeros(value.shape, F32) if first else out_ref[...].astype(F32)
        out_ref[...] = jnp.where(here, value, before).astype(out_ref.dtype)

    def more(number, carried):
        local = picks_ref[...] - base_ref[0]
        one_round(number, place_of(counts, local, number)[1], False)
        return carried

    counts = count_in(located).astype(F32)
    one_round(0, found_in(located), True)
    lax.fori_loop(1, rounds_of(counts), more, 0)


def picked_products(where, picks, located, grads, table, shards, before=None, unroll=64):
    width, total = table.shape
    count, block, place, length = token_places(picks, shards, before)
    grad_map = block.index_map
    return pl.pallas_call(
        functools.partial(picked_body, unroll=unroll),
        grid_spec=pltpu.PrefetchScalarGridSpec(
            num_scalar_prefetch=1,
            grid=(count,),
            in_specs=[block] * 2
            + [
                pl.BlockSpec((ROWS, width), grad_map),
                pl.BlockSpec((width, total), lambda i, where: (0, 0)),
            ]
            + [pl.BlockSpec(memory_space=pl.ANY)] * (0 if before is None else 1),
            out_specs=pl.BlockSpec((ROWS, PICKS), place),
            scratch_shapes=[pltpu.VMEM((ROWS, LANES), F32)] * 3
            + [pltpu.VMEM((total // NKEYS, ROWS, NKEYS), F32)],
        ),
        out_shape=jax.ShapeDtypeStruct((length * shards, PICKS), BF16),
        input_output_aliases={} if before is None else {5: 0},
        compiler_params=params(56),
        cost_estimate=pl.CostEstimate(
            flops=7 * count * ROWS * total * width,
            bytes_accessed=count * ROWS * width * 4,
            transcendentals=0,
        ),
        name="picked_products",
    )(where, picks, located, grads, table, *(() if before is None else (before,)))


def gather_lanes(block, index):
    return jnp.take_along_axis(block, index, axis=1)


def over_head(block, merge):
    lanes = lane_numbers(block.shape)
    step = 1
    while step < TOPK:
        block = merge(block, gather_lanes(block, lanes ^ step))
        step *= 2
    return block


def softmax_body(score_ref, prob_ref, weight_ref):
    scores = score_ref[...]
    raised = jnp.exp(scores - over_head(scores, jnp.maximum))
    probs = raised / over_head(raised, jnp.add)
    prob_ref[...] = probs
    weight_ref[...] = probs.astype(BF16)


def pick_softmax(scores, rows=256):
    block = pl.BlockSpec((rows, PICKS), lambda i: (i, 0))
    amount = scores.shape[0]
    return pl.pallas_call(
        softmax_body,
        grid=(amount // rows,),
        in_specs=[block],
        out_specs=[block] * 2,
        out_shape=[
            jax.ShapeDtypeStruct((amount, PICKS), F32),
            jax.ShapeDtypeStruct((amount, PICKS), BF16),
        ],
        compiler_params=params(32),
        name="pick_softmax",
    )(scores)


def store_lanes(out_ref, lead, row, block):
    rows, columns = block.shape
    for start in range(0, columns, LANES):
        out_ref[(*lead, slice(row, row + rows), slice(None))] = block[:, start : start + LANES]
        row += rows
    return row


def load_lanes(ref, lead, row, rows, columns):
    parts = []
    for _ in range(columns // LANES):
        parts.append(ref[(*lead, slice(row, row + rows), slice(None))])
        row += rows
    return jnp.concatenate(parts, axis=1), row


def pack_body(
    qkv_ref, out_ref, mixer_ref, gate_ref, query_ref, keys_ref, gain_ref, packed_ref, scores_ref
):
    row = 0
    for j in range(3):
        row = store_lanes(packed_ref, (), row, qkv_ref[j])
    row = store_lanes(packed_ref, (), row, out_ref[...].T)
    row = store_lanes(packed_ref, (), row, mixer_ref[...].T)
    row = store_lanes(packed_ref, (), row, gate_ref[...])
    store_lanes(packed_ref, (), row, gain_ref[...])
    row = 0
    for unit in range(query_ref.shape[0]):
        row = store_lanes(scores_ref, (), row, query_ref[unit])
    for unit in range(keys_ref.shape[0]):
        row = store_lanes(scores_ref, (), row, keys_ref[unit])


def pack_weights(blocks, query, keys, gains):
    first = sum(block.size for block in [*blocks, gains]) // LANES
    second = (query.size + keys.size) // LANES
    return pl.pallas_call(
        pack_body,
        out_shape=[
            jax.ShapeDtypeStruct((first, LANES), BF16),
            jax.ShapeDtypeStruct((second, LANES), BF16),
        ],
        compiler_params=params(32),
        name="pack_weights",
    )(*blocks, query, keys, gains)


def unpack_body(packed_ref, q_ref, k_ref, v_ref, out_ref, mixer_ref, gate_ref, gain_ref):
    row = 0
    for target in (q_ref, k_ref, v_ref, out_ref, mixer_ref, gate_ref):
        target[...], row = load_lanes(packed_ref, (0,), row, *target.shape)
    gain_ref[0] = packed_ref[0, row : row + gain_ref.shape[1], :]


def unpack_weights(packed, part, width):
    shards, amount, _ = packed.shape
    model = shards * part
    return pl.pallas_call(
        unpack_body,
        grid=(shards,),
        in_specs=[pl.BlockSpec((1, amount, LANES), lambda i: (i, 0, 0))],
        out_specs=[pl.BlockSpec((part, width), lambda i: (i, 0))] * 6
        + [pl.BlockSpec((1, GAIN_ROWS, LANES), lambda i: (i, 0, 0))],
        out_shape=[jax.ShapeDtypeStruct((model, width), BF16)] * 6
        + [jax.ShapeDtypeStruct((shards, GAIN_ROWS, LANES), BF16)],
        compiler_params=params(32),
        name="unpack_weights",
    )(packed)


def unpack_scores_body(me_ref, packed_ref, query_ref, keys_ref):
    row = 0
    for unit in range(query_ref.shape[1] // NKEYS):
        span = slice(unit * NKEYS, (unit + 1) * NKEYS)
        query_ref[:, span], row = load_lanes(packed_ref, (0,), row, query_ref.shape[0], NKEYS)
    for unit in range(keys_ref.shape[0]):
        keys_ref[unit], row = load_lanes(packed_ref, (0,), row, keys_ref.shape[1], NKEYS)


def unpack_scores(me, packed, part, units, key_part):
    shards, amount, _ = packed.shape
    return pl.pallas_call(
        unpack_scores_body,
        grid_spec=pltpu.PrefetchScalarGridSpec(
            num_scalar_prefetch=1,
            grid=(shards,),
            in_specs=[pl.BlockSpec((1, amount, LANES), lambda i, me: (i ^ me[0], 0, 0))],
            out_specs=[
                pl.BlockSpec((part, units * NKEYS), lambda i, me: (i, 0)),
                pl.BlockSpec((units, key_part, NKEYS), lambda i, me: (0, i, 0)),
            ],
        ),
        out_shape=[
            jax.ShapeDtypeStruct((shards * part, units * NKEYS), BF16),
            jax.ShapeDtypeStruct((units, shards * key_part, NKEYS), BF16),
        ],
        compiler_params=params(32),
        name="unpack_scores",
    )(me, packed)


def grads_body(me_ref, *refs, pairs, part, units):
    lefts, rights, rest = refs[:pairs], refs[pairs : 2 * pairs], refs[2 * pairs :]
    packed_ref = rest[-1]
    per = LANES // part
    rows = [0] * per
    places = [number ^ (me_ref[0] & (per - 1)) for number in range(per)]
    for left, right in zip(lefts, rights):
        grad = lax.dot_general(left[...], right[...], TN, preferred_element_type=F32).astype(BF16)
        for number in range(per):
            own = grad[number * part : (number + 1) * part]
            rows[number] = store_lanes(packed_ref, (places[number],), rows[number], own)
    if units:
        key_ref = rest[0]
        key_part = key_ref.shape[1] // per
        for number in range(per):
            for unit in range(units):
                own = key_ref[unit, number * key_part : (number + 1) * key_part, :].astype(BF16)
                rows[number] = store_lanes(packed_ref, (places[number],), rows[number], own)


def pack_grads(me, lefts, rights, part, key_grad=None):
    length, model = lefts[0].shape
    shards = model // part
    per = LANES // part
    amount = part * sum(right.shape[1] for right in rights) // LANES
    units = 0
    extra, extra_specs = [], []
    if key_grad is not None:
        units, keys, _ = key_grad.shape
        amount += key_grad.size // shards // LANES
        extra = [key_grad]
        extra_specs = [pl.BlockSpec((units, keys // shards * per, NKEYS), lambda i, me: (0, i, 0))]
    return pl.pallas_call(
        functools.partial(grads_body, pairs=len(lefts), part=part, units=units),
        grid_spec=pltpu.PrefetchScalarGridSpec(
            num_scalar_prefetch=1,
            grid=(shards // per,),
            in_specs=[pl.BlockSpec((length, LANES), lambda i, me: (0, i))] * len(lefts)
            + [pl.BlockSpec(right.shape, lambda i, me: (0, 0)) for right in rights]
            + extra_specs,
            out_specs=pl.BlockSpec((per, amount, LANES), lambda i, me: (i ^ (me[0] // per), 0, 0)),
        ),
        out_shape=jax.ShapeDtypeStruct((shards, amount, LANES), BF16),
        compiler_params=params(48),
        cost_estimate=pl.CostEstimate(
            flops=2 * length * model * sum(right.shape[1] for right in rights),
            bytes_accessed=2 * length * model * len(lefts),
            transcendentals=0,
        ),
        name="pack_grads",
    )(me, *lefts, *rights, *extra)


def unpack_grads_body(
    early_ref, late_ref, qkv_ref, out_ref, mixer_ref, gate_ref, query_ref, keys_ref
):
    part, width = gate_ref.shape
    row = 0
    for j in range(3):
        block, row = load_lanes(late_ref, (), row, part, width)
        qkv_ref[j] = block.astype(F32)
    block, row = load_lanes(late_ref, (), row, part, width)
    out_ref[...] = block.astype(F32).T
    row = 0
    block, row = load_lanes(early_ref, (), row, part, width)
    mixer_ref[...] = block.astype(F32).T
    block, row = load_lanes(early_ref, (), row, part, width)
    gate_ref[...] = block.astype(F32)
    for unit in range(query_ref.shape[0]):
        block, row = load_lanes(early_ref, (), row, part, NKEYS)
        query_ref[unit] = block.astype(F32)
    for unit in range(keys_ref.shape[0]):
        block, row = load_lanes(early_ref, (), row, keys_ref.shape[1], NKEYS)
        keys_ref[unit] = block.astype(F32)


def unpack_grads(early, late, part, width, units, key_part):
    shapes = [
        (3, part, width),
        (width, part),
        (width, part),
        (part, width),
        (units, part, NKEYS),
        (units, key_part, NKEYS),
    ]
    return pl.pallas_call(
        unpack_grads_body,
        out_shape=[jax.ShapeDtypeStruct(shape, F32) for shape in shapes],
        compiler_params=params(32),
        name="unpack_grads",
    )(early, late)


def unit_indices(picks, number):
    return jnp.where(number % 2 == 0, picks >> 8, picks & (NKEYS - 1))


def scores_body(column_ref, picks_ref, query_ref, keys_ref, out_ref, *, units):
    picks = picks_ref[...]
    lanes = lax.broadcasted_iota(jnp.int32, picks.shape, 1)
    total = jnp.zeros(picks.shape, F32)
    for unit in range(units):
        number = column_ref[0] * units + unit
        index = unit_indices(picks, number)
        scores = lax.dot_general(
            query_ref[:, unit * NKEYS : (unit + 1) * NKEYS],
            keys_ref[unit],
            NT,
            preferred_element_type=F32,
        )
        lower = index & (LANES - 1)
        low_part = jnp.take_along_axis(scores[:, :LANES], lower, axis=1)
        high_part = jnp.take_along_axis(scores[:, LANES:], lower, axis=1)
        found = jnp.where(index < LANES, low_part, high_part)
        total = total + jnp.where(lanes // TOPK == number // 2, found, 0.0)
    out_ref[...] = total


def pick_scores(column, picks, queries, keys, rows=256):
    amount = picks.shape[0]
    units = keys.shape[0]
    return pl.pallas_call(
        functools.partial(scores_body, units=units),
        grid=(amount // rows,),
        in_specs=[
            pl.BlockSpec(memory_space=pltpu.SMEM),
            pl.BlockSpec((rows, PICKS), lambda i: (i, 0)),
            pl.BlockSpec((rows, units * NKEYS), lambda i: (i, 0)),
            pl.BlockSpec(keys.shape, lambda i: (0, 0, 0)),
        ],
        out_specs=pl.BlockSpec((rows, PICKS), lambda i: (i, 0)),
        out_shape=jax.ShapeDtypeStruct((amount, PICKS), F32),
        compiler_params=params(32),
        name="pick_scores",
    )(column, picks, queries, keys)


def spread_body(
    column_ref, picks_ref, prob_ref, grad_ref, query_ref, keys_ref, out_ref, sum_ref, held_index,
    held_grad, *, units
):
    rows = picks_ref.shape[0]
    probs = prob_ref[...]
    pick_grad = grad_ref[...]
    centre = over_head(probs * pick_grad, jnp.add)
    held_grad[...] = (probs * (pick_grad - centre)).astype(BF16).astype(F32).T

    @pl.when(pl.program_id(0) == 0)
    def clear():
        sum_ref[...] = jnp.zeros_like(sum_ref)

    key_ids = lax.broadcasted_iota(jnp.int32, (NKEYS, rows), 0)
    for unit in range(units):
        number = column_ref[0] * units + unit
        first = (number // 2) * TOPK
        held_index[...] = unit_indices(picks_ref[...], number).T
        table = jnp.zeros((NKEYS, rows), F32)
        for slot in range(TOPK):
            index = held_index[pl.ds(first + slot, 1), :]
            grad = held_grad[pl.ds(first + slot, 1), :]
            table = table + jnp.where(key_ids == index, grad, 0.0)
        table = table.astype(BF16)
        span = slice(unit * NKEYS, (unit + 1) * NKEYS)
        out_ref[:, span] = lax.dot_general(
            table, keys_ref[unit], TN, preferred_element_type=F32
        ).astype(BF16)
        sum_ref[unit] += jnp.dot(table, query_ref[:, span], preferred_element_type=F32)


def spread_grads(column, picks, probs, grads, queries, keys, rows=128):
    amount = picks.shape[0]
    units = keys.shape[0]
    return pl.pallas_call(
        functools.partial(spread_body, units=units),
        grid=(amount // rows,),
        in_specs=[
            pl.BlockSpec(memory_space=pltpu.SMEM),
            pl.BlockSpec((rows, PICKS), lambda i: (i, 0)),
            pl.BlockSpec((rows, PICKS), lambda i: (i, 0)),
            pl.BlockSpec((rows, PICKS), lambda i: (i, 0)),
            pl.BlockSpec((rows, units * NKEYS), lambda i: (i, 0)),
            pl.BlockSpec(keys.shape, lambda i: (0, 0, 0)),
        ],
        out_specs=[
            pl.BlockSpec((rows, units * NKEYS), lambda i: (i, 0)),
            pl.BlockSpec(keys.shape, lambda i: (0, 0, 0)),
        ],
        out_shape=[
            jax.ShapeDtypeStruct((amount, units * NKEYS), BF16),
            jax.ShapeDtypeStruct(keys.shape, F32),
        ],
        scratch_shapes=[pltpu.VMEM((PICKS, rows), jnp.int32), pltpu.VMEM((PICKS, rows), F32)],
        compiler_params=params(32),
        name="spread_grads",
    )(column, picks, probs, grads, queries, keys)


def swap_narrow(block, bit):
    size = lax.axis_size("narrow")
    return lax.ppermute(block, "narrow", [(i, i ^ bit) for i in range(size)])


def swap_all(held, axis, bit):
    pairs = [(i, i ^ bit) for i in range(lax.axis_size(axis))]
    moved = {offset ^ bit: lax.ppermute(part, axis, pairs) for offset, part in held.items()}
    return {**held, **moved}


def in_order(held, axis):
    me = lax.axis_index(axis)
    size = lax.axis_size(axis)
    stacked = jnp.stack([held[offset] for offset in range(size)])
    return [lax.dynamic_index_in_dim(stacked, me ^ number, 0, False) for number in range(size)]


def gather_by_swaps(block, axis, bits):
    held = {0: block}
    for bit in bits:
        held = swap_all(held, axis, bit)
    return in_order(held, axis)


def sum_by_swaps(block, axis):
    for bit in bits_down(lax.axis_size(axis)):
        block = block + lax.ppermute(
            block, axis, [(i, i ^ bit) for i in range(lax.axis_size(axis))]
        )
    return block


def scatter_narrow(block, after=None):
    size = lax.axis_size("narrow")
    me = lax.axis_index("narrow")
    width = block.shape[1] // size
    parts = jnp.stack([block[:, n * width : (n + 1) * width] for n in range(size)])
    held = [lax.dynamic_index_in_dim(parts, me ^ offset, 0, False) for offset in range(size)]
    for bit in bits_down(size)[::-1]:
        arrived = {
            offset: swap_narrow(held[offset ^ bit].astype(BF16), bit)
            for offset in range(size)
            if not offset & (2 * bit - 1)
        }
        if len(arrived) == 1 and after is not None:
            held[0], _ = lax.optimization_barrier((held[0], after))
        held = {
            offset: held[offset].astype(F32) + value.astype(F32)
            for offset, value in arrived.items()
        }
    return held[0]


def bits_down(size):
    return [1 << level for level in reversed(range(size.bit_length() - 1))]


def send_half(held, axis, bit):
    pairs = [(i, i ^ bit) for i in range(lax.axis_size(axis))]
    sent = jnp.stack([held[offset] for offset in sorted(held) if offset & bit])
    return lax.ppermute(sent.astype(BF16), axis, pairs)


def add_half(held, arrived, bit):
    kept = [offset for offset in sorted(held) if not offset & bit]
    return {
        offset: held[offset].astype(F32) + arrived[place].astype(F32)
        for place, offset in enumerate(kept)
    }


def scatter_both(blocks, cut, axis, other):
    size = lax.axis_size(axis)
    upper = {offset: blocks[offset, :cut] for offset in range(size)}
    lower = {offset: blocks[offset, cut:] for offset in range(size)}
    bits = bits_down(size)
    for step, bit in enumerate(bits):
        back = bits[len(bits) - 1 - step]
        upper_arrived = send_half(upper, axis, back)
        lower_arrived = send_half(lower, axis, bit)
        upper = add_half(upper, upper_arrived, back)
        lower = add_half(lower, lower_arrived, bit)
        if step == 0:
            upper, lower, other = lax.optimization_barrier((upper, lower, other))
    return jnp.concatenate([upper[0], lower[0]], axis=0), other


def gather_narrow(block):
    return jnp.concatenate(
        gather_by_swaps(block, "narrow", bits_down(lax.axis_size("narrow"))), axis=1
    )


def gather_wide(block):
    return lax.all_gather(block, "wide")


def sum_wide(block):
    return lax.psum_scatter(block, "wide", scatter_dimension=0)


def per_device(
    inputs,
    segments,
    attn_gain,
    qkv_weight,
    out_weight,
    memory_gain,
    query_weight,
    sub_keys,
    gate_weight,
    memory_values,
    memory_out,
    picks,
    cotangent,
):
    length, width = inputs.shape
    shards = lax.axis_size("wide")
    column = lax.axis_index("narrow")
    column_ref = column.astype(jnp.int32).reshape(1)
    shard_rows = memory_values.shape[0]
    base = (lax.axis_index("wide") * shard_rows).astype(jnp.int32).reshape(1)
    units = sub_keys.shape[0]
    part = qkv_weight.shape[0]
    model = part * shards
    key_part = sub_keys.shape[1]

    rows_one = gather_narrow(inputs).astype(F32)
    gains = jnp.concatenate([attn_gain, memory_gain]).reshape(-1, LANES)
    gains = jnp.pad(gains, ((0, GAIN_ROWS - gains.shape[0]), (0, 0)))
    packed, scores_packed = pack_weights(
        [
            jnp.transpose(qkv_weight, (1, 0, 2)),
            out_weight,
            memory_out,
            gate_weight,
        ],
        jnp.transpose(query_weight, (1, 0, 2)),
        sub_keys,
        gains,
    )
    packed = gather_wide(packed)
    moving = {0: scores_packed}
    for bit in bits_down(shards):
        moving = swap_all(moving, "wide", bit)
    moving = jnp.stack([moving[offset] for offset in range(shards)])
    table_turned = memory_values.T
    located_own = locate(base, picks, shard_rows)
    packed, moving, table_turned, located_own = lax.optimization_barrier(
        (packed, moving, table_turned, located_own)
    )
    (
        query_matrix, key_matrix, value_matrix, out_turned, mixer_turned, gate_full, gains
    ) = unpack_weights(packed, part, width)
    me_wide = lax.axis_index("wide").astype(jnp.int32).reshape(1)
    query_full, keys_full = unpack_scores(me_wide, moving, part, units, key_part)
    qkv_full = [query_matrix, key_matrix, value_matrix]
    gains = gains.reshape(shards, -1)[:, : 2 * part].reshape(shards, 2, part).astype(F32)
    gain_one = gains[:, 0].reshape(model)
    gain_two = gains[:, 1].reshape(model)
    out_all = gather_narrow(out_turned)
    upstream = gather_narrow(cotangent)
    half = length // 2
    pairs = picks[:half] | (picks[half:] << 16)
    pairs, packed = lax.optimization_barrier((pairs, packed))
    pairs = gather_wide(pairs)
    all_picks = jnp.concatenate([pairs & 0xFFFF, (pairs >> 16) & 0xFFFF], axis=1)
    all_picks = all_picks.reshape(shards * length, PICKS)
    located = locate(base, all_picks, shard_rows)
    where = jnp.concatenate([base, me_wide])

    factor_one, normed = norm_rows(rows_one, gain_one)
    normed = normed.astype(BF16)
    queries, key_rows, value_rows = [
        jnp.dot(normed, qkv_full[j], preferred_element_type=F32).astype(BF16) for j in range(3)
    ]
    starts = document_starts(segments)
    head_rows = attend_forward(starts, queries, key_rows, value_rows)
    head_all = gather_narrow(head_rows)
    hidden = rows_one + lax.dot_general(head_all, out_all, NT, preferred_element_type=F32)
    factor_two, second = norm_rows(hidden, gain_two)
    second = second.astype(BF16)

    gate_value = jnp.dot(second, gate_full, preferred_element_type=F32)
    gate_act = jax.nn.silu(gate_value)
    product_grad = jnp.dot(upstream, mixer_turned, preferred_element_type=F32)
    memory_grad = (product_grad * gate_act).astype(BF16)
    all_grads = gather_wide(memory_grad).reshape(shards * length, width)

    memory_query = jnp.dot(second, query_full, preferred_element_type=F32).astype(BF16)
    own_scores = pick_scores(column_ref, picks, memory_query, keys_full)
    mem_probs, pick_weights = pick_softmax(sum_by_swaps(own_scores, "narrow"))
    pick_weights, memory_grad = lax.optimization_barrier((pick_weights, memory_grad))
    all_weights = gather_wide(pick_weights).reshape(shards * length, PICKS)

    pick_part = picked_products(where, picks, located_own, memory_grad, table_turned, shards)
    pick_part = picked_products(
        where, all_picks, located, all_grads, table_turned, shards, pick_part
    )
    all_weights, pick_part = lax.optimization_barrier((all_weights, pick_part))
    pick_own = sum_wide(pick_part.reshape(shards, length, PICKS)).astype(F32)
    memory_part, tables = bag_sums(base, all_picks, located, all_weights, memory_values)
    memory_part, pick_own = lax.optimization_barrier((memory_part, pick_own))
    memory_own = sum_wide(memory_part.reshape(shards, length, width))
    values_grad = lax.dot_general(tables, all_grads, TN, preferred_element_type=F32)
    memory_own, values_grad = lax.optimization_barrier((memory_own, values_grad))
    memory = memory_own.astype(F32)

    pick_grad = sum_by_swaps(pick_own, "narrow")
    memory_query_grad, key_grad = spread_grads(
        column_ref, picks, mem_probs, pick_grad, memory_query, keys_full
    )

    product = (gate_act * memory).astype(BF16)
    sigmoid = jax.nn.sigmoid(gate_value)
    gate_rows_grad = (
        product_grad * memory * sigmoid * (1.0 + gate_value * (1.0 - sigmoid))
    ).astype(BF16)
    early_pack = pack_grads(
        column_ref * 0,
        [upstream, second, second],
        [product, gate_rows_grad, memory_query_grad],
        part,
        key_grad,
    )
    early_sums = sum_wide(early_pack)
    second_part = lax.dot_general(gate_rows_grad, gate_full, NT, preferred_element_type=F32)
    second_part = second_part + lax.dot_general(
        memory_query_grad, query_full, NT, preferred_element_type=F32
    )
    turned = second_part * gain_two
    inner_part = jnp.sum(turned * hidden, axis=-1)
    gain_two_part = jnp.sum(second_part * hidden * factor_two, axis=0)
    tiny = sum_by_swaps(jnp.concatenate([inner_part, gain_two_part]), "narrow")
    inner_two = tiny[:length, None] / model
    gain_two_part = tiny[length:]
    own_second_grad = scatter_narrow(second_part)

    def own_columns(block):
        return lax.dynamic_slice_in_dim(block, column * width, width, block.ndim - 1)

    own_hidden = own_columns(hidden)
    own_hidden_grad = (
        cotangent.astype(F32)
        + factor_two * own_columns(gain_two) * own_second_grad
        - own_hidden * (factor_two * factor_two * factor_two) * inner_two
    )
    branch_grad = own_hidden_grad.astype(BF16)
    branch_grad, early_pack = lax.optimization_barrier((branch_grad, early_pack))
    branch_grad = gather_narrow(branch_grad)

    heads_grad = jnp.dot(branch_grad, out_turned, preferred_element_type=F32)
    heads_grad = heads_grad.astype(BF16)

    mixed_grad = attend_backward(starts, queries, key_rows, value_rows, heads_grad)
    normed_part = sum(
        lax.dot_general(mixed_grad[j], qkv_full[j], NT, preferred_element_type=F32)
        for j in range(3)
    )
    late_pack = pack_grads(
        me_wide, [normed, normed, normed, branch_grad], [*mixed_grad, head_rows], part
    )
    inner_part = jnp.sum(normed_part * gain_one * rows_one, axis=-1)
    gain_one_part = jnp.sum(normed_part * rows_one * factor_one, axis=0)
    tiny = sum_by_swaps(jnp.concatenate([inner_part, gain_one_part]), "narrow")
    inner_one = tiny[:length, None] / model
    gain_one_part = tiny[length:]
    late_sums, gain_parts = scatter_both(
        late_pack, late_pack.shape[1] * 5 // 8 // 16 * 16, "wide", (gain_one_part, gain_two_part)
    )
    gain_sums = sum_by_swaps(jnp.stack(gain_parts), "wide")
    mixer_part = lax.dot_general(product, mixer_turned, NT, preferred_element_type=F32)
    mixer_part, _ = lax.optimization_barrier((mixer_part, branch_grad))
    outputs = (own_hidden + scatter_narrow(mixer_part, late_sums)).astype(BF16)
    own_normed_grad = scatter_narrow(normed_part, late_sums)
    input_grad = (
        own_hidden_grad
        + factor_one * own_columns(gain_one) * own_normed_grad
        - inputs.astype(F32) * (factor_one * factor_one * factor_one) * inner_one
    )
    gain_sums = lax.dynamic_slice_in_dim(gain_sums, lax.axis_index("wide") * part, part, 1)
    qkv_sum, out_sum, mixer_sum, gate_sum, query_sum, key_sum = unpack_grads(
        early_sums, late_sums, part, width, units, key_part
    )
    return (
        outputs,
        input_grad,
        gain_sums[0],
        jnp.transpose(qkv_sum, (1, 0, 2)),
        out_sum,
        gain_sums[1],
        jnp.transpose(query_sum, (1, 0, 2)),
        key_sum,
        gate_sum,
        values_grad,
        mixer_sum,
    )


def solution(mesh):
    return jax.shard_map(
        per_device,
        mesh=mesh,
        in_specs=(
            P("wide", "narrow"),
            P("wide", None),
            P("wide"),
            P("wide", None, "narrow"),
            P("narrow", "wide"),
            P("wide"),
            P("wide", "narrow", None),
            P("narrow", "wide", None),
            P("wide", "narrow"),
            P("wide", "narrow"),
            P("narrow", "wide"),
            P("wide", None),
            P("wide", "narrow"),
        ),
        out_specs=(
            P("wide", "narrow"),
            P("wide", "narrow"),
            P("wide"),
            P("wide", None, "narrow"),
            P("narrow", "wide"),
            P("wide"),
            P("wide", "narrow", None),
            P("narrow", "wide", None),
            P("wide", "narrow"),
            P("wide", "narrow"),
            P("narrow", "wide"),
        ),
        check_vma=False,
    )
```

```python
import functools

import jax
import jax.numpy as jnp
from jax import lax
from jax.experimental import pallas as pl
from jax.experimental.pallas import tpu as pltpu
from jax.sharding import PartitionSpec as P

HD = 64
PKH = 4
NKEYS = 256
TOPK = 32
PICKS = 128
DOCS = 3
DOC_MOST = 512
LANES = 128
ROWS = 512
GAIN_ROWS = 16
COVER = 1


EPSILON = 1e-06
MASKED = -1e30
BF16 = jnp.bfloat16
F32 = jnp.float32
NT = (((1,), (1,)), ((), ()))
TN = (((0,), (0,)), ((), ()))


def norm_rows(activations, gain_row):
    factor = lax.rsqrt(jnp.mean(activations * activations, axis=-1, keepdims=True) + EPSILON)
    return (factor, activations * factor * gain_row)


def document_starts(segment_row):
    starts = jnp.zeros(segment_row.shape, jnp.int32)
    for number in range(1, DOCS):
        before = jnp.sum((segment_row == number - 1).astype(jnp.int32))
        starts = starts + jnp.where(segment_row >= number, before, 0)
    return starts


def key_window(block, rows):
    first = max(0, (block * rows - (DOC_MOST - 1)) // rows * rows)
    return first, (block + 1) * rows


def head_lanes(shape, head, axis):
    return lax.broadcasted_iota(jnp.int32, shape, axis) // HD == head


def turned_probs(keys, queries, starts, first, offset):
    scores = lax.dot_general(keys, queries, NT, preferred_element_type=F32) * HD ** (-0.5)
    key_ids = lax.broadcasted_iota(jnp.int32, scores.shape, 0) + first
    query_ids = lax.broadcasted_iota(jnp.int32, scores.shape, 1) + offset
    allowed = (key_ids >= starts) & (key_ids <= query_ids)
    scores = jnp.where(allowed, scores, MASKED)
    raised = jnp.exp(scores - jnp.max(scores, axis=0, keepdims=True))
    return raised * (1.0 / jnp.sum(raised, axis=0, keepdims=True))


def attend_body(start_ref, query_ref, key_ref, value_ref, out_ref, *, rows):
    length = query_ref.shape[0]
    values_turned = value_ref[...].T
    for block in range(length // rows):
        first, last = key_window(block, rows)
        span = slice(block * rows, last)
        queries = query_ref[span, :]
        mixture = jnp.zeros((LANES, rows), F32)
        for head in range(LANES // HD):
            own = jnp.where(head_lanes(queries.shape, head, 1), queries, jnp.zeros((), BF16))
            probs = turned_probs(
                key_ref[first:last, :], own, start_ref[:, span], first, block * rows
            )
            part = jnp.dot(
                values_turned[:, first:last], probs.astype(BF16), preferred_element_type=F32
            )
            mixture = jnp.where(head_lanes(part.shape, head, 0), part, mixture)
        out_ref[span, :] = mixture.T.astype(BF16)


def attend_forward(starts, queries, key_rows, value_rows, rows=256):
    length, width = queries.shape
    column = pl.BlockSpec((length, LANES), lambda i: (0, i))
    return pl.pallas_call(
        functools.partial(attend_body, rows=rows),
        grid=(width // LANES,),
        in_specs=[pl.BlockSpec((1, length), lambda i: (0, 0)), column, column, column],
        out_specs=column,
        out_shape=jax.ShapeDtypeStruct((length, width), BF16),
        compiler_params=params(32),
        cost_estimate=pl.CostEstimate(
            flops=16 * length * length * width, bytes_accessed=8 * length * width, transcendentals=0
        ),
        name="attend_forward",
    )(starts, queries, key_rows, value_rows)


def attend_back_body(
    start_ref, query_ref, key_ref, value_ref, grad_ref, dq_ref, dk_ref, dv_ref, key_sum, value_sum,
    *, rows
):
    length = query_ref.shape[0]
    keys_turned = key_ref[...].T
    key_sum[...] = jnp.zeros_like(key_sum)
    value_sum[...] = jnp.zeros_like(value_sum)
    zero = jnp.zeros((), BF16)
    factor = HD ** (-0.5)
    for block in range(length // rows):
        first, last = key_window(block, rows)
        span = slice(block * rows, last)
        window = slice(first, last)
        queries = query_ref[span, :]
        grads = grad_ref[span, :]
        query_sum = jnp.zeros((LANES, rows), F32)
        for head in range(LANES // HD):
            mask = head_lanes(queries.shape, head, 1)
            own = jnp.where(mask, queries, zero)
            own_grads = jnp.where(mask, grads, zero)
            probs = turned_probs(key_ref[window, :], own, start_ref[:, span], first, block * rows)
            prob_grad = lax.dot_general(
                value_ref[window, :], own_grads, NT, preferred_element_type=F32
            )
            centre = jnp.sum(probs * prob_grad, axis=0, keepdims=True)
            score_grad = (probs * (prob_grad - centre)).astype(BF16)
            part = jnp.dot(keys_turned[:, window], score_grad, preferred_element_type=F32)
            query_sum = jnp.where(head_lanes(part.shape, head, 0), part, query_sum)
            key_sum[window, :] += jnp.dot(score_grad, own, preferred_element_type=F32)
            value_sum[window, :] += jnp.dot(
                probs.astype(BF16), own_grads, preferred_element_type=F32
            )
        dq_ref[span, :] = (query_sum.T * factor).astype(BF16)
    dk_ref[...] = (key_sum[...] * factor).astype(BF16)
    dv_ref[...] = value_sum[...].astype(BF16)


def attend_backward(starts, queries, key_rows, value_rows, heads_grad, rows=256):
    length, width = queries.shape
    column = pl.BlockSpec((length, LANES), lambda i: (0, i))
    return pl.pallas_call(
        functools.partial(attend_back_body, rows=rows),
        grid=(width // LANES,),
        in_specs=[pl.BlockSpec((1, length), lambda i: (0, 0))] + [column] * 4,
        out_specs=[column] * 3,
        out_shape=[jax.ShapeDtypeStruct((length, width), BF16)] * 3,
        scratch_shapes=[pltpu.VMEM((length, LANES), F32)] * 2,
        compiler_params=params(40),
        cost_estimate=pl.CostEstimate(
            flops=COVER * length * length * width,
            bytes_accessed=14 * length * width,
            transcendentals=0,
        ),
        name="attend_backward",
    )(starts, queries, key_rows, value_rows, heads_grad)


SLOTS = 32


def params(mib):
    return pltpu.CompilerParams(vmem_limit_bytes=mib << 20)


def lane_numbers(shape):
    return lax.broadcasted_iota(jnp.int32, shape, len(shape) - 1)


def count_local(local, total):
    inside = (local >= 0) & (local < total)
    square = (LANES, LANES)
    upto = lax.broadcasted_iota(jnp.int32, square, 0) <= lax.broadcasted_iota(jnp.int32, square, 1)
    return jnp.dot(
        jnp.where(inside, 1.0, 0.0).astype(BF16),
        jnp.where(upto, 1.0, 0.0).astype(BF16),
        preferred_element_type=F32,
    )


def rounds_of(counts):
    most = jnp.max(counts[:, LANES - 1 :]).astype(jnp.int32)
    return (most + (SLOTS - 1)) // SLOTS


def search(counts, start):
    target = ((lane_numbers(counts.shape) & (SLOTS - 1)) + (start + 1)).astype(F32)
    place = jnp.zeros(counts.shape, jnp.int32)
    step = LANES // 2
    while step:
        seen = jnp.take_along_axis(counts, place + (step - 1), axis=1)
        place = jnp.where(seen < target, place + step, place)
        step //= 2
    return target <= counts[:, LANES - 1 :], place


def place_of(counts, local, number):
    valid, place = search(counts, number * SLOTS)
    return place, jnp.where(valid, jnp.take_along_axis(local, place, axis=1), -1)


def locate_body(base_ref, picks_ref, out_ref, *, total):
    local = picks_ref[...] - base_ref[0]
    counts = count_local(local, total)
    valid, place = search(counts, 0)
    found = jnp.where(valid, jnp.take_along_axis(local, place, axis=1) + 1, 0)
    inside = jnp.where((local >= 0) & (local < total), 1, 0)
    out_ref[...] = found | (place << 16) | (counts.astype(jnp.int32) << 23) | (inside << 31)


def found_in(located):
    return (located & 0xFFFF) - 1


def place_in(located):
    return (located >> 16) & (LANES - 1)


def count_in(located):
    return (located >> 23) & (2 * LANES - 1)


def locate(base, picks, total, rows=512):
    block = pl.BlockSpec((rows, PICKS), lambda i: (i, 0))
    amount = picks.shape[0]
    return pl.pallas_call(
        functools.partial(locate_body, total=total),
        grid=(amount // rows,),
        in_specs=[pl.BlockSpec(memory_space=pltpu.SMEM), block],
        out_specs=block,
        out_shape=pltpu.HBM((amount, PICKS), jnp.int32),
        compiler_params=params(32),
        cost_estimate=pl.CostEstimate(
            flops=amount * PICKS * 20000, bytes_accessed=amount * PICKS * 16, transcendentals=0
        ),
        name="locate",
    )(base, picks)


def group_masks():
    own = lax.broadcasted_iota(jnp.int32, (8, LANES), 0)
    lane = lane_numbers((8, LANES)) // SLOTS
    per = LANES // SLOTS
    return [own == lane + per * block for block in range(8 // per)]


def lane_table(low, masks):
    ids = lax.broadcasted_iota(jnp.int32, (NKEYS, LANES), 0).astype(F32).astype(BF16)
    parts = []
    for mask in masks:
        row = jnp.sum(jnp.where(mask, low, 0.0), axis=0, keepdims=True)
        row = jnp.broadcast_to(row, (16, LANES)).astype(BF16)
        row = jnp.concatenate([row] * (NKEYS // 16), axis=0)
        parts.append(jnp.where(ids == row, jnp.ones((), BF16), jnp.zeros((), BF16)))
    return jnp.concatenate(parts, axis=1)


def token_places(picks, shards, before):
    own = before is None
    length = picks.shape[0] if own else picks.shape[0] // shards
    blocks = length // ROWS

    def place(i, where):
        shard = where[1] if own else lax.rem(where[1] + 1 + i // blocks, shards)
        return (shard * blocks + i % blocks, 0)

    block = pl.BlockSpec((ROWS, PICKS), (lambda i, where: (i, 0)) if own else place)
    return (blocks if own else (shards - 1) * blocks), block, place, length


def bag_body(
    base_ref, picks_ref, located_ref, weight_ref, table_ref, out_ref, keep_ref, high, low, weights,
    *, chunk, unroll
):
    rows = picks_ref.shape[0]
    total = table_ref.shape[0]
    groups = total // NKEYS
    masks = group_masks()

    def eight(token):
        span = pl.ds(token, 8)
        own_high = high[span, :]
        weight = weights[span, :]
        weight = jnp.concatenate([weight, weight], axis=0).astype(BF16)
        zero = jnp.zeros((), BF16)
        parts = []
        for mask in masks:
            own = jnp.where(mask, own_high, -1.0)
            pair = jnp.concatenate([own, own - 1.0], axis=0).astype(BF16)
            rows_of = [
                jnp.where(pair == jnp.array(group, BF16), weight, zero)
                for group in range(0, groups, 2)
            ]
            parts.append(jnp.concatenate(rows_of, axis=0))
        return lax.dot_general(
            jnp.concatenate(parts, axis=1),
            lane_table(low[span, :], masks),
            NT,
            preferred_element_type=F32,
        )

    def one_round(place, found, first):
        high[...] = (found >> 8).astype(F32)
        low[...] = (found & (NKEYS - 1)).astype(F32)
        weights[...] = jnp.take_along_axis(weight_ref[...].astype(F32), place, axis=1)

        def some_tokens(step, carried):
            for slot in range(unroll):
                token = pl.multiple_of((step * unroll + slot) * 16, 16)
                top = eight(token)
                bottom = eight(token + 8)
                for group in range(groups):
                    part = slice(group * 8, group * 8 + 8)
                    block = jnp.concatenate([top[part], bottom[part]], axis=0).astype(BF16)
                    span = (pl.ds(token, 16), slice(group * NKEYS, (group + 1) * NKEYS))
                    keep_ref[span] = block if first else keep_ref[span] + block
            return carried

        lax.fori_loop(0, rows // (16 * unroll), some_tokens, 0)

    def more(number, carried):
        local = picks_ref[...] - base_ref[0]
        one_round(*place_of(counts, local, number), False)
        return carried

    located = located_ref[...]
    counts = count_in(located).astype(F32)
    one_round(place_in(located), found_in(located), True)
    lax.fori_loop(1, rounds_of(counts), more, 0)
    result = jnp.zeros(out_ref.shape, F32)
    for start in range(0, total, chunk):
        result = result + jnp.dot(
            keep_ref[:, pl.ds(start, chunk)],
            table_ref[pl.ds(start, chunk), :],
            preferred_element_type=F32,
        )
    out_ref[...] = result.astype(out_ref.dtype)


def bag_sums(base, picks, located, weights, table, chunk=1024, unroll=32):
    amount = picks.shape[0]
    total, width = table.shape
    block = pl.BlockSpec((ROWS, PICKS), lambda i: (i, 0))
    return pl.pallas_call(
        functools.partial(bag_body, chunk=chunk, unroll=unroll),
        grid=(amount // ROWS,),
        in_specs=[pl.BlockSpec(memory_space=pltpu.SMEM)]
        + [block] * 3
        + [pl.BlockSpec((total, width), lambda i: (0, 0))],
        out_specs=[
            pl.BlockSpec((ROWS, width), lambda i: (i, 0)),
            pl.BlockSpec((ROWS, total), lambda i: (i, 0)),
        ],
        out_shape=[
            jax.ShapeDtypeStruct((amount, width), BF16),
            jax.ShapeDtypeStruct((amount, total), BF16),
        ],
        scratch_shapes=[pltpu.VMEM((ROWS, LANES), F32)] * 3,
        compiler_params=params(56),
        cost_estimate=pl.CostEstimate(
            flops=9 * amount * total * width, bytes_accessed=amount * total * 2, transcendentals=0
        ),
        name="bag_sums",
    )(base, picks, located, weights, table)


def picked_body(
    base_ref, picks_ref, located_ref, grad_ref, table_ref, *rest, unroll
):
    out_ref, high, low, found_at, held = rest[-5:]
    rows = picks_ref.shape[0]
    total = table_ref.shape[1]
    groups = total // NKEYS
    masks = group_masks()
    located = located_ref[...]
    grads = grad_ref[...]
    for group in range(groups):
        held[group] = jnp.dot(
            grads,
            table_ref[:, group * NKEYS : (group + 1) * NKEYS],
            preferred_element_type=F32,
        )

    def eight(token):
        span = pl.ds(token, 8)
        left = jnp.concatenate([held[group, span, :] for group in range(groups)], axis=0)
        seen = jnp.dot(
            left.astype(BF16), lane_table(low[span, :], masks), preferred_element_type=F32
        )
        own_high = high[span, :]
        result = jnp.zeros((8, LANES), F32)
        for block, mask in enumerate(masks):
            own = jnp.where(mask, own_high, -1.0)
            for group in range(groups):
                part = seen[group * 8 : group * 8 + 8, block * LANES : (block + 1) * LANES]
                result = jnp.where(own == float(group), part, result)
        found_at[span, :] = result

    def one_round(number, found, first):
        high[...] = (found >> 8).astype(F32)
        low[...] = (found & (NKEYS - 1)).astype(F32)

        def some_tokens(step, carried):
            for slot in range(unroll):
                eight(pl.multiple_of((step * unroll + slot) * 8, 8))
            return carried

        lax.fori_loop(0, rows // (8 * unroll), some_tokens, 0)
        slot = count_in(located) - (1 + number * SLOTS)
        here = (slot >= 0) & (slot < SLOTS) & (located < 0)
        token = lax.broadcasted_iota(jnp.int32, slot.shape, 0) & (LANES // SLOTS - 1)
        lane = token * SLOTS + jnp.clip(slot, 0, SLOTS - 1)
        value = jnp.take_along_axis(found_at[...], lane, axis=1)
        before = jnp.zeros(value.shape, F32) if first else out_ref[...].astype(F32)
        out_ref[...] = jnp.where(here, value, before).astype(out_ref.dtype)

    def more(number, carried):
        local = picks_ref[...] - base_ref[0]
        one_round(number, place_of(counts, local, number)[1], False)
        return carried

    counts = count_in(located).astype(F32)
    one_round(0, found_in(located), True)
    lax.fori_loop(1, rounds_of(counts), more, 0)


def picked_products(where, picks, located, grads, table, shards, before=None, unroll=64):
    width, total = table.shape
    count, block, place, length = token_places(picks, shards, before)
    grad_map = block.index_map
    return pl.pallas_call(
        functools.partial(picked_body, unroll=unroll),
        grid_spec=pltpu.PrefetchScalarGridSpec(
            num_scalar_prefetch=1,
            grid=(count,),
            in_specs=[block] * 2
            + [
                pl.BlockSpec((ROWS, width), grad_map),
                pl.BlockSpec((width, total), lambda i, where: (0, 0)),
            ]
            + [pl.BlockSpec(memory_space=pl.ANY)] * (0 if before is None else 1),
            out_specs=pl.BlockSpec((ROWS, PICKS), place),
            scratch_shapes=[pltpu.VMEM((ROWS, LANES), F32)] * 3
            + [pltpu.VMEM((total // NKEYS, ROWS, NKEYS), F32)],
        ),
        out_shape=jax.ShapeDtypeStruct((length * shards, PICKS), BF16),
        input_output_aliases={} if before is None else {5: 0},
        compiler_params=params(56),
        cost_estimate=pl.CostEstimate(
            flops=7 * count * ROWS * total * width,
            bytes_accessed=count * ROWS * width * 4,
            transcendentals=0,
        ),
        name="picked_products",
    )(where, picks, located, grads, table, *(() if before is None else (before,)))


def gather_lanes(block, index):
    return jnp.take_along_axis(block, index, axis=1)


def over_head(block, merge):
    lanes = lane_numbers(block.shape)
    step = 1
    while step < TOPK:
        block = merge(block, gather_lanes(block, lanes ^ step))
        step *= 2
    return block


def softmax_body(score_ref, prob_ref, weight_ref):
    scores = score_ref[...]
    raised = jnp.exp(scores - over_head(scores, jnp.maximum))
    probs = raised / over_head(raised, jnp.add)
    prob_ref[...] = probs
    weight_ref[...] = probs.astype(BF16)


def pick_softmax(scores, rows=256):
    block = pl.BlockSpec((rows, PICKS), lambda i: (i, 0))
    amount = scores.shape[0]
    return pl.pallas_call(
        softmax_body,
        grid=(amount // rows,),
        in_specs=[block],
        out_specs=[block] * 2,
        out_shape=[
            jax.ShapeDtypeStruct((amount, PICKS), F32),
            jax.ShapeDtypeStruct((amount, PICKS), BF16),
        ],
        compiler_params=params(32),
        name="pick_softmax",
    )(scores)


def store_lanes(out_ref, lead, row, block):
    rows, columns = block.shape
    for start in range(0, columns, LANES):
        out_ref[(*lead, slice(row, row + rows), slice(None))] = block[:, start : start + LANES]
        row += rows
    return row


def load_lanes(ref, lead, row, rows, columns):
    parts = []
    for _ in range(columns // LANES):
        parts.append(ref[(*lead, slice(row, row + rows), slice(None))])
        row += rows
    return jnp.concatenate(parts, axis=1), row


def pack_body(
    qkv_ref, out_ref, mixer_ref, gate_ref, query_ref, keys_ref, gain_ref, packed_ref, scores_ref
):
    row = 0
    for j in range(3):
        row = store_lanes(packed_ref, (), row, qkv_ref[j])
    row = store_lanes(packed_ref, (), row, out_ref[...].T)
    row = store_lanes(packed_ref, (), row, mixer_ref[...].T)
    row = store_lanes(packed_ref, (), row, gate_ref[...])
    store_lanes(packed_ref, (), row, gain_ref[...])
    row = 0
    for unit in range(query_ref.shape[0]):
        row = store_lanes(scores_ref, (), row, query_ref[unit])
    for unit in range(keys_ref.shape[0]):
        row = store_lanes(scores_ref, (), row, keys_ref[unit])


def pack_weights(blocks, query, keys, gains):
    first = sum(block.size for block in [*blocks, gains]) // LANES
    second = (query.size + keys.size) // LANES
    return pl.pallas_call(
        pack_body,
        out_shape=[
            jax.ShapeDtypeStruct((first, LANES), BF16),
            jax.ShapeDtypeStruct((second, LANES), BF16),
        ],
        compiler_params=params(32),
        name="pack_weights",
    )(*blocks, query, keys, gains)


def unpack_body(packed_ref, q_ref, k_ref, v_ref, out_ref, mixer_ref, gate_ref, gain_ref):
    row = 0
    for target in (q_ref, k_ref, v_ref, out_ref, mixer_ref, gate_ref):
        target[...], row = load_lanes(packed_ref, (0,), row, *target.shape)
    gain_ref[0] = packed_ref[0, row : row + gain_ref.shape[1], :]


def unpack_weights(packed, part, width):
    shards, amount, _ = packed.shape
    model = shards * part
    return pl.pallas_call(
        unpack_body,
        grid=(shards,),
        in_specs=[pl.BlockSpec((1, amount, LANES), lambda i: (i, 0, 0))],
        out_specs=[pl.BlockSpec((part, width), lambda i: (i, 0))] * 6
        + [pl.BlockSpec((1, GAIN_ROWS, LANES), lambda i: (i, 0, 0))],
        out_shape=[jax.ShapeDtypeStruct((model, width), BF16)] * 6
        + [jax.ShapeDtypeStruct((shards, GAIN_ROWS, LANES), BF16)],
        compiler_params=params(32),
        name="unpack_weights",
    )(packed)


def unpack_scores_body(me_ref, packed_ref, query_ref, keys_ref):
    row = 0
    for unit in range(query_ref.shape[1] // NKEYS):
        span = slice(unit * NKEYS, (unit + 1) * NKEYS)
        query_ref[:, span], row = load_lanes(packed_ref, (0,), row, query_ref.shape[0], NKEYS)
    for unit in range(keys_ref.shape[0]):
        keys_ref[unit], row = load_lanes(packed_ref, (0,), row, keys_ref.shape[1], NKEYS)


def unpack_scores(me, packed, part, units, key_part):
    shards, amount, _ = packed.shape
    return pl.pallas_call(
        unpack_scores_body,
        grid_spec=pltpu.PrefetchScalarGridSpec(
            num_scalar_prefetch=1,
            grid=(shards,),
            in_specs=[pl.BlockSpec((1, amount, LANES), lambda i, me: (i ^ me[0], 0, 0))],
            out_specs=[
                pl.BlockSpec((part, units * NKEYS), lambda i, me: (i, 0)),
                pl.BlockSpec((units, key_part, NKEYS), lambda i, me: (0, i, 0)),
            ],
        ),
        out_shape=[
            jax.ShapeDtypeStruct((shards * part, units * NKEYS), BF16),
            jax.ShapeDtypeStruct((units, shards * key_part, NKEYS), BF16),
        ],
        compiler_params=params(32),
        name="unpack_scores",
    )(me, packed)


def grads_body(me_ref, *refs, pairs, part, units):
    lefts, rights, rest = refs[:pairs], refs[pairs : 2 * pairs], refs[2 * pairs :]
    packed_ref = rest[-1]
    per = LANES // part
    rows = [0] * per
    places = [number ^ (me_ref[0] & (per - 1)) for number in range(per)]
    for left, right in zip(lefts, rights):
        grad = lax.dot_general(left[...], right[...], TN, preferred_element_type=F32).astype(BF16)
        for number in range(per):
            own = grad[number * part : (number + 1) * part]
            rows[number] = store_lanes(packed_ref, (places[number],), rows[number], own)
    if units:
        key_ref = rest[0]
        key_part = key_ref.shape[1] // per
        for number in range(per):
            for unit in range(units):
                own = key_ref[unit, number * key_part : (number + 1) * key_part, :].astype(BF16)
                rows[number] = store_lanes(packed_ref, (places[number],), rows[number], own)


def pack_grads(me, lefts, rights, part, key_grad=None):
    length, model = lefts[0].shape
    shards = model // part
    per = LANES // part
    amount = part * sum(right.shape[1] for right in rights) // LANES
    units = 0
    extra, extra_specs = [], []
    if key_grad is not None:
        units, keys, _ = key_grad.shape
        amount += key_grad.size // shards // LANES
        extra = [key_grad]
        extra_specs = [pl.BlockSpec((units, keys // shards * per, NKEYS), lambda i, me: (0, i, 0))]
    return pl.pallas_call(
        functools.partial(grads_body, pairs=len(lefts), part=part, units=units),
        grid_spec=pltpu.PrefetchScalarGridSpec(
            num_scalar_prefetch=1,
            grid=(shards // per,),
            in_specs=[pl.BlockSpec((length, LANES), lambda i, me: (0, i))] * len(lefts)
            + [pl.BlockSpec(right.shape, lambda i, me: (0, 0)) for right in rights]
            + extra_specs,
            out_specs=pl.BlockSpec((per, amount, LANES), lambda i, me: (i ^ (me[0] // per), 0, 0)),
        ),
        out_shape=jax.ShapeDtypeStruct((shards, amount, LANES), BF16),
        compiler_params=params(48),
        cost_estimate=pl.CostEstimate(
            flops=2 * length * model * sum(right.shape[1] for right in rights),
            bytes_accessed=2 * length * model * len(lefts),
            transcendentals=0,
        ),
        name="pack_grads",
    )(me, *lefts, *rights, *extra)


def unpack_grads_body(
    early_ref, late_ref, qkv_ref, out_ref, mixer_ref, gate_ref, query_ref, keys_ref
):
    part, width = gate_ref.shape
    row = 0
    for j in range(3):
        block, row = load_lanes(late_ref, (), row, part, width)
        qkv_ref[j] = block.astype(F32)
    block, row = load_lanes(late_ref, (), row, part, width)
    out_ref[...] = block.astype(F32).T
    row = 0
    block, row = load_lanes(early_ref, (), row, part, width)
    mixer_ref[...] = block.astype(F32).T
    block, row = load_lanes(early_ref, (), row, part, width)
    gate_ref[...] = block.astype(F32)
    for unit in range(query_ref.shape[0]):
        block, row = load_lanes(early_ref, (), row, part, NKEYS)
        query_ref[unit] = block.astype(F32)
    for unit in range(keys_ref.shape[0]):
        block, row = load_lanes(early_ref, (), row, keys_ref.shape[1], NKEYS)
        keys_ref[unit] = block.astype(F32)


def unpack_grads(early, late, part, width, units, key_part):
    shapes = [
        (3, part, width),
        (width, part),
        (width, part),
        (part, width),
        (units, part, NKEYS),
        (units, key_part, NKEYS),
    ]
    return pl.pallas_call(
        unpack_grads_body,
        out_shape=[jax.ShapeDtypeStruct(shape, F32) for shape in shapes],
        compiler_params=params(32),
        name="unpack_grads",
    )(early, late)


def unit_indices(picks, number):
    return jnp.where(number % 2 == 0, picks >> 8, picks & (NKEYS - 1))


def scores_body(column_ref, picks_ref, query_ref, keys_ref, out_ref, *, units):
    picks = picks_ref[...]
    lanes = lax.broadcasted_iota(jnp.int32, picks.shape, 1)
    total = jnp.zeros(picks.shape, F32)
    for unit in range(units):
        number = column_ref[0] * units + unit
        index = unit_indices(picks, number)
        scores = lax.dot_general(
            query_ref[:, unit * NKEYS : (unit + 1) * NKEYS],
            keys_ref[unit],
            NT,
            preferred_element_type=F32,
        )
        lower = index & (LANES - 1)
        low_part = jnp.take_along_axis(scores[:, :LANES], lower, axis=1)
        high_part = jnp.take_along_axis(scores[:, LANES:], lower, axis=1)
        found = jnp.where(index < LANES, low_part, high_part)
        total = total + jnp.where(lanes // TOPK == number // 2, found, 0.0)
    out_ref[...] = total


def pick_scores(column, picks, queries, keys, rows=256):
    amount = picks.shape[0]
    units = keys.shape[0]
    return pl.pallas_call(
        functools.partial(scores_body, units=units),
        grid=(amount // rows,),
        in_specs=[
            pl.BlockSpec(memory_space=pltpu.SMEM),
            pl.BlockSpec((rows, PICKS), lambda i: (i, 0)),
            pl.BlockSpec((rows, units * NKEYS), lambda i: (i, 0)),
            pl.BlockSpec(keys.shape, lambda i: (0, 0, 0)),
        ],
        out_specs=pl.BlockSpec((rows, PICKS), lambda i: (i, 0)),
        out_shape=jax.ShapeDtypeStruct((amount, PICKS), F32),
        compiler_params=params(32),
        name="pick_scores",
    )(column, picks, queries, keys)


def spread_body(
    column_ref, picks_ref, prob_ref, grad_ref, query_ref, keys_ref, out_ref, sum_ref, held_index,
    held_grad, *, units
):
    rows = picks_ref.shape[0]
    probs = prob_ref[...]
    pick_grad = grad_ref[...]
    centre = over_head(probs * pick_grad, jnp.add)
    held_grad[...] = (probs * (pick_grad - centre)).astype(BF16).astype(F32).T

    @pl.when(pl.program_id(0) == 0)
    def clear():
        sum_ref[...] = jnp.zeros_like(sum_ref)

    key_ids = lax.broadcasted_iota(jnp.int32, (NKEYS, rows), 0)
    for unit in range(units):
        number = column_ref[0] * units + unit
        first = (number // 2) * TOPK
        held_index[...] = unit_indices(picks_ref[...], number).T
        table = jnp.zeros((NKEYS, rows), F32)
        for slot in range(TOPK):
            index = held_index[pl.ds(first + slot, 1), :]
            grad = held_grad[pl.ds(first + slot, 1), :]
            table = table + jnp.where(key_ids == index, grad, 0.0)
        table = table.astype(BF16)
        span = slice(unit * NKEYS, (unit + 1) * NKEYS)
        out_ref[:, span] = lax.dot_general(
            table, keys_ref[unit], TN, preferred_element_type=F32
        ).astype(BF16)
        sum_ref[unit] += jnp.dot(table, query_ref[:, span], preferred_element_type=F32)


def spread_grads(column, picks, probs, grads, queries, keys, rows=128):
    amount = picks.shape[0]
    units = keys.shape[0]
    return pl.pallas_call(
        functools.partial(spread_body, units=units),
        grid=(amount // rows,),
        in_specs=[
            pl.BlockSpec(memory_space=pltpu.SMEM),
            pl.BlockSpec((rows, PICKS), lambda i: (i, 0)),
            pl.BlockSpec((rows, PICKS), lambda i: (i, 0)),
            pl.BlockSpec((rows, PICKS), lambda i: (i, 0)),
            pl.BlockSpec((rows, units * NKEYS), lambda i: (i, 0)),
            pl.BlockSpec(keys.shape, lambda i: (0, 0, 0)),
        ],
        out_specs=[
            pl.BlockSpec((rows, units * NKEYS), lambda i: (i, 0)),
            pl.BlockSpec(keys.shape, lambda i: (0, 0, 0)),
        ],
        out_shape=[
            jax.ShapeDtypeStruct((amount, units * NKEYS), BF16),
            jax.ShapeDtypeStruct(keys.shape, F32),
        ],
        scratch_shapes=[pltpu.VMEM((PICKS, rows), jnp.int32), pltpu.VMEM((PICKS, rows), F32)],
        compiler_params=params(32),
        name="spread_grads",
    )(column, picks, probs, grads, queries, keys)


def swap_narrow(block, bit):
    size = lax.axis_size("narrow")
    return lax.ppermute(block, "narrow", [(i, i ^ bit) for i in range(size)])


def swap_all(held, axis, bit):
    pairs = [(i, i ^ bit) for i in range(lax.axis_size(axis))]
    moved = {offset ^ bit: lax.ppermute(part, axis, pairs) for offset, part in held.items()}
    return {**held, **moved}


def in_order(held, axis):
    me = lax.axis_index(axis)
    size = lax.axis_size(axis)
    stacked = jnp.stack([held[offset] for offset in range(size)])
    return [lax.dynamic_index_in_dim(stacked, me ^ number, 0, False) for number in range(size)]


def gather_by_swaps(block, axis, bits):
    held = {0: block}
    for bit in bits:
        held = swap_all(held, axis, bit)
    return in_order(held, axis)


def sum_by_swaps(block, axis):
    for bit in bits_down(lax.axis_size(axis)):
        block = block + lax.ppermute(
            block, axis, [(i, i ^ bit) for i in range(lax.axis_size(axis))]
        )
    return block


def scatter_narrow(block, after=None):
    size = lax.axis_size("narrow")
    me = lax.axis_index("narrow")
    width = block.shape[1] // size
    block = block.astype(BF16)
    parts = jnp.stack([block[:, n * width : (n + 1) * width] for n in range(size)])
    held = [lax.dynamic_index_in_dim(parts, me ^ offset, 0, False) for offset in range(size)]
    for bit in bits_down(size)[::-1]:
        arrived = {
            offset: swap_narrow(held[offset ^ bit].astype(BF16), bit)
            for offset in range(size)
            if not offset & (2 * bit - 1)
        }
        if len(arrived) == 1 and after is not None:
            held[0], _ = lax.optimization_barrier((held[0], after))
        held = {
            offset: held[offset].astype(F32) + value.astype(F32)
            for offset, value in arrived.items()
        }
    return held[0]


def bits_down(size):
    return [1 << level for level in reversed(range(size.bit_length() - 1))]


def send_half(held, axis, bit):
    pairs = [(i, i ^ bit) for i in range(lax.axis_size(axis))]
    sent = jnp.stack([held[offset] for offset in sorted(held) if offset & bit])
    return lax.ppermute(sent.astype(BF16), axis, pairs)


def add_half(held, arrived, bit):
    kept = [offset for offset in sorted(held) if not offset & bit]
    return {
        offset: held[offset].astype(F32) + arrived[place].astype(F32)
        for place, offset in enumerate(kept)
    }


def scatter_both(blocks, cut, axis, other):
    size = lax.axis_size(axis)
    upper = {offset: blocks[offset, :cut] for offset in range(size)}
    lower = {offset: blocks[offset, cut:] for offset in range(size)}
    bits = bits_down(size)
    for step, bit in enumerate(bits):
        back = bits[len(bits) - 1 - step]
        upper_arrived = send_half(upper, axis, back)
        lower_arrived = send_half(lower, axis, bit)
        upper = add_half(upper, upper_arrived, back)
        lower = add_half(lower, lower_arrived, bit)
        if step == 0:
            upper, lower, other = lax.optimization_barrier((upper, lower, other))
    return jnp.concatenate([upper[0], lower[0]], axis=0), other


def gather_narrow(block):
    return jnp.concatenate(
        gather_by_swaps(block, "narrow", bits_down(lax.axis_size("narrow"))), axis=1
    )


def gather_wide(block):
    return lax.all_gather(block, "wide")


def sum_wide(block):
    return lax.psum_scatter(block, "wide", scatter_dimension=0)


def per_device(
    inputs,
    segments,
    attn_gain,
    qkv_weight,
    out_weight,
    memory_gain,
    query_weight,
    sub_keys,
    gate_weight,
    memory_values,
    memory_out,
    picks,
    cotangent,
):
    length, width = inputs.shape
    shards = lax.axis_size("wide")
    column = lax.axis_index("narrow")
    column_ref = column.astype(jnp.int32).reshape(1)
    shard_rows = memory_values.shape[0]
    base = (lax.axis_index("wide") * shard_rows).astype(jnp.int32).reshape(1)
    units = sub_keys.shape[0]
    part = qkv_weight.shape[0]
    model = part * shards
    key_part = sub_keys.shape[1]

    rows_one = gather_narrow(inputs).astype(F32)
    gains = jnp.concatenate([attn_gain, memory_gain]).reshape(-1, LANES)
    gains = jnp.pad(gains, ((0, GAIN_ROWS - gains.shape[0]), (0, 0)))
    packed, scores_packed = pack_weights(
        [
            jnp.transpose(qkv_weight, (1, 0, 2)),
            out_weight,
            memory_out,
            gate_weight,
        ],
        jnp.transpose(query_weight, (1, 0, 2)),
        sub_keys,
        gains,
    )
    packed = gather_wide(packed)
    moving = {0: scores_packed}
    for bit in bits_down(shards):
        moving = swap_all(moving, "wide", bit)
    moving = jnp.stack([moving[offset] for offset in range(shards)])
    table_turned = memory_values.T
    located_own = locate(base, picks, shard_rows)
    packed, moving, table_turned, located_own = lax.optimization_barrier(
        (packed, moving, table_turned, located_own)
    )
    (
        query_matrix, key_matrix, value_matrix, out_turned, mixer_turned, gate_full, gains
    ) = unpack_weights(packed, part, width)
    me_wide = lax.axis_index("wide").astype(jnp.int32).reshape(1)
    query_full, keys_full = unpack_scores(me_wide, moving, part, units, key_part)
    qkv_full = [query_matrix, key_matrix, value_matrix]
    gains = gains.reshape(shards, -1)[:, : 2 * part].reshape(shards, 2, part).astype(F32)
    gain_one = gains[:, 0].reshape(model)
    gain_two = gains[:, 1].reshape(model)
    out_all = gather_narrow(out_turned)
    upstream = gather_narrow(cotangent)
    half = length // 2
    pairs = picks[:half] | (picks[half:] << 16)
    pairs, packed = lax.optimization_barrier((pairs, packed))
    pairs = gather_wide(pairs)
    all_picks = jnp.concatenate([pairs & 0xFFFF, (pairs >> 16) & 0xFFFF], axis=1)
    all_picks = all_picks.reshape(shards * length, PICKS)
    located = locate(base, all_picks, shard_rows)
    where = jnp.concatenate([base, me_wide])

    factor_one, normed = norm_rows(rows_one, gain_one)
    normed = normed.astype(BF16)
    queries, key_rows, value_rows = [
        jnp.dot(normed, qkv_full[j], preferred_element_type=F32).astype(BF16) for j in range(3)
    ]
    starts = document_starts(segments)
    head_rows = attend_forward(starts, queries, key_rows, value_rows)
    head_all = gather_narrow(head_rows)
    hidden = rows_one + lax.dot_general(head_all, out_all, NT, preferred_element_type=F32)
    factor_two, second = norm_rows(hidden, gain_two)
    second = second.astype(BF16)

    gate_value = jnp.dot(second, gate_full, preferred_element_type=F32)
    gate_act = jax.nn.silu(gate_value)
    product_grad = jnp.dot(upstream, mixer_turned, preferred_element_type=F32)
    memory_grad = (product_grad * gate_act).astype(BF16)
    all_grads = gather_wide(memory_grad).reshape(shards * length, width)

    memory_query = jnp.dot(second, query_full, preferred_element_type=F32).astype(BF16)
    own_scores = pick_scores(column_ref, picks, memory_query, keys_full)
    mem_probs, pick_weights = pick_softmax(sum_by_swaps(own_scores, "narrow"))
    pick_weights, memory_grad = lax.optimization_barrier((pick_weights, memory_grad))
    all_weights = gather_wide(pick_weights).reshape(shards * length, PICKS)

    pick_part = picked_products(where, picks, located_own, memory_grad, table_turned, shards)
    pick_part = picked_products(
        where, all_picks, located, all_grads, table_turned, shards, pick_part
    )
    all_weights, pick_part = lax.optimization_barrier((all_weights, pick_part))
    pick_own = sum_wide(pick_part.reshape(shards, length, PICKS)).astype(F32)
    memory_part, tables = bag_sums(base, all_picks, located, all_weights, memory_values)
    memory_part, pick_own = lax.optimization_barrier((memory_part, pick_own))
    memory_own = sum_wide(memory_part.reshape(shards, length, width))
    values_grad = lax.dot_general(tables, all_grads, TN, preferred_element_type=F32)
    memory_own, values_grad = lax.optimization_barrier((memory_own, values_grad))
    memory = memory_own.astype(F32)

    pick_grad = sum_by_swaps(pick_own, "narrow")
    memory_query_grad, key_grad = spread_grads(
        column_ref, picks, mem_probs, pick_grad, memory_query, keys_full
    )

    product = (gate_act * memory).astype(BF16)
    sigmoid = jax.nn.sigmoid(gate_value)
    gate_rows_grad = (
        product_grad * memory * sigmoid * (1.0 + gate_value * (1.0 - sigmoid))
    ).astype(BF16)
    early_pack = pack_grads(
        column_ref * 0,
        [upstream, second, second],
        [product, gate_rows_grad, memory_query_grad],
        part,
        key_grad,
    )
    early_sums = sum_wide(early_pack)
    second_part = lax.dot_general(gate_rows_grad, gate_full, NT, preferred_element_type=F32)
    second_part = second_part + lax.dot_general(
        memory_query_grad, query_full, NT, preferred_element_type=F32
    )
    turned = second_part * gain_two
    inner_part = jnp.sum(turned * hidden, axis=-1)
    gain_two_part = jnp.sum(second_part * hidden * factor_two, axis=0)
    tiny = sum_by_swaps(jnp.concatenate([inner_part, gain_two_part]), "narrow")
    inner_two = tiny[:length, None] / model
    gain_two_part = tiny[length:]
    own_second_grad = scatter_narrow(second_part)

    def own_columns(block):
        return lax.dynamic_slice_in_dim(block, column * width, width, block.ndim - 1)

    own_hidden = own_columns(hidden)
    own_hidden_grad = (
        cotangent.astype(F32)
        + factor_two * own_columns(gain_two) * own_second_grad
        - own_hidden * (factor_two * factor_two * factor_two) * inner_two
    )
    branch_grad = own_hidden_grad.astype(BF16)
    branch_grad, early_pack = lax.optimization_barrier((branch_grad, early_pack))
    branch_grad = gather_narrow(branch_grad)

    heads_grad = jnp.dot(branch_grad, out_turned, preferred_element_type=F32)
    heads_grad = heads_grad.astype(BF16)

    mixed_grad = attend_backward(starts, queries, key_rows, value_rows, heads_grad)
    normed_part = sum(
        lax.dot_general(mixed_grad[j], qkv_full[j], NT, preferred_element_type=F32)
        for j in range(3)
    )
    late_pack = pack_grads(
        me_wide, [normed, normed, normed, branch_grad], [*mixed_grad, head_rows], part
    )
    inner_part = jnp.sum(normed_part * gain_one * rows_one, axis=-1)
    gain_one_part = jnp.sum(normed_part * rows_one * factor_one, axis=0)
    tiny = sum_by_swaps(jnp.concatenate([inner_part, gain_one_part]), "narrow")
    inner_one = tiny[:length, None] / model
    gain_one_part = tiny[length:]
    late_sums, gain_parts = scatter_both(
        late_pack, late_pack.shape[1] * 5 // 8 // 16 * 16, "wide", (gain_one_part, gain_two_part)
    )
    gain_sums = sum_by_swaps(jnp.stack(gain_parts), "wide")
    mixer_part = lax.dot_general(product, mixer_turned, NT, preferred_element_type=F32)
    mixer_part, _ = lax.optimization_barrier((mixer_part, branch_grad))
    outputs = (own_hidden + scatter_narrow(mixer_part, late_sums)).astype(BF16)
    own_normed_grad = scatter_narrow(normed_part, late_sums)
    input_grad = (
        own_hidden_grad
        + factor_one * own_columns(gain_one) * own_normed_grad
        - inputs.astype(F32) * (factor_one * factor_one * factor_one) * inner_one
    )
    gain_sums = lax.dynamic_slice_in_dim(gain_sums, lax.axis_index("wide") * part, part, 1)
    qkv_sum, out_sum, mixer_sum, gate_sum, query_sum, key_sum = unpack_grads(
        early_sums, late_sums, part, width, units, key_part
    )
    return (
        outputs,
        input_grad,
        gain_sums[0],
        jnp.transpose(qkv_sum, (1, 0, 2)),
        out_sum,
        gain_sums[1],
        jnp.transpose(query_sum, (1, 0, 2)),
        key_sum,
        gate_sum,
        values_grad,
        mixer_sum,
    )


def solution(mesh):
    return jax.shard_map(
        per_device,
        mesh=mesh,
        in_specs=(
            P("wide", "narrow"),
            P("wide", None),
            P("wide"),
            P("wide", None, "narrow"),
            P("narrow", "wide"),
            P("wide"),
            P("wide", "narrow", None),
            P("narrow", "wide", None),
            P("wide", "narrow"),
            P("wide", "narrow"),
            P("narrow", "wide"),
            P("wide", None),
            P("wide", "narrow"),
        ),
        out_specs=(
            P("wide", "narrow"),
            P("wide", "narrow"),
            P("wide"),
            P("wide", None, "narrow"),
            P("narrow", "wide"),
            P("wide"),
            P("wide", "narrow", None),
            P("narrow", "wide", None),
            P("wide", "narrow"),
            P("wide", "narrow"),
            P("narrow", "wide"),
        ),
        check_vma=False,
    )
```
